32 devices in a mesh: grp: 4 (over y, x), mem: 8 (over z, core).
Axes of the slice: x: 2, y: 2, z: 4, core: 2. Of those that a mesh axis runs over, the one named last changes fastest.
Arguments:
- pno: bfloat16 [1024, 512, 128], P(('grp', 'mem')), may hold values from -0.5 to 0.5
- amplitudes: bfloat16 [1024, 128, 128], P(('grp', 'mem')), may hold values from -6 to 6
- pno_count: int32 [1024], P(('grp', 'mem')), may hold values from 64 to 128
- pao_coupling: bfloat16 [512, 512], replicated, may hold values from -0.25 to 0.25
- row_owner: int32 [2048, 1], P(('grp', 'mem')), may hold values from 0 to 7; in each aligned block of 64 rows (0 to 63, 64 to 127, ...) at most 16 rows name the same one
- row_pair: int32 [2048], P(('grp', 'mem')), may hold values from 0 to 31
- row_target: int32 [2048], P(('grp', 'mem')), may hold values from 0 to 31
- row_coef: float32 [2048], P(('grp', 'mem')), may hold values from -6 to 6
- column_owner: int32 [512, 1], P(('grp', 'mem')), may hold values from 0 to 3; in each aligned block of 16 rows (0 to 15, 16 to 31, ...) at most 8 rows name the same one
- column_pair: int32 [512], P(('grp', 'mem')), may hold values from 0 to 31
- column_target: int32 [512], P(('grp', 'mem')), may hold values from 0 to 31
- column_coef: float32 [512], P(('grp', 'mem')), may hold values from -6 to 6
Outputs:
- coupling_residual: float32 [1024, 128, 128], P(('grp', 'mem'))
The draws below stay inside these ranges and needn't reach their ends.
Inputs may be any that keep to these rules, and one draw needn't show every extreme that they name: `row_owner`: among one device's in-group couplings at most 16 name the same member index, and some device's rows reach it. `column_owner`: among one device's cross-group couplings at most 8 name the same group index, and some device's rows reach it.
All inputs are finite; a program needn't handle non-finite values.
Results may differ from the reference program's by a relative error of at most 0.0064.
Values may be sent and summed in bfloat16 or wider, within the bound.
No kernel may reach another device: no remote copies, remote signals or barrier semaphores. Data moves between devices by JAX's collectives and lax.ppermute only.
A program may use at most 128 MiB of HBM per device.

```python
import math
import jax
import jax.numpy as jnp
import numpy as np
from jax import lax

K = 512
P_SIZE = 128
PAIR_DEV = 32
TASK_DEV = 64
COL_DEV = 16
CAP_M = 16
CAP_G = 8
PAIRS = 1024
TASKS = 2048
COLS = 512
N_GRP = 4
N_MEM = 8


def with_ends(drawn, own_key, least, largest):
    longest = drawn.shape.index(max(drawn.shape))
    spots = []
    for shift in (0, 1):
        where = [jax.random.randint(jax.random.fold_in(own_key, axis), (), 0, length) for axis, length in enumerate(drawn.shape)]
        where[longest] = (where[longest] + shift) % drawn.shape[longest]
        spots.append(tuple(where))
    return drawn.at[spots[0]].set(least).at[spots[1]].set(largest)


def block_levels(stream_key, dims, pieces, least, high):
    loudness, own = 1.0, jax.random.fold_in(stream_key, 6)
    for axis_at, parts in pieces:
        draws = jnp.exp(jax.random.uniform(jax.random.fold_in(own, axis_at), (parts,), jnp.float32, least / len(pieces), high / len(pieces)))
        loudness = loudness * jnp.repeat(draws, dims[axis_at] // parts).reshape([-1 if axis == axis_at else 1 for axis in range(len(dims))])
    return loudness


def deal_out(stream_key, own, number, rows, number_of, top, limit, slope):
    sequence = jax.random.permutation(stream_key, number_of)
    crowded, common = shares(number_of, rows * top, limit, slope, True), shares(number_of, rows * top, limit, slope, False)
    places = jnp.arange(number_of)

    def named(lengths, rotation):
        used = int((lengths > 0).sum())
        fixed = max(1, used // 4)
        passed = fixed + (places - fixed + rotation * (used - fixed)) % max(1, number_of - fixed)
        return jnp.zeros((number_of,), jnp.int32).at[sequence[jnp.where(places < fixed, places, passed)]].set(jnp.asarray(lengths, jnp.int32))

    lengths = jnp.where(number % 4 == 0, named(crowded, number // 4), named(common, number - number // 4 - 1))
    mixed = jax.random.permutation(jax.random.fold_in(own, 3), number_of)
    source_of, receiver = mixed[0:number_of // 2 * 2:2], mixed[1:number_of // 2 * 2:2]
    slack = jnp.minimum(lengths[source_of] - 1, limit - lengths[receiver]) // 2
    slack = jnp.where((source_of == sequence[0]) | (receiver == sequence[0]) | (lengths[receiver] == 0), 0, jnp.maximum(slack, 0))
    passed = jax.random.randint(jax.random.fold_in(own, 4), (number_of // 2,), 0, 1 << 20) % (slack + 1)
    lengths = lengths.at[source_of].add(-passed).at[receiver].add(passed)
    items = jnp.searchsorted(jnp.cumsum(lengths), jnp.arange(rows * top), side="right").astype(jnp.int32)
    grid = items.reshape(top, rows).T
    grid = grid[jax.random.permutation(jax.random.fold_in(own, 1), rows)]
    rotation = jax.random.randint(jax.random.fold_in(own, 2), (rows, 1), 0, top)
    return jnp.take_along_axis(grid, (jnp.arange(top)[None, :] + rotation) % top, axis=1)


def shares(number_of, total, most, skew, full):
    weights = [(1 << 20) // math.isqrt(grade ** skew) + 1 for grade in range(1, number_of + 1)]
    largest = most if full else min(most, max(-(-total // number_of), total * weights[0] // sum(weights)))
    least = 1 if total - largest >= number_of - 1 else 0
    counts, rest = [largest] + [least] * (number_of - 1), total - largest - least * (number_of - 1)
    while rest > 0:
        candidates = [i for i in range(1, number_of) if counts[i] < largest] or [i for i in range(1, number_of) if counts[i] < most]
        mass, left = sum([weights[i] for i in candidates]), rest
        for i in candidates:
            addition = min(most - counts[i], max(1, left * weights[i] // mass), rest)
            counts[i] = counts[i] + addition
            rest = rest - addition
    return np.array(counts)


def normal_values(stream_key, extent, deviation, limit, cuts=(), kind=jnp.bfloat16):
    level = block_levels(stream_key, extent, cuts, -0.22, 0.18) if cuts else 1.0
    drawn = jax.random.normal(stream_key, extent, jnp.float32) * deviation * level
    return jnp.minimum(jnp.maximum(drawn, -limit), limit).astype(kind)


def setup_inputs(seed: int = 0) -> dict:
    key_of = jax.random.split(jax.random.key(seed), 13)
    pno = normal_values(key_of[0], (PAIRS, K, P_SIZE), 0.0625, 0.5, ((0, 32),))
    amplitudes = normal_values(key_of[1], (PAIRS, P_SIZE, P_SIZE), 1.0, 6.0, ((0, 32),))
    pno_count = with_ends(jax.random.randint(key_of[2], (PAIRS,), P_SIZE // 2, P_SIZE + 1), jax.random.fold_in(key_of[2], 1), P_SIZE // 2, P_SIZE).astype(jnp.int32)
    pao_coupling = normal_values(key_of[3], (K, K), K ** -0.5, 0.25)
    row_owner_keys = jax.random.split(jax.random.fold_in(key_of[4], 1), TASKS // TASK_DEV)
    row_owner_turns = jax.random.permutation(jax.random.fold_in(key_of[4], 3), TASKS // TASK_DEV)
    row_owner = jax.vmap(lambda own, number: deal_out(jax.random.fold_in(key_of[4], 2), own, number, TASK_DEV, N_MEM, 1, CAP_M, 2))(row_owner_keys, row_owner_turns).reshape((TASKS, 1))
    row_pair = with_ends(jax.random.randint(key_of[5], (TASKS,), 0, PAIR_DEV), jax.random.fold_in(key_of[5], 1), 0, PAIR_DEV - 1).astype(jnp.int32)
    row_target = with_ends(jax.random.randint(key_of[6], (TASKS,), 0, PAIR_DEV), jax.random.fold_in(key_of[6], 1), 0, PAIR_DEV - 1).astype(jnp.int32)
    row_coef = normal_values(key_of[7], (TASKS,), 1.0, 6.0, ((0, 32),), jnp.float32)
    column_owner_keys = jax.random.split(jax.random.fold_in(key_of[8], 1), COLS // COL_DEV)
    column_owner_turns = jax.random.permutation(jax.random.fold_in(key_of[8], 3), COLS // COL_DEV)
    column_owner = jax.vmap(lambda own, number: deal_out(jax.random.fold_in(key_of[8], 2), own, number, COL_DEV, N_GRP, 1, CAP_G, 2))(column_owner_keys, column_owner_turns).reshape((COLS, 1))
    column_pair = with_ends(jax.random.randint(key_of[9], (COLS,), 0, PAIR_DEV), jax.random.fold_in(key_of[9], 1), 0, PAIR_DEV - 1).astype(jnp.int32)
    column_target = with_ends(jax.random.randint(key_of[10], (COLS,), 0, PAIR_DEV), jax.random.fold_in(key_of[10], 1), 0, PAIR_DEV - 1).astype(jnp.int32)
    column_coef = normal_values(key_of[11], (COLS,), 1.0, 6.0, ((0, 32),), jnp.float32)
    return dict(pno=pno, amplitudes=amplitudes, pno_count=pno_count, pao_coupling=pao_coupling, row_owner=row_owner, row_pair=row_pair, row_target=row_target, row_coef=row_coef, column_owner=column_owner, column_pair=column_pair, column_target=column_target, column_coef=column_coef)


def masked_blocks(pno, amplitudes, pno_count):
    width = pno.shape[2]
    live = jnp.arange(width, dtype=jnp.int32)[None, :] < pno_count[:, None]
    live_pno = jnp.where(live[:, None, :], pno, jnp.zeros((), pno.dtype))
    live_amp = jnp.where(live[:, :, None] & live[:, None, :], amplitudes, jnp.zeros((), amplitudes.dtype))
    return live_pno, live_amp


def metric_blocks(live_pno, pao_coupling):
    mixed = jnp.einsum('kj,tkp->tjp', pao_coupling.astype(jnp.float32), live_pno.astype(jnp.float32))
    return (live_pno.astype(jnp.float32) + mixed).astype(jnp.bfloat16)


def coupling_terms(metric_rows, source_pno, source_amp):
    intersection = jnp.einsum('tkp,tkq->tpq', metric_rows.astype(jnp.float32), source_pno.astype(jnp.float32)).astype(jnp.bfloat16)
    half = jnp.einsum('tpq,tqr->tpr', intersection.astype(jnp.float32), source_amp.astype(jnp.float32)).astype(jnp.bfloat16)
    return jnp.einsum('tpr,tsr->tps', half.astype(jnp.float32), intersection.astype(jnp.float32))


def pair_total(target, terms):
    onehot = (jnp.arange(PAIR_DEV, dtype=jnp.int32)[:, None] == target[None, :]).astype(jnp.float32)
    return jnp.einsum('at,tps->aps', onehot, terms, precision=lax.Precision.HIGHEST)


def reference(pno, amplitudes, pno_count, pao_coupling, row_owner, row_pair, row_target, row_coef, column_owner, column_pair, column_target, column_coef):
    live_pno, live_amp = masked_blocks(pno, amplitudes, pno_count)
    devices = N_GRP * N_MEM

    def one_device(index):
        group = index // N_MEM
        member = index % N_MEM
        own_pno = lax.dynamic_slice_in_dim(live_pno, (index * PAIR_DEV).astype(jnp.int32), PAIR_DEV, 0)
        metric = metric_blocks(own_pno, pao_coupling)
        start = (index * TASK_DEV).astype(jnp.int32)
        owner_rows = lax.dynamic_slice_in_dim(row_owner, start, TASK_DEV, 0)[:, 0]
        pair_rows = lax.dynamic_slice_in_dim(row_pair, start, TASK_DEV, 0)
        target_rows = lax.dynamic_slice_in_dim(row_target, start, TASK_DEV, 0)
        coef_rows = lax.dynamic_slice_in_dim(row_coef, start, TASK_DEV, 0)
        source_rows = ((group * N_MEM + owner_rows) * PAIR_DEV + pair_rows).astype(jnp.int32)
        row_terms = coupling_terms(metric[target_rows], live_pno[source_rows], live_amp[source_rows])
        row_terms = coef_rows[:, None, None] * row_terms
        begin = (index * COL_DEV).astype(jnp.int32)
        owner_cols = lax.dynamic_slice_in_dim(column_owner, begin, COL_DEV, 0)[:, 0]
        pair_cols = lax.dynamic_slice_in_dim(column_pair, begin, COL_DEV, 0)
        target_cols = lax.dynamic_slice_in_dim(column_target, begin, COL_DEV, 0)
        coef_cols = lax.dynamic_slice_in_dim(column_coef, begin, COL_DEV, 0)
        source_cols = ((owner_cols * N_MEM + member) * PAIR_DEV + pair_cols).astype(jnp.int32)
        col_terms = coupling_terms(metric[target_cols], live_pno[source_cols], live_amp[source_cols])
        col_terms = coef_cols[:, None, None] * col_terms
        return -(pair_total(target_rows, row_terms) + pair_total(target_cols, col_terms))

    result = lax.map(one_device, jnp.arange(devices, dtype=jnp.int32))
    return result.reshape(devices * PAIR_DEV, pno.shape[2], pno.shape[2])
```

```python
import functools

import jax
import jax.numpy as jnp
from jax import lax
from jax.experimental import pallas as pl
from jax.experimental.pallas import tpu as pltpu
from jax.sharding import PartitionSpec as P

UNIT = 16
ROUNDS = 10
SIZES = (24, 27, 30, 34)
VMEM = 48 * 2**20
ROW_BITS = 20
ANY = pl.BlockSpec(memory_space=pl.ANY)
SMEM = pl.BlockSpec(memory_space=pltpu.SMEM)
IN_VMEM = pl.BlockSpec(memory_space=pltpu.VMEM)


def params():
    return pltpu.CompilerParams(vmem_limit_bytes=VMEM)


def block_kernel(count_ref, pno_ref, amp_ref, out_ref):
    step = pl.program_id(0)
    many, depth, width = pno_ref.shape
    for i in range(many):
        count = count_ref[step * many + i]
        rows = lax.broadcasted_iota(jnp.int32, (width, depth), 0)
        turned = pno_ref[i].T
        out_ref[pl.ds(i * width, width), pl.ds(0, depth)] = jnp.where(rows < count, turned, jnp.zeros_like(turned))
        down = lax.broadcasted_iota(jnp.int32, (width, width), 0)
        across = lax.broadcasted_iota(jnp.int32, (width, width), 1)
        amp = amp_ref[i]
        live = (down < count) & (across < count)
        out_ref[pl.ds(i * width, width), pl.ds(depth, width)] = jnp.where(live, amp, jnp.zeros_like(amp))


def blocks_of(pno, amplitudes, pno_count):
    pairs, depth, width = pno.shape
    many = 4
    return pl.pallas_call(
        block_kernel,
        grid=(pairs // many,),
        in_specs=[
            SMEM,
            pl.BlockSpec((many, depth, width), lambda i: (i, 0, 0)),
            pl.BlockSpec((many, width, width), lambda i: (i, 0, 0)),
        ],
        out_specs=pl.BlockSpec((many * width, depth + width), lambda i: (i, 0)),
        out_shape=jax.ShapeDtypeStruct((pairs * width, depth + width), pno.dtype),
        compiler_params=params(),
    )(pno_count, pno, amplitudes)


def pick(array, index):
    return lax.dynamic_index_in_dim(array, index, 0, keepdims=False)


def starts_of(lengths, chips, delay):
    starts, ends = {}, []
    for c in range(chips - 1):
        at = jnp.zeros_like(lengths[0][chips - 1])
        for f in range(chips - 1, c, -1):
            for o in range(c, -1, -1):
                if o < c:
                    at = jnp.where(lengths[o][f] > 0, jnp.maximum(at, starts[o, f, c - 1] + delay), at)
                starts[o, f, c] = at
                at = at + lengths[o][f]
        ends.append(at)
    return starts, functools.reduce(jnp.maximum, ends)


def relay_plan(code, count, group, member, mine):
    groups, members, _ = code.shape
    pairs = count.shape[2]
    chips, items = members // 2, 2 * pairs
    chip, core = member // 2, member % 2
    ids = jnp.arange(members * pairs, dtype=jnp.int32)
    asked = jnp.any(code[..., None, :] == ids[:, None], axis=-1)
    asked = jnp.any(asked.reshape(groups, chips, 2, chips, items), axis=2)
    asked = jnp.stack([asked, asked[:, ::-1, ::-1]])
    line = jnp.arange(chips, dtype=jnp.int32)
    later = (line[:, None] > line[None, :])[:, :, None]
    far = jnp.max(jnp.where(asked & later, line[:, None, None], 0), axis=2)
    units = ((count + UNIT - 1) // UNIT).reshape(groups, chips, items)
    units = jnp.stack([units, units[:, ::-1]])
    order = far * items + (items - 1 - jnp.arange(items, dtype=jnp.int32))
    before = (order[..., None, :] > order[..., :, None]) & (far[..., None, :] > 0)
    lane = jnp.sum(before.astype(jnp.int32), axis=-1) & 1
    kind = far * 2 + lane
    ahead = before & (kind[..., None, :] == kind[..., :, None])
    prefix = jnp.sum(jnp.where(ahead, units[..., None, :], 0), axis=-1)
    kinds = jnp.arange(2 * chips, dtype=jnp.int32)
    total = jnp.sum(jnp.where(kind[..., None, :] == kinds[:, None], units[..., None, :], 0), axis=-1)
    total = total.reshape(2, groups, chips, chips, 2)
    lengths = [[total[:, :, o, f] for f in range(chips)] for o in range(chips)]
    branch, size = jnp.int32(len(SIZES)), jnp.int32(SIZES[-1])
    for b in range(len(SIZES) - 1, -1, -1):
        fits = jnp.max(starts_of(lengths, chips, 2 * SIZES[b])[1]) <= ROUNDS * SIZES[b]
        branch, size = jnp.where(fits, b, branch), jnp.where(fits, SIZES[b], size)

    def own_group(x):
        return lax.dynamic_index_in_dim(x, group, 1, keepdims=False)

    far, lane, prefix, units, total = (own_group(x) for x in (far, lane, prefix, units, total))
    lengths = [[total[:, o, f] for f in range(chips)] for o in range(chips)]
    starts = starts_of(lengths, chips, 2 * size)[0]
    none = jnp.zeros_like(lengths[0][0])
    runs = []
    most = max(c * (chips - 1 - c) for c in range(chips))
    for c in range(chips):
        own = [(starts[c, f, c], lengths[c][f], none) if f > c else (none, none, none) for f in range(1, chips)]
        passed = [(starts[o, f, c], lengths[o][f], starts[o, f, c - 1]) for o in range(c) for f in range(c + 1, chips)]
        passed += [(none, none, none)] * (most - len(passed))
        runs.append(jnp.stack([jnp.stack(r) for r in own + passed]))
    runs = jnp.stack(runs)
    outgo = jnp.stack([jnp.stack([starts[c, f, c] if f > c else none for f in range(chips)]) for c in range(chips)])
    income = jnp.stack(
        [
            jnp.stack([jnp.stack([starts[o, f, c - 1] if o < c <= f else none for f in range(chips)]) for o in range(chips)])
            for c in range(chips)
        ]
    )
    table, place, need, spot, side = [], [], [], [], []
    for d in range(2):
        at = chip if d == 0 else chips - 1 - chip
        table.append(lax.dynamic_index_in_dim(pick(runs, at)[..., d, :], core, 2, keepdims=False))
        home = pick(far[d], at)
        chosen = lax.dynamic_index_in_dim(pick(outgo, at)[:, d, :], core, 1, keepdims=False)
        first = jnp.sum(jnp.where(home[:, None] == line, chosen, 0), axis=1)
        place.append(first + pick(prefix[d], at))
        need.append(jnp.where((home > 0) & (pick(lane[d], at) == core), pick(units[d], at), 0))
        came = pick(income, at)[:, :, d, :]
        hit = (far[d][:, :, None, None] == line[:, None]) & (lane[d][:, :, None, None] == jnp.arange(2, dtype=jnp.int32))
        where = prefix[d] + jnp.sum(jnp.where(hit, came[:, None], 0), axis=(2, 3))
        spot.append(where if d == 0 else where[::-1])
        side.append(lane[d] if d == 0 else lane[d][::-1])
    stretch = ROUNDS * size + 8
    origin = line[:, None]
    item = jnp.arange(items, dtype=jnp.int32)[None, :]
    width = mine[1]
    down = (origin > chip).astype(jnp.int32)
    lies = jnp.where(down == 1, spot[1], spot[0])
    on = jnp.where(down == 1, side[1], side[0])
    far_row = ((2 * down + (on != core)) * stretch + lies) * UNIT + (2 << ROW_BITS)
    near_row = (item % pairs) * width + ((item // pairs != core).astype(jnp.int32) << ROW_BITS)
    rows = jnp.where(origin == chip, near_row, far_row).reshape(-1)
    location = jnp.sum(jnp.where(mine[0][:, None] == ids, rows, 0), axis=1)
    return branch, jnp.stack(table), jnp.stack(place), jnp.stack(need), location


def ranks_of(owner):
    spots = jnp.arange(owner.shape[-1], dtype=jnp.int32)
    ahead = (owner[..., None, :] == owner[..., :, None]) & (spots[None, :] < spots[:, None])
    return jnp.sum(ahead.astype(jnp.int32), axis=-1)


def wanted_from(owner, pair, me, capacity):
    slot = jnp.where(owner == me, ranks_of(owner), capacity)
    hit = slot[:, None, :] == jnp.arange(capacity, dtype=jnp.int32)[:, None]
    return jnp.sum(jnp.where(hit, pair[:, None, :], 0), axis=-1)


def take_kernel(width, depth, index_ref, blocks_ref, *refs):
    outs, sem = refs[:-1], refs[-1]
    slots = outs[0].shape[0] // width

    def copies(i):
        for k, out in enumerate(outs):
            row = pl.multiple_of(index_ref[k * slots + i] * width, UNIT)
            yield pltpu.make_async_copy(
                blocks_ref.at[pl.ds(row, width)], out.at[pl.ds(pl.multiple_of(i * width, UNIT), width)], sem
            )

    @pl.loop(0, slots)
    def _(i):
        for c in copies(i):
            c.start()

    @pl.loop(0, slots)
    def _(i):
        for c in copies(i):
            c.wait()


def take(blocks, index, width, parts):
    slots = index.shape[0] // parts
    shape = jax.ShapeDtypeStruct((slots * width, blocks.shape[1]), blocks.dtype)
    return pl.pallas_call(
        functools.partial(take_kernel, width, blocks.shape[1]),
        in_specs=[SMEM, ANY],
        out_specs=[ANY] * parts,
        out_shape=[shape] * parts,
        scratch_shapes=[pltpu.SemaphoreType.DMA],
        compiler_params=params(),
        cost_estimate=pl.CostEstimate(flops=0, bytes_accessed=2 * parts * slots * width * blocks.shape[1] * 2, transcendentals=0),
    )(index, blocks)


def run_copies(runs_ref, d, r, window, size, source, out, sem, shift):
    first, length, back = runs_ref[d, r, 0], runs_ref[d, r, 1], runs_ref[d, r, 2]
    low = jnp.maximum(first, window * size)
    high = jnp.minimum(first + length, (window + 1) * size)
    taken = jnp.maximum(high - low, 0)
    begin = back + low - first if shift else low
    rows = taken * UNIT
    return taken, pltpu.make_async_copy(
        source.at[d, pl.ds(pl.multiple_of(jnp.maximum(begin, 0) * UNIT, UNIT), rows)],
        out.at[pl.ds(pl.multiple_of((low - window * size) * UNIT, UNIT), rows)],
        sem,
    )


def windows(runs_ref, picks, window, size, source, outs, sem, shift, act):
    for d in range(2):
        for r in picks:
            taken, copy = run_copies(runs_ref, d, r, window, size, source, outs[d], sem, shift)

            @pl.when(taken > 0)
            def _():
                getattr(copy, act)()


def open_kernel(size, pairs, width, own, place_ref, need_ref, runs_ref, core_ref, mine_ref, other_ref, stream_ref, *refs):
    outs, sem = refs[:-1], refs[-1]

    def each(act):
        for half, source in ((0, mine_ref), (1, other_ref)):

            @pl.loop(0, pairs)
            def _(i):
                for d in range(2):
                    item = (core_ref[0] ^ half) * pairs + i
                    units = need_ref[d, item]
                    rows = units * UNIT

                    @pl.when(units > 0)
                    def _():
                        copy = pltpu.make_async_copy(
                            source.at[pl.ds(pl.multiple_of(i * width, UNIT), rows)],
                            stream_ref.at[d, pl.ds(pl.multiple_of(place_ref[d, item] * UNIT, UNIT), rows)],
                            sem,
                        )
                        getattr(copy, act)()

    each("start")
    each("wait")
    for act in ("start", "wait"):
        for window in range(2):
            windows(runs_ref, range(own), window, size, stream_ref, outs[2 * window : 2 * window + 2], sem, False, act)


def step_kernel(size, stretch, number, sends, own, runs_ref, stream_ref, *refs):
    refs = list(refs)
    held = refs.pop(0) if number > 0 else None
    came = [refs.pop(0), refs.pop(0)]
    other = [refs.pop(0), refs.pop(0)] if number > 0 else []
    del held
    hold = refs.pop(0)
    outs = [refs.pop(0), refs.pop(0)] if sends else []
    arrive, rest, lay = refs
    rows = size * UNIT
    first = [
        pltpu.make_async_copy(came[d], hold.at[2 * d, pl.ds(number * rows, rows)], arrive.at[d]) for d in range(2)
    ]
    second = [
        pltpu.make_async_copy(other[d], hold.at[2 * d + 1, pl.ds((number - 1) * rows, rows)], rest.at[d])
        for d in range(2)
        if other
    ]
    for c in first + second:
        c.start()
    if sends:
        windows(runs_ref, range(own), number + 2, size, stream_ref, outs, lay, False, "start")
        windows(runs_ref, range(own), number + 2, size, stream_ref, outs, lay, False, "wait")
    for c in first:
        c.wait()
    if sends:
        for act in ("start", "wait"):
            for d in range(2):
                for r in range(own, runs_ref.shape[1]):
                    taken, copy = run_copies(runs_ref, d, r, number + 2, size, hold.at[pl.ds(d, 2)], outs[d], lay, True)

                    @pl.when(taken > 0)
                    def _():
                        getattr(copy, act)()
    for c in second:
        c.wait()


def close_kernel(size, number, came_up, came_down, held_ref, hold, sem):
    del held_ref
    rows = size * UNIT
    copies = [
        pltpu.make_async_copy(c, hold.at[2 * d + 1, pl.ds(number * rows, rows)], sem.at[d])
        for d, c in enumerate((came_up, came_down))
    ]
    for c in copies:
        c.start()
    for c in copies:
        c.wait()


def couple_kernel(tasks, width, depth, many, loc_ref, count_ref, target_ref, coef_ref, metric_ref, *refs):
    out_ref, slots, sems = refs[-3], refs[-2], refs[-1]
    buffers = refs[:-3]
    out_ref[...] = jnp.zeros_like(out_ref)

    def fetch(group, phase):
        for u in range(many):
            code = loc_ref[group * many + u]
            row = pl.multiple_of(code & ((1 << ROW_BITS) - 1), UNIT)
            for b, source in enumerate(buffers):

                @pl.when((code >> ROW_BITS) == b)
                def _():
                    pltpu.make_async_copy(source.at[pl.ds(row, width)], slots.at[phase, u], sems.at[phase, u]).start()

    groups = tasks // many
    fetch(0, 0)

    @pl.loop(0, groups)
    def _(group):
        phase = lax.rem(group, 2)

        @pl.when(group + 1 < groups)
        def _():
            fetch(group + 1, 1 - phase)

        terms = []
        for u in range(many):
            pltpu.make_async_copy(buffers[0].at[pl.ds(0, width)], slots.at[phase, u], sems.at[phase, u]).wait()
        for u in range(many):
            t = group * many + u
            held = slots[phase, u]
            rows = lax.broadcasted_iota(jnp.int32, held.shape, 0)
            held = jnp.where(rows < count_ref[t], held, jnp.zeros_like(held))
            turned = lax.dot_general(
                held[:, :depth], metric_ref[target_ref[t]], (((1,), (1,)), ((), ())), preferred_element_type=jnp.float32
            ).astype(jnp.bfloat16)
            half = lax.dot_general(
                turned, held[:, depth:], (((0,), (0,)), ((), ())), preferred_element_type=jnp.float32
            ).astype(jnp.bfloat16)
            terms.append(coef_ref[t] * jnp.dot(half, turned, preferred_element_type=jnp.float32))
        for u in range(many):
            target = target_ref[group * many + u]
            out_ref[target] = out_ref[target] - terms[u]


def couple(location, count, target, coef, metric, buffers, width, depth):
    tasks, pairs = location.shape[0], metric.shape[0]
    many = 4
    return pl.pallas_call(
        functools.partial(couple_kernel, tasks, width, depth, many),
        in_specs=[SMEM] * 4 + [IN_VMEM] + [ANY] * len(buffers),
        out_specs=IN_VMEM,
        out_shape=jax.ShapeDtypeStruct((pairs, width, width), jnp.float32),
        scratch_shapes=[
            pltpu.VMEM((2, many, width, depth + width), jnp.bfloat16),
            pltpu.SemaphoreType.DMA((2, many)),
        ],
        compiler_params=params(),
    )(location, count, target, coef, metric, *buffers)


def relay(size, chips, pairs, width, table, place, need, core, mine, other):
    columns = mine.shape[1]
    stretch = ROUNDS * size + 8
    own = chips - 1
    piece = jax.ShapeDtypeStruct((size * UNIT, columns), mine.dtype)
    stream_shape = jax.ShapeDtypeStruct((2, ROUNDS * size * UNIT, columns), mine.dtype)
    hold_shape = jax.ShapeDtypeStruct((4, stretch * UNIT, columns), mine.dtype)
    members = 2 * chips
    ways = [
        [(i, i + 2) for i in range(members - 2)],
        [(i + 2, i) for i in range(members - 2)],
    ]
    across = [(i, i ^ 1) for i in range(members)]
    stream, *opened = pl.pallas_call(
        functools.partial(open_kernel, size, pairs, width, own),
        in_specs=[SMEM] * 4 + [ANY] * 2,
        out_specs=[ANY] * 5,
        out_shape=[stream_shape] + [piece] * 4,
        scratch_shapes=[pltpu.SemaphoreType.DMA],
        compiler_params=params(),
    )(place, need, table, core, mine, other)
    sends = [opened[:2], opened[2:]]
    hold, swapped = None, None
    for number in range(ROUNDS):
        came = [lax.ppermute(sends[number][d], "mem", ways[d]) for d in range(2)]
        ends = number + 2 >= ROUNDS
        operands = [table, stream] + ([hold] if number else []) + came + (swapped if number else [])
        results = pl.pallas_call(
            functools.partial(step_kernel, size, stretch, number, not ends, own),
            in_specs=[SMEM] + [ANY] * (len(operands) - 1),
            out_specs=[ANY] * (1 if ends else 3),
            out_shape=[hold_shape] + ([] if ends else [piece] * 2),
            input_output_aliases={2: 0} if number else {},
            scratch_shapes=[pltpu.SemaphoreType.DMA((2,)), pltpu.SemaphoreType.DMA((2,)), pltpu.SemaphoreType.DMA],
            compiler_params=params(),
            cost_estimate=pl.CostEstimate(flops=0, bytes_accessed=12 * size * UNIT * columns * 2, transcendentals=0),
        )(*operands)
        hold = results[0]
        sends.append(results[1:])
        swapped = [lax.ppermute(came[d], "mem", across) for d in range(2)]
    return pl.pallas_call(
        functools.partial(close_kernel, size, ROUNDS - 1),
        in_specs=[ANY] * 3,
        out_specs=ANY,
        out_shape=hold_shape,
        input_output_aliases={2: 0},
        scratch_shapes=[pltpu.SemaphoreType.DMA((2,))],
        compiler_params=params(),
    )(*swapped, hold)


def shards(
    pno,
    amplitudes,
    pno_count,
    pao_coupling,
    row_owner,
    row_pair,
    row_target,
    row_coef,
    column_owner,
    column_pair,
    column_target,
    column_coef,
):
    pairs, depth, width = pno.shape
    tasks, crossings = row_pair.shape[0], column_pair.shape[0]
    members, groups = lax.axis_size("mem"), lax.axis_size("grp")
    member, group = lax.axis_index("mem"), lax.axis_index("grp")
    row_cap = max(2, 2 * tasks // members)
    col_cap = max(2, 2 * crossings // groups)
    chips = members // 2
    row_owner, column_owner = row_owner[:, 0], column_owner[:, 0]
    row_code = row_owner * pairs + row_pair
    col_code = column_owner * pairs + column_pair
    told = lax.all_gather(jnp.concatenate([row_code, col_code, pno_count]), ("grp", "mem"))
    told = told.reshape(groups, members, -1)
    code, cols, count = told[..., :tasks], told[..., tasks : tasks + crossings], told[..., tasks + crossings :]
    blocks = blocks_of(pno, amplitudes, pno_count)
    metric = blocks[:, :depth].astype(jnp.float32) + jnp.dot(
        blocks[:, :depth], pao_coupling, preferred_element_type=jnp.float32
    )
    metric = metric.astype(jnp.bfloat16).reshape(pairs, width, depth)
    ids = jnp.arange(members * pairs, dtype=jnp.int32)
    here = pick(count, group).reshape(-1)
    row_count = jnp.sum(jnp.where(row_code[:, None] == ids, here, 0), axis=1)
    beside = lax.dynamic_index_in_dim(count, member, 1, keepdims=False).reshape(-1)
    col_ids = jnp.arange(groups * pairs, dtype=jnp.int32)
    col_count = jnp.sum(jnp.where(col_code[:, None] == col_ids, beside, 0), axis=1)
    ask = lax.dynamic_index_in_dim(cols, member, 1, keepdims=False)
    asked = wanted_from(ask // pairs, ask % pairs, group, col_cap)
    shifts = range(1, groups)
    index = jnp.concatenate([pick(asked, (group + k) % groups) for k in shifts])
    step = (group - column_owner) % groups
    col_row = (ranks_of(column_owner) + 0) * width
    target = jnp.concatenate([row_target, column_target])
    coef = jnp.concatenate([row_coef, column_coef])
    counts = jnp.concatenate([row_count, col_count])

    def crossed():
        parts = take(blocks, index, width, groups - 1)
        return [
            lax.ppermute(parts[k - 1], "grp", [(g, (g + k) % groups) for g in range(groups)]) for k in shifts
        ]

    def finish(location, buffers):
        from_own = column_pair * width
        first = len(buffers)
        col_location = jnp.where(step == 0, from_own, col_row + ((first + step - 1) << ROW_BITS))
        return couple(
            jnp.concatenate([location, col_location]), counts, target, coef, metric, buffers + crossed(), width, depth
        )

    def plain(*_):
        want = wanted_from(pick(code, group) // pairs, pick(code, group) % pairs, member, row_cap)
        [sent] = take(blocks, want.reshape(-1), width, 1)
        got = lax.all_to_all(sent, "mem", split_axis=0, concat_axis=0, tiled=True)
        location = (row_owner * row_cap + ranks_of(row_owner)) * width + (1 << ROW_BITS)
        return finish(location, [blocks, got])

    if members % 2 or chips < 2 or chips > 4:
        return plain()
    other = lax.ppermute(blocks, "mem", [(i, i ^ 1) for i in range(members)])
    branch, table, place, need, location = relay_plan(code, count, group, member, (row_code, width))
    core = (member % 2).reshape(1).astype(jnp.int32)

    def relayed(size, table, place, need, location, other):
        hold = relay(size, chips, pairs, width, table, place, need, core, blocks, other)
        return finish(location, [blocks, other, hold.reshape(-1, hold.shape[2])])

    branches = [functools.partial(relayed, size) for size in SIZES] + [plain]
    return lax.switch(branch, branches, table, place, need, location, other)


def solution(mesh):
    in_specs = (
        P(("grp", "mem"), None, None),
        P(("grp", "mem"), None, None),
        P(("grp", "mem")),
        P(),
        P(("grp", "mem"), None),
        P(("grp", "mem")),
        P(("grp", "mem")),
        P(("grp", "mem")),
        P(("grp", "mem"), None),
        P(("grp", "mem")),
        P(("grp", "mem")),
        P(("grp", "mem")),
    )
    out_specs = P(("grp", "mem"), None, None)
    return jax.shard_map(shards, mesh=mesh, in_specs=in_specs, out_specs=out_specs, check_vma=False)
```

```python
import functools

import jax
import jax.numpy as jnp
from jax import lax
from jax.experimental import pallas as pl
from jax.experimental.pallas import tpu as pltpu
from jax.sharding import PartitionSpec as P

UNIT = 16
ROUNDS = 10
SIZES = (27, 29, 31, 34)
VMEM = 48 * 2**20
ROW_BITS = 20
ANY = pl.BlockSpec(memory_space=pl.ANY)
SMEM = pl.BlockSpec(memory_space=pltpu.SMEM)
IN_VMEM = pl.BlockSpec(memory_space=pltpu.VMEM)


def params():
    return pltpu.CompilerParams(vmem_limit_bytes=VMEM)


def block_kernel(count_ref, pno_ref, amp_ref, out_ref):
    step = pl.program_id(0)
    many, depth, width = pno_ref.shape
    for i in range(many):
        count = count_ref[step * many + i]
        rows = lax.broadcasted_iota(jnp.int32, (width, depth), 0)
        turned = pno_ref[i].T
        out_ref[pl.ds(i * width, width), pl.ds(0, depth)] = jnp.where(rows < count, turned, jnp.zeros_like(turned))
        down = lax.broadcasted_iota(jnp.int32, (width, width), 0)
        across = lax.broadcasted_iota(jnp.int32, (width, width), 1)
        amp = amp_ref[i]
        live = (down < count) & (across < count)
        out_ref[pl.ds(i * width, width), pl.ds(depth, width)] = jnp.where(live, amp, jnp.zeros_like(amp))


def blocks_of(pno, amplitudes, pno_count):
    pairs, depth, width = pno.shape
    many = 4
    return pl.pallas_call(
        block_kernel,
        grid=(pairs // many,),
        in_specs=[
            SMEM,
            pl.BlockSpec((many, depth, width), lambda i: (i, 0, 0)),
            pl.BlockSpec((many, width, width), lambda i: (i, 0, 0)),
        ],
        out_specs=pl.BlockSpec((many * width, depth + width), lambda i: (i, 0)),
        out_shape=jax.ShapeDtypeStruct((pairs * width, depth + width), pno.dtype),
        compiler_params=params(),
    )(pno_count, pno, amplitudes)


def pick(array, index):
    return lax.dynamic_index_in_dim(array, index, 0, keepdims=False)


def starts_of(lengths, chips, delay):
    starts, ends = {}, []
    for c in range(chips - 1):
        at = jnp.zeros_like(lengths[0][chips - 1])
        for f in range(chips - 1, c, -1):
            for o in range(c, -1, -1):
                if o < c:
                    at = jnp.where(lengths[o][f] > 0, jnp.maximum(at, starts[o, f, c - 1] + delay), at)
                starts[o, f, c] = at
                at = at + lengths[o][f]
        ends.append(at)
    return starts, functools.reduce(jnp.maximum, ends)


def relay_plan(code, count, group, member, mine):
    groups, members, _ = code.shape
    pairs = count.shape[2]
    chips, items = members // 2, 2 * pairs
    chip, core = member // 2, member % 2
    ids = jnp.arange(members * pairs, dtype=jnp.int32)
    asked = jnp.any(code[..., None, :] == ids[:, None], axis=-1)
    asked = jnp.any(asked.reshape(groups, chips, 2, chips, items), axis=2)
    asked = jnp.stack([asked, asked[:, ::-1, ::-1]])
    line = jnp.arange(chips, dtype=jnp.int32)
    later = (line[:, None] > line[None, :])[:, :, None]
    far = jnp.max(jnp.where(asked & later, line[:, None, None], 0), axis=2)
    units = ((count + UNIT - 1) // UNIT).reshape(groups, chips, items)
    units = jnp.stack([units, units[:, ::-1]])
    order = far * items + (items - 1 - jnp.arange(items, dtype=jnp.int32))
    before = (order[..., None, :] > order[..., :, None]) & (far[..., None, :] > 0)
    lane = jnp.sum(before.astype(jnp.int32), axis=-1) & 1
    kind = far * 2 + lane
    ahead = before & (kind[..., None, :] == kind[..., :, None])
    prefix = jnp.sum(jnp.where(ahead, units[..., None, :], 0), axis=-1)
    kinds = jnp.arange(2 * chips, dtype=jnp.int32)
    total = jnp.sum(jnp.where(kind[..., None, :] == kinds[:, None], units[..., None, :], 0), axis=-1)
    total = total.reshape(2, groups, chips, chips, 2)
    lengths = [[total[:, :, o, f] for f in range(chips)] for o in range(chips)]
    branch, size = jnp.int32(len(SIZES)), jnp.int32(SIZES[-1])
    for b in range(len(SIZES) - 1, -1, -1):
        fits = jnp.max(starts_of(lengths, chips, 2 * SIZES[b])[1]) <= ROUNDS * SIZES[b]
        branch, size = jnp.where(fits, b, branch), jnp.where(fits, SIZES[b], size)

    def own_group(x):
        return lax.dynamic_index_in_dim(x, group, 1, keepdims=False)

    far, lane, prefix, units, total = (own_group(x) for x in (far, lane, prefix, units, total))
    lengths = [[total[:, o, f] for f in range(chips)] for o in range(chips)]
    starts = starts_of(lengths, chips, 2 * size)[0]
    none = jnp.zeros_like(lengths[0][0])
    runs = []
    most = max(c * (chips - 1 - c) for c in range(chips))
    for c in range(chips):
        own = [(starts[c, f, c], lengths[c][f], none) if f > c else (none, none, none) for f in range(1, chips)]
        passed = [(starts[o, f, c], lengths[o][f], starts[o, f, c - 1]) for o in range(c) for f in range(c + 1, chips)]
        passed += [(none, none, none)] * (most - len(passed))
        runs.append(jnp.stack([jnp.stack(r) for r in own + passed]))
    runs = jnp.stack(runs)
    outgo = jnp.stack([jnp.stack([starts[c, f, c] if f > c else none for f in range(chips)]) for c in range(chips)])
    income = jnp.stack(
        [
            jnp.stack([jnp.stack([starts[o, f, c - 1] if o < c <= f else none for f in range(chips)]) for o in range(chips)])
            for c in range(chips)
        ]
    )
    table, place, need, spot, side = [], [], [], [], []
    for d in range(2):
        at = chip if d == 0 else chips - 1 - chip
        table.append(lax.dynamic_index_in_dim(pick(runs, at)[..., d, :], core, 2, keepdims=False))
        home = pick(far[d], at)
        chosen = lax.dynamic_index_in_dim(pick(outgo, at)[:, d, :], core, 1, keepdims=False)
        first = jnp.sum(jnp.where(home[:, None] == line, chosen, 0), axis=1)
        place.append(first + pick(prefix[d], at))
        need.append(jnp.where((home > 0) & (pick(lane[d], at) == core), pick(units[d], at), 0))
        came = pick(income, at)[:, :, d, :]
        hit = (far[d][:, :, None, None] == line[:, None]) & (lane[d][:, :, None, None] == jnp.arange(2, dtype=jnp.int32))
        where = prefix[d] + jnp.sum(jnp.where(hit, came[:, None], 0), axis=(2, 3))
        spot.append(where if d == 0 else where[::-1])
        side.append(lane[d] if d == 0 else lane[d][::-1])
    stretch = ROUNDS * size + 8
    origin = line[:, None]
    item = jnp.arange(items, dtype=jnp.int32)[None, :]
    width = mine[1]
    down = (origin > chip).astype(jnp.int32)
    lies = jnp.where(down == 1, spot[1], spot[0])
    on = jnp.where(down == 1, side[1], side[0])
    far_row = ((2 * down + (on != core)) * stretch + lies) * UNIT + (2 << ROW_BITS)
    near_row = (item % pairs) * width + ((item // pairs != core).astype(jnp.int32) << ROW_BITS)
    rows = jnp.where(origin == chip, near_row, far_row).reshape(-1)
    location = jnp.sum(jnp.where(mine[0][:, None] == ids, rows, 0), axis=1)
    return branch, jnp.stack(table), jnp.stack(place), jnp.stack(need), location


def ranks_of(owner):
    spots = jnp.arange(owner.shape[-1], dtype=jnp.int32)
    ahead = (owner[..., None, :] == owner[..., :, None]) & (spots[None, :] < spots[:, None])
    return jnp.sum(ahead.astype(jnp.int32), axis=-1)


def wanted_from(owner, pair, me, capacity):
    slot = jnp.where(owner == me, ranks_of(owner), capacity)
    hit = slot[:, None, :] == jnp.arange(capacity, dtype=jnp.int32)[:, None]
    return jnp.sum(jnp.where(hit, pair[:, None, :], 0), axis=-1)


def load_all(source, scratch, sem, parts=8):
    rows = source.shape[0] // parts
    return [
        pltpu.make_async_copy(source.at[pl.ds(i * rows, rows)], scratch.at[pl.ds(i * rows, rows)], sem) for i in range(parts)
    ]


def take_kernel(width, index_ref, blocks_ref, *refs):
    outs, (scratch, load, sem) = refs[:-3], refs[-3:]
    slots = outs[0].shape[0] // width
    loads = load_all(blocks_ref, scratch, load)
    for c in loads:
        c.start()
    for c in loads:
        c.wait()

    def copies(i):
        for k, out in enumerate(outs):
            row = pl.multiple_of(index_ref[k * slots + i] * width, UNIT)
            yield pltpu.make_async_copy(
                scratch.at[pl.ds(row, width)], out.at[pl.ds(pl.multiple_of(i * width, UNIT), width)], sem
            )

    @pl.loop(0, slots)
    def _(i):
        for c in copies(i):
            c.start()

    @pl.loop(0, slots)
    def _(i):
        for c in copies(i):
            c.wait()


def take(blocks, index, width, parts):
    slots = index.shape[0] // parts
    shape = jax.ShapeDtypeStruct((slots * width, blocks.shape[1]), blocks.dtype)
    return pl.pallas_call(
        functools.partial(take_kernel, width),
        in_specs=[SMEM, ANY],
        out_specs=[ANY] * parts,
        out_shape=[shape] * parts,
        scratch_shapes=[pltpu.VMEM(blocks.shape, blocks.dtype), pltpu.SemaphoreType.DMA, pltpu.SemaphoreType.DMA],
        compiler_params=params(),
        cost_estimate=pl.CostEstimate(flops=0, bytes_accessed=2 * parts * slots * width * blocks.shape[1] * 2, transcendentals=0),
    )(index, blocks)


def run_copies(runs_ref, d, r, window, size, source, out, sem, shift):
    first, length, back = runs_ref[d, r, 0], runs_ref[d, r, 1], runs_ref[d, r, 2]
    low = jnp.maximum(first, window * size)
    high = jnp.minimum(first + length, (window + 1) * size)
    taken = jnp.maximum(high - low, 0)
    begin = back + low - first if shift else low
    rows = taken * UNIT
    return taken, pltpu.make_async_copy(
        source.at[d, pl.ds(pl.multiple_of(jnp.maximum(begin, 0) * UNIT, UNIT), rows)],
        out.at[pl.ds(pl.multiple_of((low - window * size) * UNIT, UNIT), rows)],
        sem,
    )


def windows(runs_ref, picks, window, size, source, outs, sem, shift, act):
    for d in range(2):
        for r in picks:
            taken, copy = run_copies(runs_ref, d, r, window, size, source, outs[d], sem, shift)

            @pl.when(taken > 0)
            def _():
                getattr(copy, act)()


def open_kernel(size, pairs, width, own, place_ref, need_ref, runs_ref, core_ref, mine_ref, other_ref, stream_ref, *refs):
    outs, (near, beside, load, sem) = refs[:-4], refs[-4:]
    loads = load_all(mine_ref, near, load) + load_all(other_ref, beside, load)
    for c in loads:
        c.start()
    for c in loads:
        c.wait()

    def each(act):
        for half, source in ((0, near), (1, beside)):

            @pl.loop(0, pairs)
            def _(i):
                for d in range(2):
                    item = (core_ref[0] ^ half) * pairs + i
                    units = need_ref[d, item]
                    rows = units * UNIT

                    @pl.when(units > 0)
                    def _():
                        copy = pltpu.make_async_copy(
                            source.at[pl.ds(pl.multiple_of(i * width, UNIT), rows)],
                            stream_ref.at[d, pl.ds(pl.multiple_of(place_ref[d, item] * UNIT, UNIT), rows)],
                            sem,
                        )
                        getattr(copy, act)()

    each("start")
    each("wait")
    for act in ("start", "wait"):
        for window in range(2):
            windows(runs_ref, range(own), window, size, stream_ref, outs[2 * window : 2 * window + 2], sem, False, act)


def step_kernel(size, stretch, number, sends, own, runs_ref, stream_ref, *refs):
    refs = list(refs)
    held = refs.pop(0) if number > 0 else None
    came = [refs.pop(0), refs.pop(0)]
    other = [refs.pop(0), refs.pop(0)] if number > 0 else []
    del held
    hold = refs.pop(0)
    outs = [refs.pop(0), refs.pop(0)] if sends else []
    arrive, rest, lay = refs
    rows = size * UNIT
    first = [
        pltpu.make_async_copy(came[d], hold.at[2 * d, pl.ds(number * rows, rows)], arrive.at[d]) for d in range(2)
    ]
    second = [
        pltpu.make_async_copy(other[d], hold.at[2 * d + 1, pl.ds((number - 1) * rows, rows)], rest.at[d])
        for d in range(2)
        if other
    ]
    for c in first + second:
        c.start()
    if sends:
        windows(runs_ref, range(own), number + 2, size, stream_ref, outs, lay, False, "start")
        windows(runs_ref, range(own), number + 2, size, stream_ref, outs, lay, False, "wait")
    for c in first:
        c.wait()
    if sends:
        for act in ("start", "wait"):
            for d in range(2):
                for r in range(own, runs_ref.shape[1]):
                    taken, copy = run_copies(runs_ref, d, r, number + 2, size, hold.at[pl.ds(d, 2)], outs[d], lay, True)

                    @pl.when(taken > 0)
                    def _():
                        getattr(copy, act)()
    for c in second:
        c.wait()


def close_kernel(size, number, came_up, came_down, held_ref, hold, sem):
    del held_ref
    rows = size * UNIT
    copies = [
        pltpu.make_async_copy(c, hold.at[2 * d + 1, pl.ds(number * rows, rows)], sem.at[d])
        for d, c in enumerate((came_up, came_down))
    ]
    for c in copies:
        c.start()
    for c in copies:
        c.wait()


def couple_kernel(tasks, width, depth, many, loc_ref, count_ref, target_ref, coef_ref, metric_ref, *refs):
    out_ref, slots, sems = refs[-3], refs[-2], refs[-1]
    buffers = refs[:-3]
    out_ref[...] = jnp.zeros_like(out_ref)

    def fetch(group, phase):
        for u in range(many):
            code = loc_ref[group * many + u]
            row = pl.multiple_of(code & ((1 << ROW_BITS) - 1), UNIT)
            for b, source in enumerate(buffers):

                @pl.when((code >> ROW_BITS) == b)
                def _():
                    pltpu.make_async_copy(source.at[pl.ds(row, width)], slots.at[phase, u], sems.at[phase, u]).start()

    groups = tasks // many
    fetch(0, 0)

    @pl.loop(0, groups)
    def _(group):
        phase = lax.rem(group, 2)

        @pl.when(group + 1 < groups)
        def _():
            fetch(group + 1, 1 - phase)

        terms = []
        for u in range(many):
            pltpu.make_async_copy(buffers[0].at[pl.ds(0, width)], slots.at[phase, u], sems.at[phase, u]).wait()
        for u in range(many):
            t = group * many + u
            held = slots[phase, u]
            rows = lax.broadcasted_iota(jnp.int32, held.shape, 0)
            held = jnp.where(rows < count_ref[t], held, jnp.zeros_like(held))
            turned = lax.dot_general(
                held[:, :depth], metric_ref[target_ref[t]], (((1,), (1,)), ((), ())), preferred_element_type=jnp.float32
            ).astype(jnp.bfloat16)
            half = lax.dot_general(
                turned, held[:, depth:], (((0,), (0,)), ((), ())), preferred_element_type=jnp.float32
            ).astype(jnp.bfloat16)
            terms.append(coef_ref[t] * jnp.dot(half, turned, preferred_element_type=jnp.float32))
        for u in range(many):
            target = target_ref[group * many + u]
            out_ref[target] = out_ref[target] - terms[u]


def couple(location, count, target, coef, metric, buffers, width, depth):
    tasks, pairs = location.shape[0], metric.shape[0]
    many = 4
    return pl.pallas_call(
        functools.partial(couple_kernel, tasks, width, depth, many),
        in_specs=[SMEM] * 4 + [IN_VMEM] + [ANY] * len(buffers),
        out_specs=IN_VMEM,
        out_shape=jax.ShapeDtypeStruct((pairs, width, width), jnp.float32),
        scratch_shapes=[
            pltpu.VMEM((2, many, width, depth + width), jnp.bfloat16),
            pltpu.SemaphoreType.DMA((2, many)),
        ],
        compiler_params=params(),
    )(location, count, target, coef, metric, *buffers)


def relay(size, chips, pairs, width, table, place, need, core, mine, other):
    columns = mine.shape[1]
    stretch = ROUNDS * size + 8
    own = chips - 1
    piece = jax.ShapeDtypeStruct((size * UNIT, columns), mine.dtype)
    stream_shape = jax.ShapeDtypeStruct((2, ROUNDS * size * UNIT, columns), mine.dtype)
    hold_shape = jax.ShapeDtypeStruct((4, stretch * UNIT, columns), mine.dtype)
    members = 2 * chips
    ways = [
        [(i, i + 2) for i in range(members - 2)],
        [(i + 2, i) for i in range(members - 2)],
    ]
    across = [(i, i ^ 1) for i in range(members)]
    stream, *opened = pl.pallas_call(
        functools.partial(open_kernel, size, pairs, width, own),
        in_specs=[SMEM] * 4 + [ANY] * 2,
        out_specs=[ANY] + [IN_VMEM] * 4,
        out_shape=[stream_shape] + [piece] * 4,
        scratch_shapes=[pltpu.VMEM(mine.shape, mine.dtype)] * 2 + [pltpu.SemaphoreType.DMA] * 2,
        compiler_params=params(),
    )(place, need, table, core, mine, other)
    sends = [opened[:2], opened[2:]]
    hold, swapped = None, None
    for number in range(ROUNDS):
        came = [lax.ppermute(sends[number][d], "mem", ways[d]) for d in range(2)]
        ends = number + 2 >= ROUNDS
        operands = [table, stream] + ([hold] if number else []) + came + (swapped if number else [])
        results = pl.pallas_call(
            functools.partial(step_kernel, size, stretch, number, not ends, own),
            in_specs=[SMEM, ANY] + ([ANY] if number else []) + [IN_VMEM] * (4 if number else 2),
            out_specs=[ANY] + ([] if ends else [IN_VMEM] * 2),
            out_shape=[hold_shape] + ([] if ends else [piece] * 2),
            input_output_aliases={2: 0} if number else {},
            scratch_shapes=[pltpu.SemaphoreType.DMA((2,)), pltpu.SemaphoreType.DMA((2,)), pltpu.SemaphoreType.DMA],
            compiler_params=params(),
            cost_estimate=pl.CostEstimate(flops=0, bytes_accessed=12 * size * UNIT * columns * 2, transcendentals=0),
        )(*operands)
        hold = results[0]
        sends.append(results[1:])
        swapped = [lax.ppermute(came[d], "mem", across) for d in range(2)]
    return pl.pallas_call(
        functools.partial(close_kernel, size, ROUNDS - 1),
        in_specs=[IN_VMEM] * 2 + [ANY],
        out_specs=ANY,
        out_shape=hold_shape,
        input_output_aliases={2: 0},
        scratch_shapes=[pltpu.SemaphoreType.DMA((2,))],
        compiler_params=params(),
    )(*swapped, hold)


def shards(
    pno,
    amplitudes,
    pno_count,
    pao_coupling,
    row_owner,
    row_pair,
    row_target,
    row_coef,
    column_owner,
    column_pair,
    column_target,
    column_coef,
):
    pairs, depth, width = pno.shape
    tasks, crossings = row_pair.shape[0], column_pair.shape[0]
    members, groups = lax.axis_size("mem"), lax.axis_size("grp")
    member, group = lax.axis_index("mem"), lax.axis_index("grp")
    row_cap = max(2, 2 * tasks // members)
    col_cap = max(2, 2 * crossings // groups)
    chips = members // 2
    row_owner, column_owner = row_owner[:, 0], column_owner[:, 0]
    row_code = row_owner * pairs + row_pair
    col_code = column_owner * pairs + column_pair
    tell = jnp.concatenate([row_code, col_code, pno_count])
    told = lax.all_to_all(
        jnp.broadcast_to(tell, (groups * members, tell.shape[0])), ("grp", "mem"), split_axis=0, concat_axis=0, tiled=True
    )
    told = told.reshape(groups, members, -1)
    code, cols, count = told[..., :tasks], told[..., tasks : tasks + crossings], told[..., tasks + crossings :]
    blocks = blocks_of(pno, amplitudes, pno_count)
    ids = jnp.arange(members * pairs, dtype=jnp.int32)
    here = pick(count, group).reshape(-1)
    row_count = jnp.sum(jnp.where(row_code[:, None] == ids, here, 0), axis=1)
    beside = lax.dynamic_index_in_dim(count, member, 1, keepdims=False).reshape(-1)
    col_ids = jnp.arange(groups * pairs, dtype=jnp.int32)
    col_count = jnp.sum(jnp.where(col_code[:, None] == col_ids, beside, 0), axis=1)
    ask = lax.dynamic_index_in_dim(cols, member, 1, keepdims=False)
    asked = wanted_from(ask // pairs, ask % pairs, group, col_cap)
    shifts = range(1, groups)
    index = jnp.concatenate([pick(asked, (group + k) % groups) for k in shifts])
    step = (group - column_owner) % groups
    col_row = (ranks_of(column_owner) + 0) * width
    target = jnp.concatenate([row_target, column_target])
    coef = jnp.concatenate([row_coef, column_coef])
    counts = jnp.concatenate([row_count, col_count])

    def crossed():
        parts = take(blocks, index, width, groups - 1)
        return [
            lax.ppermute(parts[k - 1], "grp", [(g, (g + k) % groups) for g in range(groups)]) for k in shifts
        ]

    def finish(location, buffers):
        metric = blocks[:, :depth].astype(jnp.float32) + jnp.dot(
            blocks[:, :depth], pao_coupling, preferred_element_type=jnp.float32
        )
        metric = metric.astype(jnp.bfloat16).reshape(pairs, width, depth)
        from_own = column_pair * width
        first = len(buffers)
        col_location = jnp.where(step == 0, from_own, col_row + ((first + step - 1) << ROW_BITS))
        return couple(
            jnp.concatenate([location, col_location]), counts, target, coef, metric, buffers + crossed(), width, depth
        )

    def plain(*_):
        want = wanted_from(pick(code, group) // pairs, pick(code, group) % pairs, member, row_cap)
        [sent] = take(blocks, want.reshape(-1), width, 1)
        got = lax.all_to_all(sent, "mem", split_axis=0, concat_axis=0, tiled=True)
        location = (row_owner * row_cap + ranks_of(row_owner)) * width + (1 << ROW_BITS)
        return finish(location, [blocks, got])

    if members % 2 or chips < 2 or chips > 4:
        return plain()
    other = lax.ppermute(blocks, "mem", [(i, i ^ 1) for i in range(members)])
    branch, table, place, need, location = relay_plan(code, count, group, member, (row_code, width))
    core = (member % 2).reshape(1).astype(jnp.int32)

    def relayed(size, table, place, need, location, other):
        hold = relay(size, chips, pairs, width, table, place, need, core, blocks, other)
        return finish(location, [blocks, other, hold.reshape(-1, hold.shape[2])])

    branches = [functools.partial(relayed, size) for size in SIZES] + [plain]
    return lax.switch(branch, branches, table, place, need, location, other)


def solution(mesh):
    in_specs = (
        P(("grp", "mem"), None, None),
        P(("grp", "mem"), None, None),
        P(("grp", "mem")),
        P(),
        P(("grp", "mem"), None),
        P(("grp", "mem")),
        P(("grp", "mem")),
        P(("grp", "mem")),
        P(("grp", "mem"), None),
        P(("grp", "mem")),
        P(("grp", "mem")),
        P(("grp", "mem")),
    )
    out_specs = P(("grp", "mem"), None, None)
    return jax.shard_map(shards, mesh=mesh, in_specs=in_specs, out_specs=out_specs, check_vma=False)
```

```python
import functools

import jax
import jax.numpy as jnp
from jax import lax
from jax.experimental import pallas as pl
from jax.experimental.pallas import tpu as pltpu
from jax.sharding import PartitionSpec as P

UNIT = 16
ROUNDS = 10
SIZES = (27, 29, 31, 34)
VMEM = 48 * 2**20
PARTS = (1, 3, 5, 7, 8)
CROSS_AFTER = 6
ROW_BITS = 20
ANY = pl.BlockSpec(memory_space=pl.ANY)
SMEM = pl.BlockSpec(memory_space=pltpu.SMEM)
IN_VMEM = pl.BlockSpec(memory_space=pltpu.VMEM)


def params():
    return pltpu.CompilerParams(vmem_limit_bytes=VMEM)


def block_kernel(count_ref, pno_ref, amp_ref, out_ref):
    step = pl.program_id(0)
    many, depth, width = pno_ref.shape
    for i in range(many):
        count = count_ref[step * many + i]
        rows = lax.broadcasted_iota(jnp.int32, (width, depth), 0)
        turned = pno_ref[i].T
        out_ref[pl.ds(i * width, width), pl.ds(0, depth)] = jnp.where(rows < count, turned, jnp.zeros_like(turned))
        down = lax.broadcasted_iota(jnp.int32, (width, width), 0)
        across = lax.broadcasted_iota(jnp.int32, (width, width), 1)
        amp = amp_ref[i]
        live = (down < count) & (across < count)
        out_ref[pl.ds(i * width, width), pl.ds(depth, width)] = jnp.where(live, amp, jnp.zeros_like(amp))


def blocks_of(pno, amplitudes, pno_count):
    pairs, depth, width = pno.shape
    many = 4
    return pl.pallas_call(
        block_kernel,
        grid=(pairs // many,),
        in_specs=[
            SMEM,
            pl.BlockSpec((many, depth, width), lambda i: (i, 0, 0)),
            pl.BlockSpec((many, width, width), lambda i: (i, 0, 0)),
        ],
        out_specs=pl.BlockSpec((many * width, depth + width), lambda i: (i, 0)),
        out_shape=jax.ShapeDtypeStruct((pairs * width, depth + width), pno.dtype),
        compiler_params=params(),
    )(pno_count, pno, amplitudes)


def pick(array, index):
    return lax.dynamic_index_in_dim(array, index, 0, keepdims=False)


def starts_of(lengths, chips, delay):
    starts, ends = {}, []
    for c in range(chips - 1):
        at = jnp.zeros_like(lengths[0][chips - 1])
        for f in range(chips - 1, c, -1):
            for o in range(c, -1, -1):
                if o < c:
                    at = jnp.where(lengths[o][f] > 0, jnp.maximum(at, starts[o, f, c - 1] + delay), at)
                starts[o, f, c] = at
                at = at + lengths[o][f]
        ends.append(at)
    return starts, functools.reduce(jnp.maximum, ends)


def relay_plan(code, count, group, member, mine):
    groups, members, _ = code.shape
    pairs = count.shape[2]
    chips, items = members // 2, 2 * pairs
    chip, core = member // 2, member % 2
    ids = jnp.arange(members * pairs, dtype=jnp.int32)
    asked = jnp.any(code[..., None, :] == ids[:, None], axis=-1)
    asked = jnp.any(asked.reshape(groups, chips, 2, chips, items), axis=2)
    asked = jnp.stack([asked, asked[:, ::-1, ::-1]])
    line = jnp.arange(chips, dtype=jnp.int32)
    later = (line[:, None] > line[None, :])[:, :, None]
    far = jnp.max(jnp.where(asked & later, line[:, None, None], 0), axis=2)
    units = ((count + UNIT - 1) // UNIT).reshape(groups, chips, items)
    units = jnp.stack([units, units[:, ::-1]])
    order = far * items + (items - 1 - jnp.arange(items, dtype=jnp.int32))
    before = (order[..., None, :] > order[..., :, None]) & (far[..., None, :] > 0)
    lane = jnp.sum(before.astype(jnp.int32), axis=-1) & 1
    kind = far * 2 + lane
    ahead = before & (kind[..., None, :] == kind[..., :, None])
    prefix = jnp.sum(jnp.where(ahead, units[..., None, :], 0), axis=-1)
    kinds = jnp.arange(2 * chips, dtype=jnp.int32)
    total = jnp.sum(jnp.where(kind[..., None, :] == kinds[:, None], units[..., None, :], 0), axis=-1)
    total = total.reshape(2, groups, chips, chips, 2)
    lengths = [[total[:, :, o, f] for f in range(chips)] for o in range(chips)]
    branch, size = jnp.int32(len(SIZES)), jnp.int32(SIZES[-1])
    for b in range(len(SIZES) - 1, -1, -1):
        fits = jnp.max(starts_of(lengths, chips, 2 * SIZES[b])[1]) <= ROUNDS * SIZES[b]
        branch, size = jnp.where(fits, b, branch), jnp.where(fits, SIZES[b], size)

    def own_group(x):
        return lax.dynamic_index_in_dim(x, group, 1, keepdims=False)

    far, lane, prefix, units, total = (own_group(x) for x in (far, lane, prefix, units, total))
    lengths = [[total[:, o, f] for f in range(chips)] for o in range(chips)]
    starts = starts_of(lengths, chips, 2 * size)[0]
    none = jnp.zeros_like(lengths[0][0])
    runs = []
    most = max(c * (chips - 1 - c) for c in range(chips))
    for c in range(chips):
        own = [(starts[c, f, c], lengths[c][f], none) if f > c else (none, none, none) for f in range(1, chips)]
        passed = [(starts[o, f, c], lengths[o][f], starts[o, f, c - 1]) for o in range(c) for f in range(c + 1, chips)]
        passed += [(none, none, none)] * (most - len(passed))
        runs.append(jnp.stack([jnp.stack(r) for r in own + passed]))
    runs = jnp.stack(runs)
    outgo = jnp.stack([jnp.stack([starts[c, f, c] if f > c else none for f in range(chips)]) for c in range(chips)])
    income = jnp.stack(
        [
            jnp.stack([jnp.stack([starts[o, f, c - 1] if o < c <= f else none for f in range(chips)]) for o in range(chips)])
            for c in range(chips)
        ]
    )
    table, place, need, spot, side = [], [], [], [], []
    for d in range(2):
        at = chip if d == 0 else chips - 1 - chip
        table.append(lax.dynamic_index_in_dim(pick(runs, at)[..., d, :], core, 2, keepdims=False))
        home = pick(far[d], at)
        chosen = lax.dynamic_index_in_dim(pick(outgo, at)[:, d, :], core, 1, keepdims=False)
        first = jnp.sum(jnp.where(home[:, None] == line, chosen, 0), axis=1)
        place.append(first + pick(prefix[d], at))
        need.append(jnp.where((home > 0) & (pick(lane[d], at) == core), pick(units[d], at), 0))
        came = pick(income, at)[:, :, d, :]
        hit = (far[d][:, :, None, None] == line[:, None]) & (lane[d][:, :, None, None] == jnp.arange(2, dtype=jnp.int32))
        where = prefix[d] + jnp.sum(jnp.where(hit, came[:, None], 0), axis=(2, 3))
        spot.append(where if d == 0 else where[::-1])
        side.append(lane[d] if d == 0 else lane[d][::-1])
    stretch = ROUNDS * size + 8
    origin = line[:, None]
    item = jnp.arange(items, dtype=jnp.int32)[None, :]
    width = mine[1]
    down = (origin > chip).astype(jnp.int32)
    lies = jnp.where(down == 1, spot[1], spot[0])
    on = jnp.where(down == 1, side[1], side[0])
    far_row = ((2 * down + (on != core)) * stretch + lies) * UNIT + (2 << ROW_BITS)
    near_row = (item % pairs) * width + ((item // pairs != core).astype(jnp.int32) << ROW_BITS)
    rows = jnp.where(origin == chip, near_row, far_row).reshape(-1)
    last = lies + units[0] - 1
    passed = sum((last >= r * size).astype(jnp.int32) for r in range(1, ROUNDS))
    ready = jnp.where(origin == chip, 0, passed + (on != core)).reshape(-1)
    found = mine[0][:, None] == ids
    location = jnp.sum(jnp.where(found, rows, 0), axis=1)
    when = jnp.sum(jnp.where(found, ready, 0), axis=1)
    return branch, jnp.stack(table), jnp.stack(place), jnp.stack(need), location, when


def ranks_of(owner):
    spots = jnp.arange(owner.shape[-1], dtype=jnp.int32)
    ahead = (owner[..., None, :] == owner[..., :, None]) & (spots[None, :] < spots[:, None])
    return jnp.sum(ahead.astype(jnp.int32), axis=-1)


def wanted_from(owner, pair, me, capacity):
    slot = jnp.where(owner == me, ranks_of(owner), capacity)
    hit = slot[:, None, :] == jnp.arange(capacity, dtype=jnp.int32)[:, None]
    return jnp.sum(jnp.where(hit, pair[:, None, :], 0), axis=-1)


def load_all(source, scratch, sem, parts=8):
    rows = source.shape[0] // parts
    return [
        pltpu.make_async_copy(source.at[pl.ds(i * rows, rows)], scratch.at[pl.ds(i * rows, rows)], sem) for i in range(parts)
    ]


def take_kernel(width, index_ref, blocks_ref, *refs):
    outs, (scratch, load, sem) = refs[:-3], refs[-3:]
    slots = outs[0].shape[0] // width
    loads = load_all(blocks_ref, scratch, load)
    for c in loads:
        c.start()
    for c in loads:
        c.wait()

    def copies(i):
        for k, out in enumerate(outs):
            row = pl.multiple_of(index_ref[k * slots + i] * width, UNIT)
            yield pltpu.make_async_copy(
                scratch.at[pl.ds(row, width)], out.at[pl.ds(pl.multiple_of(i * width, UNIT), width)], sem
            )

    @pl.loop(0, slots)
    def _(i):
        for c in copies(i):
            c.start()

    @pl.loop(0, slots)
    def _(i):
        for c in copies(i):
            c.wait()


def take(blocks, index, width, parts):
    slots = index.shape[0] // parts
    shape = jax.ShapeDtypeStruct((slots * width, blocks.shape[1]), blocks.dtype)
    return pl.pallas_call(
        functools.partial(take_kernel, width),
        in_specs=[SMEM, ANY],
        out_specs=[ANY] * parts,
        out_shape=[shape] * parts,
        scratch_shapes=[pltpu.VMEM(blocks.shape, blocks.dtype), pltpu.SemaphoreType.DMA, pltpu.SemaphoreType.DMA],
        compiler_params=params(),
        cost_estimate=pl.CostEstimate(flops=0, bytes_accessed=2 * parts * slots * width * blocks.shape[1] * 2, transcendentals=0),
    )(index, blocks)


def run_copies(runs_ref, d, r, window, size, source, base, out, sem, shift):
    first, length, back = runs_ref[d, r, 0], runs_ref[d, r, 1], runs_ref[d, r, 2]
    low = jnp.maximum(first, window * size)
    high = jnp.minimum(first + length, (window + 1) * size)
    taken = jnp.maximum(high - low, 0)
    begin = back + low - first if shift else low
    rows = taken * UNIT
    return taken, pltpu.make_async_copy(
        source.at[pl.ds(pl.multiple_of((base + jnp.maximum(begin, 0)) * UNIT, UNIT), rows)],
        out.at[pl.ds(pl.multiple_of((low - window * size) * UNIT, UNIT), rows)],
        sem,
    )


def windows(runs_ref, picks, window, size, source, bases, outs, sem, shift, act):
    for d in range(2):
        for r in picks:
            taken, copy = run_copies(runs_ref, d, r, window, size, source, bases[d], outs[d], sem, shift)

            @pl.when(taken > 0)
            def _():
                getattr(copy, act)()


def items_of(pairs, core_ref, sources, visit):
    for half, source in enumerate(sources):

        @pl.loop(0, pairs)
        def _(i):
            for d in range(2):
                visit(source, i, d, (core_ref[0] ^ half) * pairs + i)


def first_kernel(size, pairs, width, place_ref, need_ref, core_ref, mine_ref, other_ref, *refs):
    outs, sem = refs[:-1], refs[-1]

    def each(act):
        def visit(source, i, d, item):
            place, units = place_ref[d, item], need_ref[d, item]
            for w in range(2):
                low = jnp.maximum(place, w * size)
                taken = jnp.maximum(jnp.minimum(place + units, (w + 1) * size) - low, 0)

                @pl.when(taken > 0)
                def _():
                    copy = pltpu.make_async_copy(
                        source.at[pl.ds(pl.multiple_of(i * width + (low - place) * UNIT, UNIT), taken * UNIT)],
                        outs[2 * w + d].at[pl.ds(pl.multiple_of((low - w * size) * UNIT, UNIT), taken * UNIT)],
                        sem,
                    )
                    getattr(copy, act)()

        items_of(pairs, core_ref, (mine_ref, other_ref), visit)

    each("start")
    each("wait")


def stream_kernel(span, pairs, width, place_ref, need_ref, core_ref, mine_ref, other_ref, stream_ref, near, beside, load, sem):
    loads = load_all(mine_ref, near, load) + load_all(other_ref, beside, load)
    for c in loads:
        c.start()
    for c in loads:
        c.wait()

    def each(act):
        def visit(source, i, d, item):
            units = need_ref[d, item]

            @pl.when(units > 0)
            def _():
                copy = pltpu.make_async_copy(
                    source.at[pl.ds(pl.multiple_of(i * width, UNIT), units * UNIT)],
                    stream_ref.at[pl.ds(pl.multiple_of((d * span + place_ref[d, item]) * UNIT, UNIT), units * UNIT)],
                    sem,
                )
                getattr(copy, act)()

        items_of(pairs, core_ref, (near, beside), visit)

    each("start")
    each("wait")


def step_kernel(size, stretch, number, sends, own, runs_ref, stream_ref, *refs):
    refs = list(refs)
    if number > 0:
        refs.pop(0)
    came = [refs.pop(0), refs.pop(0)]
    other = [refs.pop(0), refs.pop(0)] if number > 0 else []
    hold = refs.pop(0)
    outs = [refs.pop(0), refs.pop(0)] if sends else []
    arrive, rest, lay = refs
    rows = size * UNIT
    first = [
        pltpu.make_async_copy(came[d], hold.at[pl.ds(2 * d * stretch * UNIT + number * rows, rows)], arrive.at[d])
        for d in range(2)
    ]
    second = [
        pltpu.make_async_copy(
            other[d], hold.at[pl.ds((2 * d + 1) * stretch * UNIT + (number - 1) * rows, rows)], rest.at[d]
        )
        for d in range(2)
        if other
    ]
    for c in first + second:
        c.start()
    mine, passed = range(own), range(own, runs_ref.shape[1])
    straight, through = (0, ROUNDS * size), (0, 2 * stretch)
    if sends:
        windows(runs_ref, mine, number + 2, size, stream_ref, straight, outs, lay, False, "start")
    for c in first:
        c.wait()
    if sends:
        windows(runs_ref, passed, number + 2, size, hold, through, outs, lay, True, "start")
        windows(runs_ref, mine, number + 2, size, stream_ref, straight, outs, lay, False, "wait")
        windows(runs_ref, passed, number + 2, size, hold, through, outs, lay, True, "wait")
    for c in second:
        c.wait()


def close_kernel(size, stretch, number, came_up, came_down, held_ref, hold, sem):
    del held_ref
    rows = size * UNIT
    copies = [
        pltpu.make_async_copy(c, hold.at[pl.ds((2 * d + 1) * stretch * UNIT + number * rows, rows)], sem.at[d])
        for d, c in enumerate((came_up, came_down))
    ]
    for c in copies:
        c.start()
    for c in copies:
        c.wait()


def couple_kernel(width, depth, many, low, high, begun, threads, loc_ref, when_ref, count_ref, target_ref, coef_ref, metric_ref, *refs):
    refs = list(refs)
    tasks = loc_ref.shape[0] - 1
    acc_ref = refs.pop(0) if begun else None
    line, slots, sems = refs[-3:]
    out_ref = refs[-5] if threads else refs[-4]
    buffers = refs[: -5 if threads else -4]
    out_ref[...] = acc_ref[...] if begun else jnp.zeros_like(out_ref)

    def gather(t, found):
        line[found] = t
        return found + ((when_ref[t] > low) & (when_ref[t] <= high)).astype(jnp.int32)

    found = lax.fori_loop(0, tasks, gather, jnp.int32(0))
    for u in range(many):
        line[found + u] = tasks
    groups = lax.div(found + (many - 1), jnp.int32(many))

    def fetch(group, phase):
        for u in range(many):
            code = loc_ref[line[group * many + u]]
            row = pl.multiple_of(code & ((1 << ROW_BITS) - 1), UNIT)
            for b, source in enumerate(buffers):

                @pl.when((code >> ROW_BITS) == b)
                def _():
                    pltpu.make_async_copy(source.at[pl.ds(row, width)], slots.at[phase, u], sems.at[phase, u]).start()

    @pl.when(groups > 0)
    def _():
        fetch(0, 0)

    @pl.loop(0, groups)
    def _(group):
        phase = lax.rem(group, 2)

        @pl.when(group + 1 < groups)
        def _():
            fetch(group + 1, 1 - phase)

        terms = []
        for u in range(many):
            pltpu.make_async_copy(buffers[0].at[pl.ds(0, width)], slots.at[phase, u], sems.at[phase, u]).wait()
        for u in range(many):
            t = line[group * many + u]
            held = slots[phase, u]
            rows = lax.broadcasted_iota(jnp.int32, held.shape, 0)
            held = jnp.where(rows < count_ref[t], held, jnp.zeros_like(held))
            turned = lax.dot_general(
                held[:, :depth], metric_ref[target_ref[t]], (((1,), (1,)), ((), ())), preferred_element_type=jnp.float32
            ).astype(jnp.bfloat16)
            half = lax.dot_general(
                turned, held[:, depth:], (((0,), (0,)), ((), ())), preferred_element_type=jnp.float32
            ).astype(jnp.bfloat16)
            terms.append(coef_ref[t] * jnp.dot(half, turned, preferred_element_type=jnp.float32))
        for u in range(many):
            target = target_ref[line[group * many + u]]
            out_ref[target] = out_ref[target] - terms[u]


def couple(lists, metric, acc, buffers, low, high, threaded=None):
    tasks, (pairs, width, depth) = lists[0].shape[0] - 1, metric.shape
    many = 4
    operands = list(lists) + [metric] + ([] if acc is None else [acc]) + buffers
    out_shape = [jax.ShapeDtypeStruct((pairs, width, width), jnp.float32)]
    out_specs, aliases = [IN_VMEM], {}
    if threaded is not None:
        at = len(operands) - len(buffers) + threaded
        aliases = {at: 1}
        out_shape.append(jax.ShapeDtypeStruct(operands[at].shape, operands[at].dtype))
        out_specs.append(ANY)
    return pl.pallas_call(
        functools.partial(couple_kernel, width, depth, many, low, high, acc is not None, threaded is not None),
        in_specs=[SMEM] * 5 + [IN_VMEM] * (1 if acc is None else 2) + [ANY] * len(buffers),
        out_specs=out_specs,
        out_shape=out_shape,
        input_output_aliases=aliases,
        scratch_shapes=[
            pltpu.SMEM((tasks + many,), jnp.int32),
            pltpu.VMEM((2, many, width, depth + width), jnp.bfloat16),
            pltpu.SemaphoreType.DMA((2, many)),
        ],
        compiler_params=params(),
    )(*operands)


def relay(size, chips, pairs, width, table, place, need, core, lists, mine, other, metric_of, crossed):
    columns = mine.shape[1]
    stretch = ROUNDS * size + 8
    own = chips - 1
    piece = jax.ShapeDtypeStruct((size * UNIT, columns), mine.dtype)
    stream_shape = jax.ShapeDtypeStruct((2 * ROUNDS * size * UNIT, columns), mine.dtype)
    hold_shape = jax.ShapeDtypeStruct((4 * stretch * UNIT, columns), mine.dtype)
    members = 2 * chips
    ways = [
        [(i, i + 2) for i in range(members - 2)],
        [(i + 2, i) for i in range(members - 2)],
    ]
    across = [(i, i ^ 1) for i in range(members)]
    opened = pl.pallas_call(
        functools.partial(first_kernel, size, pairs, width),
        in_specs=[SMEM] * 3 + [ANY] * 2,
        out_specs=[IN_VMEM] * 4,
        out_shape=[piece] * 4,
        scratch_shapes=[pltpu.SemaphoreType.DMA],
        compiler_params=params(),
    )(place, need, core, mine, other)
    sends = [opened[:2], opened[2:]]
    table, after, _ = lax.optimization_barrier((table, mine, opened[0]))
    stream = pl.pallas_call(
        functools.partial(stream_kernel, ROUNDS * size, pairs, width),
        in_specs=[SMEM] * 3 + [ANY] * 2,
        out_specs=ANY,
        out_shape=stream_shape,
        scratch_shapes=[pltpu.VMEM(mine.shape, mine.dtype)] * 2 + [pltpu.SemaphoreType.DMA] * 2,
        compiler_params=params(),
        cost_estimate=pl.CostEstimate(flops=0, bytes_accessed=6 * mine.size * 2, transcendentals=0),
    )(place, need, core, after, other)
    metric = metric_of(after)
    crossing = crossed(after)
    hold, swapped, acc, done = None, None, None, -1
    cross_at = {}
    for i in range(len(crossing)):
        cross_at.setdefault(2 + (CROSS_AFTER - 2) * i // max(1, len(crossing) - 1), []).append(i)
    for number in range(ROUNDS):
        came = [lax.ppermute(sends[number][d], "mem", ways[d]) for d in range(2)]
        swapping = [lax.ppermute(came[d], "mem", across) for d in range(2)]
        if number in cross_at:
            picked = cross_at[number]
            tied = lax.optimization_barrier(tuple(came) + tuple(crossing[i] for i in picked))
            came = list(tied[:2])
            for i, x in zip(picked, tied[2:]):
                crossing[i] = x
        ends = number + 2 >= ROUNDS
        operands = [table, stream] + ([hold] if number else []) + came + (swapped if number else [])
        results = pl.pallas_call(
            functools.partial(step_kernel, size, stretch, number, not ends, own),
            in_specs=[SMEM, ANY] + ([ANY] if number else []) + [IN_VMEM] * (4 if number else 2),
            out_specs=[ANY] + ([] if ends else [IN_VMEM] * 2),
            out_shape=[hold_shape] + ([] if ends else [piece] * 2),
            input_output_aliases={2: 0} if number else {},
            scratch_shapes=[pltpu.SemaphoreType.DMA((2,)), pltpu.SemaphoreType.DMA((2,)), pltpu.SemaphoreType.DMA],
            compiler_params=params(),
            cost_estimate=pl.CostEstimate(flops=0, bytes_accessed=12 * size * UNIT * columns * 2, transcendentals=0),
        )(*operands)
        hold = results[0]
        sends.append(results[1:])
        swapped = swapping
        if number in PARTS:
            buffers = [mine, other, hold] + (crossing if number >= CROSS_AFTER else [])
            acc, hold = couple(lists, metric, acc, buffers, done, number, 2)
            done = number
    hold = pl.pallas_call(
        functools.partial(close_kernel, size, stretch, ROUNDS - 1),
        in_specs=[IN_VMEM] * 2 + [ANY],
        out_specs=ANY,
        out_shape=hold_shape,
        input_output_aliases={2: 0},
        scratch_shapes=[pltpu.SemaphoreType.DMA((2,))],
        compiler_params=params(),
    )(*swapped, hold)
    [acc] = couple(lists, metric, acc, [mine, other, hold] + crossing, done, ROUNDS)
    return acc


def shards(
    pno,
    amplitudes,
    pno_count,
    pao_coupling,
    row_owner,
    row_pair,
    row_target,
    row_coef,
    column_owner,
    column_pair,
    column_target,
    column_coef,
):
    pairs, depth, width = pno.shape
    tasks, crossings = row_pair.shape[0], column_pair.shape[0]
    members, groups = lax.axis_size("mem"), lax.axis_size("grp")
    member, group = lax.axis_index("mem"), lax.axis_index("grp")
    row_cap = max(2, 2 * tasks // members)
    col_cap = max(2, 2 * crossings // groups)
    chips = members // 2
    row_owner, column_owner = row_owner[:, 0], column_owner[:, 0]
    row_code = row_owner * pairs + row_pair
    col_code = column_owner * pairs + column_pair
    tell = jnp.concatenate([row_code, col_code, pno_count])
    told = lax.all_to_all(
        jnp.broadcast_to(tell, (groups * members, tell.shape[0])), ("grp", "mem"), split_axis=0, concat_axis=0, tiled=True
    )
    told = told.reshape(groups, members, -1)
    code, cols, count = told[..., :tasks], told[..., tasks : tasks + crossings], told[..., tasks + crossings :]
    blocks = blocks_of(pno, amplitudes, pno_count)
    ids = jnp.arange(members * pairs, dtype=jnp.int32)
    here = pick(count, group).reshape(-1)
    row_count = jnp.sum(jnp.where(row_code[:, None] == ids, here, 0), axis=1)
    beside = lax.dynamic_index_in_dim(count, member, 1, keepdims=False).reshape(-1)
    col_ids = jnp.arange(groups * pairs, dtype=jnp.int32)
    col_count = jnp.sum(jnp.where(col_code[:, None] == col_ids, beside, 0), axis=1)
    ask = lax.dynamic_index_in_dim(cols, member, 1, keepdims=False)
    asked = wanted_from(ask // pairs, ask % pairs, group, col_cap)
    shifts = range(1, groups)
    index = jnp.concatenate([pick(asked, (group + k) % groups) for k in shifts]) if groups > 1 else None
    step = (group - column_owner) % groups
    col_row = ranks_of(column_owner) * width

    def metric_of(blocks):
        metric = blocks[:, :depth].astype(jnp.float32) + jnp.dot(
            blocks[:, :depth], pao_coupling, preferred_element_type=jnp.float32
        )
        return metric.astype(jnp.bfloat16).reshape(pairs, width, depth)

    def crossed(blocks):
        parts = take(blocks, index, width, groups - 1) if groups > 1 else []
        return [
            lax.ppermute(parts[k - 1], "grp", [(g, (g + k) % groups) for g in range(groups)]) for k in shifts
        ]

    def lists_of(location, when, first):
        col_location = jnp.where(step == 0, column_pair * width, col_row + ((first + step - 1) << ROW_BITS))
        none = jnp.zeros((1,), jnp.int32)
        return (
            jnp.concatenate([location, col_location, none]),
            jnp.concatenate([when, jnp.full_like(col_location, CROSS_AFTER), none]),
            jnp.concatenate([row_count, col_count, none]),
            jnp.concatenate([row_target, column_target, none]),
            jnp.concatenate([row_coef, column_coef, none.astype(jnp.float32)]),
        )

    def plain(*_):
        want = wanted_from(pick(code, group) // pairs, pick(code, group) % pairs, member, row_cap)
        [sent] = take(blocks, want.reshape(-1), width, 1)
        got = lax.all_to_all(sent, "mem", split_axis=0, concat_axis=0, tiled=True)
        location = (row_owner * row_cap + ranks_of(row_owner)) * width + (1 << ROW_BITS)
        lists = lists_of(location, jnp.zeros_like(location), 2)
        [acc] = couple(lists, metric_of(blocks), None, [blocks, got] + crossed(blocks), -1, ROUNDS)
        return acc

    if members % 2 or chips < 2 or chips > 4:
        return plain()
    other = lax.ppermute(blocks, "mem", [(i, i ^ 1) for i in range(members)])
    branch, table, place, need, location, when = relay_plan(code, count, group, member, (row_code, width))
    core = (member % 2).reshape(1).astype(jnp.int32)

    lists = lists_of(location, when, 3)

    def relayed(size):
        return relay(size, chips, pairs, width, table, place, need, core, lists, blocks, other, metric_of, crossed)

    return lax.switch(branch, [functools.partial(relayed, size) for size in SIZES] + [plain])


def solution(mesh):
    in_specs = (
        P(("grp", "mem"), None, None),
        P(("grp", "mem"), None, None),
        P(("grp", "mem")),
        P(),
        P(("grp", "mem"), None),
        P(("grp", "mem")),
        P(("grp", "mem")),
        P(("grp", "mem")),
        P(("grp", "mem"), None),
        P(("grp", "mem")),
        P(("grp", "mem")),
        P(("grp", "mem")),
    )
    out_specs = P(("grp", "mem"), None, None)
    return jax.shard_map(shards, mesh=mesh, in_specs=in_specs, out_specs=out_specs, check_vma=False)
```

```python
import functools

import jax
import jax.numpy as jnp
from jax import lax
from jax.experimental import pallas as pl
from jax.experimental.pallas import tpu as pltpu
from jax.sharding import PartitionSpec as P

UNIT = 16
ROUNDS = 8
SIZES = (35, 37, 39, 42)
VMEM = 48 * 2**20
PARTS = (2, 4, 6, 7)
CROSS_AFTER = 5
ROW_BITS = 20
MANY = 8
ANY = pl.BlockSpec(memory_space=pl.ANY)
SMEM = pl.BlockSpec(memory_space=pltpu.SMEM)
IN_VMEM = pl.BlockSpec(memory_space=pltpu.VMEM)


def params():
    return pltpu.CompilerParams(vmem_limit_bytes=VMEM)


def block_kernel(count_ref, pno_ref, amp_ref, out_ref):
    step = pl.program_id(0)
    many, depth, width = pno_ref.shape
    for i in range(many):
        count = count_ref[step * many + i]
        rows = lax.broadcasted_iota(jnp.int32, (width, depth), 0)
        turned = pno_ref[i].T
        out_ref[pl.ds(i * width, width), pl.ds(0, depth)] = jnp.where(rows < count, turned, jnp.zeros_like(turned))
        down = lax.broadcasted_iota(jnp.int32, (width, width), 0)
        across = lax.broadcasted_iota(jnp.int32, (width, width), 1)
        amp = amp_ref[i]
        live = (down < count) & (across < count)
        out_ref[pl.ds(i * width, width), pl.ds(depth, width)] = jnp.where(live, amp, jnp.zeros_like(amp))


def blocks_of(pno, amplitudes, pno_count):
    pairs, depth, width = pno.shape
    many = 4
    return pl.pallas_call(
        block_kernel,
        grid=(pairs // many,),
        in_specs=[
            SMEM,
            pl.BlockSpec((many, depth, width), lambda i: (i, 0, 0)),
            pl.BlockSpec((many, width, width), lambda i: (i, 0, 0)),
        ],
        out_specs=pl.BlockSpec((many * width, depth + width), lambda i: (i, 0)),
        out_shape=jax.ShapeDtypeStruct((pairs * width, depth + width), pno.dtype),
        compiler_params=params(),
    )(pno_count, pno, amplitudes)


def pick(array, index):
    return lax.dynamic_index_in_dim(array, index, 0, keepdims=False)


def starts_of(lengths, chips, delay):
    starts, ends = {}, []
    for c in range(chips - 1):
        at = jnp.zeros_like(lengths[0][chips - 1])
        for f in range(chips - 1, c, -1):
            for o in range(c, -1, -1):
                if o < c:
                    at = jnp.where(lengths[o][f] > 0, jnp.maximum(at, starts[o, f, c - 1] + delay), at)
                starts[o, f, c] = at
                at = at + lengths[o][f]
        ends.append(at)
    return starts, functools.reduce(jnp.maximum, ends)


def relay_plan(code, count, group, member, mine):
    groups, members, _ = code.shape
    pairs = count.shape[2]
    chips, items = members // 2, 2 * pairs
    chip, core = member // 2, member % 2
    ids = jnp.arange(members * pairs, dtype=jnp.int32)
    asked = jnp.any(code[..., None, :] == ids[:, None], axis=-1)
    asked = jnp.any(asked.reshape(groups, chips, 2, chips, items), axis=2)
    asked = jnp.stack([asked, asked[:, ::-1, ::-1]])
    line = jnp.arange(chips, dtype=jnp.int32)
    later = (line[:, None] > line[None, :])[:, :, None]
    far = jnp.max(jnp.where(asked & later, line[:, None, None], 0), axis=2)
    units = ((count + UNIT - 1) // UNIT).reshape(groups, chips, items)
    units = jnp.stack([units, units[:, ::-1]])
    order = far * items + (items - 1 - jnp.arange(items, dtype=jnp.int32))
    before = (order[..., None, :] > order[..., :, None]) & (far[..., None, :] > 0)
    lane = jnp.sum(before.astype(jnp.int32), axis=-1) & 1
    kind = far * 2 + lane
    ahead = before & (kind[..., None, :] == kind[..., :, None])
    prefix = jnp.sum(jnp.where(ahead, units[..., None, :], 0), axis=-1)
    kinds = jnp.arange(2 * chips, dtype=jnp.int32)
    total = jnp.sum(jnp.where(kind[..., None, :] == kinds[:, None], units[..., None, :], 0), axis=-1)
    total = total.reshape(2, groups, chips, chips, 2)
    lengths = [[total[:, :, o, f] for f in range(chips)] for o in range(chips)]
    branch, size = jnp.int32(len(SIZES)), jnp.int32(SIZES[-1])
    for b in range(len(SIZES) - 1, -1, -1):
        fits = jnp.max(starts_of(lengths, chips, 2 * SIZES[b])[1]) <= ROUNDS * SIZES[b]
        branch, size = jnp.where(fits, b, branch), jnp.where(fits, SIZES[b], size)

    def own_group(x):
        return lax.dynamic_index_in_dim(x, group, 1, keepdims=False)

    far, lane, prefix, units, total = (own_group(x) for x in (far, lane, prefix, units, total))
    lengths = [[total[:, o, f] for f in range(chips)] for o in range(chips)]
    starts = starts_of(lengths, chips, 2 * size)[0]
    none = jnp.zeros_like(lengths[0][0])
    runs = []
    most = max(c * (chips - 1 - c) for c in range(chips))
    for c in range(chips):
        own = [(starts[c, f, c], lengths[c][f], none) if f > c else (none, none, none) for f in range(1, chips)]
        passed = [(starts[o, f, c], lengths[o][f], starts[o, f, c - 1]) for o in range(c) for f in range(c + 1, chips)]
        passed += [(none, none, none)] * (most - len(passed))
        runs.append(jnp.stack([jnp.stack(r) for r in own + passed]))
    runs = jnp.stack(runs)
    outgo = jnp.stack([jnp.stack([starts[c, f, c] if f > c else none for f in range(chips)]) for c in range(chips)])
    income = jnp.stack(
        [
            jnp.stack([jnp.stack([starts[o, f, c - 1] if o < c <= f else none for f in range(chips)]) for o in range(chips)])
            for c in range(chips)
        ]
    )
    table, place, need, spot, side = [], [], [], [], []
    for d in range(2):
        at = chip if d == 0 else chips - 1 - chip
        table.append(lax.dynamic_index_in_dim(pick(runs, at)[..., d, :], core, 2, keepdims=False))
        home = pick(far[d], at)
        chosen = lax.dynamic_index_in_dim(pick(outgo, at)[:, d, :], core, 1, keepdims=False)
        first = jnp.sum(jnp.where(home[:, None] == line, chosen, 0), axis=1)
        place.append(first + pick(prefix[d], at))
        need.append(jnp.where((home > 0) & (pick(lane[d], at) == core), pick(units[d], at), 0))
        came = pick(income, at)[:, :, d, :]
        hit = (far[d][:, :, None, None] == line[:, None]) & (lane[d][:, :, None, None] == jnp.arange(2, dtype=jnp.int32))
        where = prefix[d] + jnp.sum(jnp.where(hit, came[:, None], 0), axis=(2, 3))
        spot.append(where if d == 0 else where[::-1])
        side.append(lane[d] if d == 0 else lane[d][::-1])
    stretch = ROUNDS * size + 8
    origin = line[:, None]
    item = jnp.arange(items, dtype=jnp.int32)[None, :]
    width = mine[1]
    down = (origin > chip).astype(jnp.int32)
    lies = jnp.where(down == 1, spot[1], spot[0])
    on = jnp.where(down == 1, side[1], side[0])
    far_row = ((2 * down + (on != core)) * stretch + lies) * UNIT + (2 << ROW_BITS)
    near_row = (item % pairs) * width + ((item // pairs != core).astype(jnp.int32) << ROW_BITS)
    rows = jnp.where(origin == chip, near_row, far_row).reshape(-1)
    last = lies + units[0] - 1
    passed = sum((last >= r * size).astype(jnp.int32) for r in range(1, ROUNDS))
    ready = jnp.where(origin == chip, 0, passed + (on != core)).reshape(-1)
    found = mine[0][:, None] == ids
    location = jnp.sum(jnp.where(found, rows, 0), axis=1)
    when = jnp.sum(jnp.where(found, ready, 0), axis=1)
    return branch, jnp.stack(table), jnp.stack(place), jnp.stack(need), location, when


def ranks_of(owner):
    spots = jnp.arange(owner.shape[-1], dtype=jnp.int32)
    ahead = (owner[..., None, :] == owner[..., :, None]) & (spots[None, :] < spots[:, None])
    return jnp.sum(ahead.astype(jnp.int32), axis=-1)


def wanted_from(owner, pair, me, capacity):
    slot = jnp.where(owner == me, ranks_of(owner), capacity)
    hit = slot[:, None, :] == jnp.arange(capacity, dtype=jnp.int32)[:, None]
    return jnp.sum(jnp.where(hit, pair[:, None, :], 0), axis=-1)


def load_all(source, scratch, sem, parts=8):
    rows = source.shape[0] // parts
    return [
        pltpu.make_async_copy(source.at[pl.ds(i * rows, rows)], scratch.at[pl.ds(i * rows, rows)], sem) for i in range(parts)
    ]


def take_kernel(width, index_ref, blocks_ref, *refs):
    outs, (scratch, load, sem) = refs[:-3], refs[-3:]
    slots = outs[0].shape[0] // width
    loads = load_all(blocks_ref, scratch, load)
    for c in loads:
        c.start()
    for c in loads:
        c.wait()

    def copies(i):
        for k, out in enumerate(outs):
            row = pl.multiple_of(index_ref[k * slots + i] * width, UNIT)
            yield pltpu.make_async_copy(
                scratch.at[pl.ds(row, width)], out.at[pl.ds(pl.multiple_of(i * width, UNIT), width)], sem
            )

    @pl.loop(0, slots)
    def _(i):
        for c in copies(i):
            c.start()

    @pl.loop(0, slots)
    def _(i):
        for c in copies(i):
            c.wait()


def take(blocks, index, width, parts):
    slots = index.shape[0] // parts
    shape = jax.ShapeDtypeStruct((slots * width, blocks.shape[1]), blocks.dtype)
    return pl.pallas_call(
        functools.partial(take_kernel, width),
        in_specs=[SMEM, ANY],
        out_specs=[ANY] * parts,
        out_shape=[shape] * parts,
        scratch_shapes=[pltpu.VMEM(blocks.shape, blocks.dtype), pltpu.SemaphoreType.DMA, pltpu.SemaphoreType.DMA],
        compiler_params=params(),
        cost_estimate=pl.CostEstimate(flops=0, bytes_accessed=2 * parts * slots * width * blocks.shape[1] * 2, transcendentals=0),
    )(index, blocks)


def run_copies(runs_ref, d, r, window, size, source, base, out, sem, shift):
    first, length, back = runs_ref[d, r, 0], runs_ref[d, r, 1], runs_ref[d, r, 2]
    low = jnp.maximum(first, window * size)
    high = jnp.minimum(first + length, (window + 1) * size)
    taken = jnp.maximum(high - low, 0)
    begin = back + low - first if shift else low
    rows = taken * UNIT
    return taken, pltpu.make_async_copy(
        source.at[pl.ds(pl.multiple_of((base + jnp.maximum(begin, 0)) * UNIT, UNIT), rows)],
        out.at[pl.ds(pl.multiple_of((low - window * size) * UNIT, UNIT), rows)],
        sem,
    )


def windows(runs_ref, picks, window, size, source, bases, outs, sem, shift, act):
    for d in range(2):
        for r in picks:
            taken, copy = run_copies(runs_ref, d, r, window, size, source, bases[d], outs[d], sem, shift)

            @pl.when(taken > 0)
            def _():
                getattr(copy, act)()


def items_of(pairs, core_ref, sources, visit):
    for half, source in enumerate(sources):

        @pl.loop(0, pairs)
        def _(i):
            for d in range(2):
                visit(source, i, d, (core_ref[0] ^ half) * pairs + i)


def open_kernel(size, pairs, width, own, place_ref, need_ref, runs_ref, core_ref, mine_ref, other_ref, stream_ref, *refs):
    outs, (near, beside, load, sem) = refs[:-4], refs[-4:]
    loads = load_all(mine_ref, near, load) + load_all(other_ref, beside, load)
    for c in loads:
        c.start()
    for c in loads:
        c.wait()
    straight = (0, ROUNDS * size)

    def visit(source, i, d, item):
        units = need_ref[d, item]

        @pl.when(units > 0)
        def _():
            pltpu.make_async_copy(
                source.at[pl.ds(pl.multiple_of(i * width, UNIT), units * UNIT)],
                stream_ref.at[pl.ds(pl.multiple_of((straight[d] + place_ref[d, item]) * UNIT, UNIT), units * UNIT)],
                sem,
            ).start()

    items_of(pairs, core_ref, (near, beside), visit)
    for d in range(2):
        total = sum(runs_ref[d, r, 1] for r in range(own)) * UNIT

        @pl.when(total > 0)
        def _():
            pltpu.make_async_copy(near.at[pl.ds(0, total)], stream_ref.at[pl.ds(0, total)], sem).wait()

    for act in ("start", "wait"):
        for window in range(2):
            windows(runs_ref, range(own), window, size, stream_ref, straight, outs[2 * window : 2 * window + 2], sem, False, act)


def step_kernel(size, stretch, number, sends, own, runs_ref, stream_ref, *refs):
    refs = list(refs)
    if number > 0:
        refs.pop(0)
    came = [refs.pop(0), refs.pop(0)]
    other = [refs.pop(0), refs.pop(0)] if number > 0 else []
    hold = refs.pop(0)
    outs = [refs.pop(0), refs.pop(0)] if sends else []
    arrive, rest, lay = refs
    rows = size * UNIT
    first = [
        pltpu.make_async_copy(came[d], hold.at[pl.ds(2 * d * stretch * UNIT + number * rows, rows)], arrive.at[d])
        for d in range(2)
    ]
    second = [
        pltpu.make_async_copy(
            other[d], hold.at[pl.ds((2 * d + 1) * stretch * UNIT + (number - 1) * rows, rows)], rest.at[d]
        )
        for d in range(2)
        if other
    ]
    for c in first + second:
        c.start()
    mine, passed = range(own), range(own, runs_ref.shape[1])
    straight, through = (0, ROUNDS * size), (0, 2 * stretch)
    if sends:
        windows(runs_ref, mine, number + 2, size, stream_ref, straight, outs, lay, False, "start")
    for c in first:
        c.wait()
    if sends:
        windows(runs_ref, passed, number + 2, size, hold, through, outs, lay, True, "start")
        windows(runs_ref, mine, number + 2, size, stream_ref, straight, outs, lay, False, "wait")
        windows(runs_ref, passed, number + 2, size, hold, through, outs, lay, True, "wait")
    for c in second:
        c.wait()


def close_kernel(size, stretch, number, came_up, came_down, held_ref, hold, sem):
    del held_ref
    rows = size * UNIT
    copies = [
        pltpu.make_async_copy(c, hold.at[pl.ds((2 * d + 1) * stretch * UNIT + number * rows, rows)], sem.at[d])
        for d, c in enumerate((came_up, came_down))
    ]
    for c in copies:
        c.start()
    for c in copies:
        c.wait()


def couple_kernel(width, depth, many, low, high, begun, threads, loc_ref, when_ref, count_ref, target_ref, coef_ref, metric_ref, *refs):
    refs = list(refs)
    tasks = loc_ref.shape[0] - 1
    acc_ref = refs.pop(0) if begun else None
    line, slots, sems = refs[-3:]
    out_ref = refs[-5] if threads else refs[-4]
    buffers = refs[: -5 if threads else -4]
    out_ref[...] = acc_ref[...] if begun else jnp.zeros_like(out_ref)

    def gather(t, found):
        line[found] = t
        return found + ((when_ref[t] > low) & (when_ref[t] <= high)).astype(jnp.int32)

    found = lax.fori_loop(0, tasks, gather, jnp.int32(0))
    for u in range(many):
        line[found + u] = tasks
    groups = lax.div(found + (many - 1), jnp.int32(many))

    def fetch(group, phase):
        for u in range(many):
            code = loc_ref[line[group * many + u]]
            row = pl.multiple_of(code & ((1 << ROW_BITS) - 1), UNIT)
            for b, source in enumerate(buffers):

                @pl.when((code >> ROW_BITS) == b)
                def _():
                    pltpu.make_async_copy(source.at[pl.ds(row, width)], slots.at[phase, u], sems.at[phase, u]).start()

    @pl.when(groups > 0)
    def _():
        fetch(0, 0)

    @pl.loop(0, groups)
    def _(group):
        phase = lax.rem(group, 2)

        @pl.when(group + 1 < groups)
        def _():
            fetch(group + 1, 1 - phase)

        for u in range(many):
            pltpu.make_async_copy(buffers[0].at[pl.ds(0, width)], slots.at[phase, u], sems.at[phase, u]).wait()
        crossed, amps = [], []
        for u in range(many):
            t = line[group * many + u]
            live = lax.broadcasted_iota(jnp.int32, (width, width), 0) < count_ref[t]
            turned = lax.dot_general(
                slots[phase, u, :, pl.ds(0, depth)],
                metric_ref[target_ref[t]],
                (((1,), (1,)), ((), ())),
                preferred_element_type=jnp.float32,
            )
            crossed.append(jnp.where(live, turned, 0.0).astype(jnp.bfloat16))
            amp = slots[phase, u, :, pl.ds(depth, width)]
            amps.append(jnp.where(live, amp, jnp.zeros_like(amp)))
        halves = [
            lax.dot_general(turned, amp, (((0,), (0,)), ((), ())), preferred_element_type=jnp.float32).astype(jnp.bfloat16)
            for turned, amp in zip(crossed, amps)
        ]
        terms = [
            coef_ref[line[group * many + u]] * jnp.dot(halves[u], crossed[u], preferred_element_type=jnp.float32)
            for u in range(many)
        ]
        for u in range(many):
            target = target_ref[line[group * many + u]]
            out_ref[target] = out_ref[target] - terms[u]


def couple(lists, metric, acc, buffers, low, high, threaded=None):
    tasks, (pairs, width, depth) = lists[0].shape[0] - 1, metric.shape
    many = MANY
    operands = list(lists) + [metric] + ([] if acc is None else [acc]) + buffers
    out_shape = [jax.ShapeDtypeStruct((pairs, width, width), jnp.float32)]
    out_specs, aliases = [IN_VMEM], {}
    if threaded is not None:
        at = len(operands) - len(buffers) + threaded
        aliases = {at: 1}
        out_shape.append(jax.ShapeDtypeStruct(operands[at].shape, operands[at].dtype))
        out_specs.append(ANY)
    return pl.pallas_call(
        functools.partial(couple_kernel, width, depth, many, low, high, acc is not None, threaded is not None),
        in_specs=[SMEM] * 5 + [IN_VMEM] * (1 if acc is None else 2) + [ANY] * len(buffers),
        out_specs=out_specs,
        out_shape=out_shape,
        input_output_aliases=aliases,
        scratch_shapes=[
            pltpu.SMEM((tasks + many,), jnp.int32),
            pltpu.VMEM((2, many, width, depth + width), jnp.bfloat16),
            pltpu.SemaphoreType.DMA((2, many)),
        ],
        compiler_params=params(),
        cost_estimate=pl.CostEstimate(flops=0, bytes_accessed=20_000_000, transcendentals=0),
    )(*operands)


def relay(size, chips, pairs, width, table, place, need, core, lists, mine, other, metric_of, cross_take, crossed):
    columns = mine.shape[1]
    stretch = ROUNDS * size + 8
    own = chips - 1
    piece = jax.ShapeDtypeStruct((size * UNIT, columns), mine.dtype)
    stream_shape = jax.ShapeDtypeStruct((2 * ROUNDS * size * UNIT, columns), mine.dtype)
    hold_shape = jax.ShapeDtypeStruct((4 * stretch * UNIT, columns), mine.dtype)
    members = 2 * chips
    ways = [
        [(i, i + 2) for i in range(members - 2)],
        [(i + 2, i) for i in range(members - 2)],
    ]
    across = [(i, i ^ 1) for i in range(members)]
    stream, *opened = pl.pallas_call(
        functools.partial(open_kernel, size, pairs, width, own),
        in_specs=[SMEM] * 4 + [ANY] * 2,
        out_specs=[ANY] + [IN_VMEM] * 4,
        out_shape=[stream_shape] + [piece] * 4,
        scratch_shapes=[pltpu.VMEM(mine.shape, mine.dtype)] * 2 + [pltpu.SemaphoreType.DMA] * 2,
        compiler_params=params(),
        cost_estimate=pl.CostEstimate(flops=0, bytes_accessed=6 * mine.size * 2, transcendentals=0),
    )(place, need, table, core, mine, other)
    sends = [opened[:2], opened[2:]]
    stream, after = lax.optimization_barrier((stream, mine))
    taken = cross_take(after)
    metric, crossing = metric_of(after), None
    hold, swapped, acc, done = None, None, None, -1
    for number in range(ROUNDS):
        came = [lax.ppermute(sends[number][d], "mem", ways[d]) for d in range(2)]
        swapping = [lax.ppermute(came[d], "mem", across) for d in range(2)]
        if number == 0:
            *came, taken, metric = lax.optimization_barrier((*came, taken, metric))
            crossing = crossed(taken)
        elif number == CROSS_AFTER:
            *came, crossing = lax.optimization_barrier((*came, crossing))
        ends = number + 2 >= ROUNDS
        operands = [table, stream] + ([hold] if number else []) + came + (swapped if number else [])
        results = pl.pallas_call(
            functools.partial(step_kernel, size, stretch, number, not ends, own),
            in_specs=[SMEM, ANY] + ([ANY] if number else []) + [IN_VMEM] * (4 if number else 2),
            out_specs=[ANY] + ([] if ends else [IN_VMEM] * 2),
            out_shape=[hold_shape] + ([] if ends else [piece] * 2),
            input_output_aliases={2: 0} if number else {},
            scratch_shapes=[pltpu.SemaphoreType.DMA((2,)), pltpu.SemaphoreType.DMA((2,)), pltpu.SemaphoreType.DMA],
            compiler_params=params(),
            cost_estimate=pl.CostEstimate(flops=0, bytes_accessed=12 * size * UNIT * columns * 2, transcendentals=0),
        )(*operands)
        hold = results[0]
        going = list(results[1:])
        sends.append(going)
        swapped = swapping
        if number in PARTS:
            buffers = [mine, other, hold] + ([crossing] if number >= CROSS_AFTER else [])
            acc, hold = couple(lists, metric, acc, buffers, done, number, 2)
            done = number
    hold = pl.pallas_call(
        functools.partial(close_kernel, size, stretch, ROUNDS - 1),
        in_specs=[IN_VMEM] * 2 + [ANY],
        out_specs=ANY,
        out_shape=hold_shape,
        input_output_aliases={2: 0},
        scratch_shapes=[pltpu.SemaphoreType.DMA((2,))],
        compiler_params=params(),
    )(*swapped, hold)
    [acc] = couple(lists, metric, acc, [mine, other, hold, crossing], done, ROUNDS)
    return acc


def shards(
    pno,
    amplitudes,
    pno_count,
    pao_coupling,
    row_owner,
    row_pair,
    row_target,
    row_coef,
    column_owner,
    column_pair,
    column_target,
    column_coef,
):
    pairs, depth, width = pno.shape
    tasks, crossings = row_pair.shape[0], column_pair.shape[0]
    members, groups = lax.axis_size("mem"), lax.axis_size("grp")
    member, group = lax.axis_index("mem"), lax.axis_index("grp")
    row_cap = max(2, 2 * tasks // members)
    col_cap = max(2, 2 * crossings // groups)
    chips = members // 2
    row_owner, column_owner = row_owner[:, 0], column_owner[:, 0]
    row_code = row_owner * pairs + row_pair
    col_code = column_owner * pairs + column_pair
    tell = jnp.concatenate([row_code, col_code, pno_count])
    told = lax.all_to_all(
        jnp.broadcast_to(tell, (groups * members, tell.shape[0])), ("grp", "mem"), split_axis=0, concat_axis=0, tiled=True
    )
    told = told.reshape(groups, members, -1)
    code, cols, count = told[..., :tasks], told[..., tasks : tasks + crossings], told[..., tasks + crossings :]
    blocks = blocks_of(pno, amplitudes, pno_count)
    ids = jnp.arange(members * pairs, dtype=jnp.int32)
    here = pick(count, group).reshape(-1)
    row_count = jnp.sum(jnp.where(row_code[:, None] == ids, here, 0), axis=1)
    beside = lax.dynamic_index_in_dim(count, member, 1, keepdims=False).reshape(-1)
    col_ids = jnp.arange(groups * pairs, dtype=jnp.int32)
    col_count = jnp.sum(jnp.where(col_code[:, None] == col_ids, beside, 0), axis=1)
    ask = lax.dynamic_index_in_dim(cols, member, 1, keepdims=False)
    asked = wanted_from(ask // pairs, ask % pairs, group, col_cap)
    col_row = (column_owner * col_cap + ranks_of(column_owner)) * width

    def metric_of(blocks):
        metric = blocks[:, :depth].astype(jnp.float32) + jnp.dot(
            blocks[:, :depth], pao_coupling, preferred_element_type=jnp.float32
        )
        return metric.astype(jnp.bfloat16).reshape(pairs, width, depth)

    def cross_take(blocks):
        return take(blocks, asked.reshape(-1), width, 1)[0]

    def crossed(sent):
        return lax.all_to_all(sent, "grp", split_axis=0, concat_axis=0, tiled=True)

    def lists_of(location, when, first):
        col_location = col_row + (first << ROW_BITS)
        none = jnp.zeros((1,), jnp.int32)
        return (
            jnp.concatenate([location, col_location, none]),
            jnp.concatenate([when, jnp.full_like(col_location, CROSS_AFTER), none]),
            jnp.concatenate([row_count, col_count, none]),
            jnp.concatenate([row_target, column_target, none]),
            jnp.concatenate([row_coef, column_coef, none.astype(jnp.float32)]),
        )

    def plain(*_):
        want = wanted_from(pick(code, group) // pairs, pick(code, group) % pairs, member, row_cap)
        [sent] = take(blocks, want.reshape(-1), width, 1)
        got = lax.all_to_all(sent, "mem", split_axis=0, concat_axis=0, tiled=True)
        location = (row_owner * row_cap + ranks_of(row_owner)) * width + (1 << ROW_BITS)
        lists = lists_of(location, jnp.zeros_like(location), 2)
        [acc] = couple(lists, metric_of(blocks), None, [blocks, got, crossed(cross_take(blocks))], -1, ROUNDS)
        return acc

    if members % 2 or chips < 2 or chips > 4:
        return plain()
    other = lax.ppermute(blocks, "mem", [(i, i ^ 1) for i in range(members)])
    branch, table, place, need, location, when = relay_plan(code, count, group, member, (row_code, width))
    core = (member % 2).reshape(1).astype(jnp.int32)

    lists = lists_of(location, when, 3)

    def relayed(size):
        return relay(size, chips, pairs, width, table, place, need, core, lists, blocks, other, metric_of, cross_take, crossed)

    return lax.switch(branch, [functools.partial(relayed, size) for size in SIZES] + [plain])


def solution(mesh):
    in_specs = (
        P(("grp", "mem"), None, None),
        P(("grp", "mem"), None, None),
        P(("grp", "mem")),
        P(),
        P(("grp", "mem"), None),
        P(("grp", "mem")),
        P(("grp", "mem")),
        P(("grp", "mem")),
        P(("grp", "mem"), None),
        P(("grp", "mem")),
        P(("grp", "mem")),
        P(("grp", "mem")),
    )
    out_specs = P(("grp", "mem"), None, None)
    return jax.shard_map(shards, mesh=mesh, in_specs=in_specs, out_specs=out_specs, check_vma=False)
```

```python
import functools

import jax
import jax.numpy as jnp
from jax import lax
from jax.experimental import pallas as pl
from jax.experimental.pallas import tpu as pltpu
from jax.sharding import PartitionSpec as P

UNIT = 16
ROUNDS = 8
SIZES = (35, 37, 39, 42)
VMEM = 48 * 2**20
PARTS = (2, 4, 5)
CROSS_AFTER = 5
ROW_BITS = 20
MANY = 8
ANY = pl.BlockSpec(memory_space=pl.ANY)
SMEM = pl.BlockSpec(memory_space=pltpu.SMEM)
IN_VMEM = pl.BlockSpec(memory_space=pltpu.VMEM)


def params():
    return pltpu.CompilerParams(vmem_limit_bytes=VMEM)


def block_kernel(count_ref, pno_ref, amp_ref, out_ref):
    step = pl.program_id(0)
    many, depth, width = pno_ref.shape
    for i in range(many):
        count = count_ref[step * many + i]
        rows = lax.broadcasted_iota(jnp.int32, (width, depth), 0)
        turned = pno_ref[i].T
        out_ref[pl.ds(i * width, width), pl.ds(0, depth)] = jnp.where(rows < count, turned, jnp.zeros_like(turned))
        down = lax.broadcasted_iota(jnp.int32, (width, width), 0)
        across = lax.broadcasted_iota(jnp.int32, (width, width), 1)
        amp = amp_ref[i]
        live = (down < count) & (across < count)
        out_ref[pl.ds(i * width, width), pl.ds(depth, width)] = jnp.where(live, amp, jnp.zeros_like(amp))


def blocks_of(pno, amplitudes, pno_count):
    pairs, depth, width = pno.shape
    many = 4
    return pl.pallas_call(
        block_kernel,
        grid=(pairs // many,),
        in_specs=[
            SMEM,
            pl.BlockSpec((many, depth, width), lambda i: (i, 0, 0)),
            pl.BlockSpec((many, width, width), lambda i: (i, 0, 0)),
        ],
        out_specs=pl.BlockSpec((many * width, depth + width), lambda i: (i, 0)),
        out_shape=jax.ShapeDtypeStruct((pairs * width, depth + width), pno.dtype),
        compiler_params=pltpu.CompilerParams(vmem_limit_bytes=60 * 2**20),
    )(pno_count, pno, amplitudes)


def metric_kernel(depth, block_ref, coupling_ref, out_ref):
    live = block_ref[:, pl.ds(0, depth)]
    mixed = jnp.dot(live, coupling_ref[...], preferred_element_type=jnp.float32)
    out_ref[...] = (live.astype(jnp.float32) + mixed).astype(out_ref.dtype)


def metric_blocks(blocks, pao_coupling):
    rows, columns = blocks.shape
    depth = pao_coupling.shape[0]
    tile = 512
    return pl.pallas_call(
        functools.partial(metric_kernel, depth),
        grid=(rows // tile,),
        in_specs=[pl.BlockSpec((tile, columns), lambda i: (i, 0)), pl.BlockSpec((depth, depth), lambda i: (0, 0))],
        out_specs=pl.BlockSpec((tile, depth), lambda i: (i, 0)),
        out_shape=jax.ShapeDtypeStruct((rows, depth), blocks.dtype),
        compiler_params=params(),
        cost_estimate=pl.CostEstimate(flops=0, bytes_accessed=20_000_000, transcendentals=0),
    )(blocks, pao_coupling)


def pick(array, index):
    return lax.dynamic_index_in_dim(array, index, 0, keepdims=False)


def starts_of(lengths, chips, delay):
    starts, ends = {}, []
    for c in range(chips - 1):
        at = jnp.zeros_like(lengths[0][chips - 1])
        for f in range(chips - 1, c, -1):
            for o in range(c, -1, -1):
                if o < c:
                    at = jnp.where(lengths[o][f] > 0, jnp.maximum(at, starts[o, f, c - 1] + delay), at)
                starts[o, f, c] = at
                at = at + lengths[o][f]
        ends.append(at)
    return starts, functools.reduce(jnp.maximum, ends)


def relay_plan(code, count, group, member, mine):
    groups, members, _ = code.shape
    pairs = count.shape[2]
    chips, items = members // 2, 2 * pairs
    chip, core = member // 2, member % 2
    ids = jnp.arange(members * pairs, dtype=jnp.int32)
    asked = jnp.any(code[..., None, :] == ids[:, None], axis=-1)
    asked = jnp.any(asked.reshape(groups, chips, 2, chips, items), axis=2)
    asked = jnp.stack([asked, asked[:, ::-1, ::-1]])
    line = jnp.arange(chips, dtype=jnp.int32)
    later = (line[:, None] > line[None, :])[:, :, None]
    far = jnp.max(jnp.where(asked & later, line[:, None, None], 0), axis=2)
    units = ((count + UNIT - 1) // UNIT).reshape(groups, chips, items)
    units = jnp.stack([units, units[:, ::-1]])
    order = far * items + (items - 1 - jnp.arange(items, dtype=jnp.int32))
    before = (order[..., None, :] > order[..., :, None]) & (far[..., None, :] > 0)
    lane = jnp.sum(before.astype(jnp.int32), axis=-1) & 1
    kind = far * 2 + lane
    ahead = before & (kind[..., None, :] == kind[..., :, None])
    prefix = jnp.sum(jnp.where(ahead, units[..., None, :], 0), axis=-1)
    kinds = jnp.arange(2 * chips, dtype=jnp.int32)
    total = jnp.sum(jnp.where(kind[..., None, :] == kinds[:, None], units[..., None, :], 0), axis=-1)
    total = total.reshape(2, groups, chips, chips, 2)
    lengths = [[total[:, :, o, f] for f in range(chips)] for o in range(chips)]
    branch, size = jnp.int32(len(SIZES)), jnp.int32(SIZES[-1])
    for b in range(len(SIZES) - 1, -1, -1):
        fits = jnp.max(starts_of(lengths, chips, 2 * SIZES[b])[1]) <= ROUNDS * SIZES[b]
        branch, size = jnp.where(fits, b, branch), jnp.where(fits, SIZES[b], size)

    def own_group(x):
        return lax.dynamic_index_in_dim(x, group, 1, keepdims=False)

    far, lane, prefix, units, total = (own_group(x) for x in (far, lane, prefix, units, total))
    lengths = [[total[:, o, f] for f in range(chips)] for o in range(chips)]
    starts = starts_of(lengths, chips, 2 * size)[0]
    none = jnp.zeros_like(lengths[0][0])
    runs = []
    most = max(c * (chips - 1 - c) for c in range(chips))
    for c in range(chips):
        own = [(starts[c, f, c], lengths[c][f], none) if f > c else (none, none, none) for f in range(1, chips)]
        passed = [(starts[o, f, c], lengths[o][f], starts[o, f, c - 1]) for o in range(c) for f in range(c + 1, chips)]
        passed += [(none, none, none)] * (most - len(passed))
        runs.append(jnp.stack([jnp.stack(r) for r in own + passed]))
    runs = jnp.stack(runs)
    outgo = jnp.stack([jnp.stack([starts[c, f, c] if f > c else none for f in range(chips)]) for c in range(chips)])
    income = jnp.stack(
        [
            jnp.stack([jnp.stack([starts[o, f, c - 1] if o < c <= f else none for f in range(chips)]) for o in range(chips)])
            for c in range(chips)
        ]
    )
    table, place, need, spot, side = [], [], [], [], []
    for d in range(2):
        at = chip if d == 0 else chips - 1 - chip
        table.append(lax.dynamic_index_in_dim(pick(runs, at)[..., d, :], core, 2, keepdims=False))
        home = pick(far[d], at)
        chosen = lax.dynamic_index_in_dim(pick(outgo, at)[:, d, :], core, 1, keepdims=False)
        first = jnp.sum(jnp.where(home[:, None] == line, chosen, 0), axis=1)
        place.append(first + pick(prefix[d], at))
        need.append(jnp.where((home > 0) & (pick(lane[d], at) == core), pick(units[d], at), 0))
        came = pick(income, at)[:, :, d, :]
        hit = (far[d][:, :, None, None] == line[:, None]) & (lane[d][:, :, None, None] == jnp.arange(2, dtype=jnp.int32))
        where = prefix[d] + jnp.sum(jnp.where(hit, came[:, None], 0), axis=(2, 3))
        spot.append(where if d == 0 else where[::-1])
        side.append(lane[d] if d == 0 else lane[d][::-1])
    stretch = ROUNDS * size + 8
    origin = line[:, None]
    item = jnp.arange(items, dtype=jnp.int32)[None, :]
    width = mine[1]
    down = (origin > chip).astype(jnp.int32)
    lies = jnp.where(down == 1, spot[1], spot[0])
    on = jnp.where(down == 1, side[1], side[0])
    far_row = ((2 * down + (on != core)) * stretch + lies) * UNIT + (2 << ROW_BITS)
    near_row = (item % pairs) * width + ((item // pairs != core).astype(jnp.int32) << ROW_BITS)
    rows = jnp.where(origin == chip, near_row, far_row).reshape(-1)
    last = lies + units[0] - 1
    passed = sum((last >= r * size).astype(jnp.int32) for r in range(1, ROUNDS))
    ready = jnp.where(origin == chip, 0, passed + (on != core)).reshape(-1)
    found = mine[0][:, None] == ids
    location = jnp.sum(jnp.where(found, rows, 0), axis=1)
    when = jnp.sum(jnp.where(found, ready, 0), axis=1)
    return branch, jnp.stack(table), jnp.stack(place), jnp.stack(need), location, when


def ranks_of(owner):
    spots = jnp.arange(owner.shape[-1], dtype=jnp.int32)
    ahead = (owner[..., None, :] == owner[..., :, None]) & (spots[None, :] < spots[:, None])
    return jnp.sum(ahead.astype(jnp.int32), axis=-1)


def wanted_from(owner, pair, me, capacity):
    slot = jnp.where(owner == me, ranks_of(owner), capacity)
    hit = slot[:, None, :] == jnp.arange(capacity, dtype=jnp.int32)[:, None]
    return jnp.sum(jnp.where(hit, pair[:, None, :], 0), axis=-1)


def load_all(source, scratch, sem, parts=8):
    rows = source.shape[0] // parts
    return [
        pltpu.make_async_copy(source.at[pl.ds(i * rows, rows)], scratch.at[pl.ds(i * rows, rows)], sem) for i in range(parts)
    ]


def take_kernel(width, index_ref, blocks_ref, *refs):
    outs, (scratch, load, sem) = refs[:-3], refs[-3:]
    slots = outs[0].shape[0] // width
    loads = load_all(blocks_ref, scratch, load)
    for c in loads:
        c.start()
    for c in loads:
        c.wait()

    def copies(i):
        for k, out in enumerate(outs):
            row = pl.multiple_of(index_ref[k * slots + i] * width, UNIT)
            yield pltpu.make_async_copy(
                scratch.at[pl.ds(row, width)], out.at[pl.ds(pl.multiple_of(i * width, UNIT), width)], sem
            )

    @pl.loop(0, slots)
    def _(i):
        for c in copies(i):
            c.start()

    @pl.loop(0, slots)
    def _(i):
        for c in copies(i):
            c.wait()


def take(blocks, index, width, parts):
    slots = index.shape[0] // parts
    shape = jax.ShapeDtypeStruct((slots * width, blocks.shape[1]), blocks.dtype)
    return pl.pallas_call(
        functools.partial(take_kernel, width),
        in_specs=[SMEM, ANY],
        out_specs=[ANY] * parts,
        out_shape=[shape] * parts,
        scratch_shapes=[pltpu.VMEM(blocks.shape, blocks.dtype), pltpu.SemaphoreType.DMA, pltpu.SemaphoreType.DMA],
        compiler_params=params(),
        cost_estimate=pl.CostEstimate(flops=0, bytes_accessed=2 * parts * slots * width * blocks.shape[1] * 2, transcendentals=0),
    )(index, blocks)


def run_copies(runs_ref, d, r, window, size, source, base, out, sem, shift):
    first, length, back = runs_ref[d, r, 0], runs_ref[d, r, 1], runs_ref[d, r, 2]
    low = jnp.maximum(first, window * size)
    high = jnp.minimum(first + length, (window + 1) * size)
    taken = jnp.maximum(high - low, 0)
    begin = back + low - first if shift else low
    rows = taken * UNIT
    return taken, pltpu.make_async_copy(
        source.at[pl.ds(pl.multiple_of((base + jnp.maximum(begin, 0)) * UNIT, UNIT), rows)],
        out.at[pl.ds(pl.multiple_of((low - window * size) * UNIT, UNIT), rows)],
        sem,
    )


def windows(runs_ref, picks, window, size, source, bases, outs, sem, shift, act):
    for d in range(2):
        for r in picks:
            taken, copy = run_copies(runs_ref, d, r, window, size, source, bases[d], outs[d], sem, shift)

            @pl.when(taken > 0)
            def _():
                getattr(copy, act)()


def items_of(pairs, core_ref, sources, visit):
    for half, source in enumerate(sources):

        @pl.loop(0, pairs)
        def _(i):
            for d in range(2):
                visit(source, i, d, (core_ref[0] ^ half) * pairs + i)


def open_kernel(size, pairs, width, own, place_ref, need_ref, runs_ref, core_ref, mine_ref, other_ref, stream_ref, *refs):
    outs, (near, beside, load, sem) = refs[:-4], refs[-4:]
    loads = load_all(mine_ref, near, load) + load_all(other_ref, beside, load)
    for c in loads:
        c.start()
    for c in loads:
        c.wait()
    straight = (0, ROUNDS * size)

    def visit(source, i, d, item):
        units = need_ref[d, item]

        @pl.when(units > 0)
        def _():
            pltpu.make_async_copy(
                source.at[pl.ds(pl.multiple_of(i * width, UNIT), units * UNIT)],
                stream_ref.at[pl.ds(pl.multiple_of((straight[d] + place_ref[d, item]) * UNIT, UNIT), units * UNIT)],
                sem,
            ).start()

    items_of(pairs, core_ref, (near, beside), visit)
    for d in range(2):
        total = sum(runs_ref[d, r, 1] for r in range(own)) * UNIT

        @pl.when(total > 0)
        def _():
            pltpu.make_async_copy(near.at[pl.ds(0, total)], stream_ref.at[pl.ds(0, total)], sem).wait()

    for act in ("start", "wait"):
        for window in range(2):
            part = [out.at[pl.ds(window * size * UNIT, size * UNIT)] for out in outs]
            windows(runs_ref, range(own), window, size, stream_ref, straight, part, sem, False, act)


def step_kernel(size, stretch, own, at, other_at, next_windows, runs_ref, stream_ref, *refs):
    refs = list(refs)
    if other_at is not None:
        refs.pop(0)
    came = [refs.pop(0), refs.pop(0)]
    other = [refs.pop(0), refs.pop(0)] if other_at is not None else []
    hold = refs.pop(0)
    arrive, rest, lay = refs[-3:]
    outs = refs[:-3]
    rows = size * UNIT

    def filed(piece, section, number, sem):
        return pltpu.make_async_copy(
            piece, hold.at[pl.ds(section * stretch * UNIT + number * rows, piece.shape[0])], sem
        )

    first = [filed(c, 2 * d, at, arrive.at[d]) for d, c in enumerate(came)]
    second = [filed(c, 2 * d + 1, other_at, rest.at[d]) for d, c in enumerate(other)]
    for c in first + second:
        c.start()
    straight, through = (0, ROUNDS * size), (0, 2 * stretch)

    def lay_out(passed, act):
        picks = range(own, runs_ref.shape[1]) if passed else range(own)
        for i, window in enumerate(next_windows):
            source, bases = (hold, through) if passed else (stream_ref, straight)
            windows(runs_ref, picks, window, size, source, bases, outs[2 * i : 2 * i + 2], lay, passed, act)

    lay_out(False, "start")
    for c in first:
        c.wait()
    lay_out(True, "start")
    lay_out(False, "wait")
    lay_out(True, "wait")
    for c in second:
        c.wait()


def close_kernel(size, stretch, number, came_up, came_down, held_ref, hold, sem):
    del held_ref
    rows = size * UNIT
    copies = [
        pltpu.make_async_copy(c, hold.at[pl.ds((2 * d + 1) * stretch * UNIT + number * rows, rows)], sem.at[d])
        for d, c in enumerate((came_up, came_down))
    ]
    for c in copies:
        c.start()
    for c in copies:
        c.wait()


def couple_kernel(width, depth, many, low, high, begun, threads, loc_ref, when_ref, count_ref, target_ref, coef_ref, metric_ref, *refs):
    refs = list(refs)
    tasks = loc_ref.shape[0] - 1
    acc_ref = refs.pop(0) if begun else None
    line, slots, sems = refs[-3:]
    out_ref = refs[-5] if threads else refs[-4]
    buffers = refs[: -5 if threads else -4]
    out_ref[...] = acc_ref[...] if begun else jnp.zeros_like(out_ref)

    def gather(t, found):
        line[found] = t
        return found + ((when_ref[t] > low) & (when_ref[t] <= high)).astype(jnp.int32)

    found = lax.fori_loop(0, tasks, gather, jnp.int32(0))
    for u in range(many):
        line[found + u] = tasks
    groups = lax.div(found + (many - 1), jnp.int32(many))

    def fetch(group, phase):
        for u in range(many):
            code = loc_ref[line[group * many + u]]
            row = pl.multiple_of(code & ((1 << ROW_BITS) - 1), UNIT)
            for b, source in enumerate(buffers):

                @pl.when((code >> ROW_BITS) == b)
                def _():
                    pltpu.make_async_copy(source.at[pl.ds(row, width)], slots.at[phase, u], sems.at[phase, u]).start()

    @pl.when(groups > 0)
    def _():
        fetch(0, 0)

    @pl.loop(0, groups)
    def _(group):
        phase = lax.rem(group, 2)

        @pl.when(group + 1 < groups)
        def _():
            fetch(group + 1, 1 - phase)

        for u in range(many):
            pltpu.make_async_copy(buffers[0].at[pl.ds(0, width)], slots.at[phase, u], sems.at[phase, u]).wait()
        crossed, amps = [], []
        for u in range(many):
            t = line[group * many + u]
            live = lax.broadcasted_iota(jnp.int32, (width, width), 0) < count_ref[t]
            turned = lax.dot_general(
                slots[phase, u, :, pl.ds(0, depth)],
                metric_ref[target_ref[t]],
                (((1,), (1,)), ((), ())),
                preferred_element_type=jnp.float32,
            )
            crossed.append(jnp.where(live, turned, 0.0).astype(jnp.bfloat16))
            amp = slots[phase, u, :, pl.ds(depth, width)]
            amps.append(jnp.where(live, amp, jnp.zeros_like(amp)))
        halves = [
            lax.dot_general(turned, amp, (((0,), (0,)), ((), ())), preferred_element_type=jnp.float32).astype(jnp.bfloat16)
            for turned, amp in zip(crossed, amps)
        ]
        terms = [
            coef_ref[line[group * many + u]] * jnp.dot(halves[u], crossed[u], preferred_element_type=jnp.float32)
            for u in range(many)
        ]
        for u in range(many):
            target = target_ref[line[group * many + u]]
            out_ref[target] = out_ref[target] - terms[u]


def couple(lists, metric, acc, buffers, low, high, threaded=None):
    tasks, (pairs, width, depth) = lists[0].shape[0] - 1, metric.shape
    many = MANY
    operands = list(lists) + [metric] + ([] if acc is None else [acc]) + buffers
    out_shape = [jax.ShapeDtypeStruct((pairs, width, width), jnp.float32)]
    out_specs, aliases = [IN_VMEM], {}
    if threaded is not None:
        at = len(operands) - len(buffers) + threaded
        aliases = {at: 1}
        out_shape.append(jax.ShapeDtypeStruct(operands[at].shape, operands[at].dtype))
        out_specs.append(ANY)
    return pl.pallas_call(
        functools.partial(couple_kernel, width, depth, many, low, high, acc is not None, threaded is not None),
        in_specs=[SMEM] * 5 + [IN_VMEM] * (1 if acc is None else 2) + [ANY] * len(buffers),
        out_specs=out_specs,
        out_shape=out_shape,
        input_output_aliases=aliases,
        scratch_shapes=[
            pltpu.SMEM((tasks + many,), jnp.int32),
            pltpu.VMEM((2, many, width, depth + width), jnp.bfloat16),
            pltpu.SemaphoreType.DMA((2, many)),
        ],
        compiler_params=params(),
        cost_estimate=pl.CostEstimate(flops=0, bytes_accessed=20_000_000, transcendentals=0),
    )(*operands)


def relay(size, chips, pairs, width, table, place, need, core, lists, mine, other, metric_of, cross_take, crossed):
    columns = mine.shape[1]
    stretch = ROUNDS * size + 8
    own = chips - 1
    piece = jax.ShapeDtypeStruct((size * UNIT, columns), mine.dtype)
    double = jax.ShapeDtypeStruct((2 * size * UNIT, columns), mine.dtype)
    stream_shape = jax.ShapeDtypeStruct((2 * ROUNDS * size * UNIT, columns), mine.dtype)
    hold_shape = jax.ShapeDtypeStruct((4 * stretch * UNIT, columns), mine.dtype)
    members = 2 * chips
    ways = [
        [(i, i + 2) for i in range(members - 2)],
        [(i + 2, i) for i in range(members - 2)],
    ]
    across = [(i, i ^ 1) for i in range(members)]
    stream, *opened = pl.pallas_call(
        functools.partial(open_kernel, size, pairs, width, own),
        in_specs=[SMEM] * 4 + [ANY] * 2,
        out_specs=[ANY] + [IN_VMEM] * 2,
        out_shape=[stream_shape] + [double] * 2,
        scratch_shapes=[pltpu.VMEM(mine.shape, mine.dtype)] * 2 + [pltpu.SemaphoreType.DMA] * 2,
        compiler_params=params(),
        cost_estimate=pl.CostEstimate(flops=0, bytes_accessed=6 * mine.size * 2, transcendentals=0),
    )(place, need, table, core, mine, other)
    sends = {1: opened}
    stream, after = lax.optimization_barrier((stream, mine))
    taken = cross_take(after)
    metric, crossing = metric_of(after), crossed(taken)
    hold, swapped, acc, done = None, None, None, -1
    for number in range(1, ROUNDS):
        came = [lax.ppermute(sends[number][d], "mem", ways[d]) for d in range(2)]
        swapping = [lax.ppermute(came[d], "mem", across) for d in range(2)]
        if number == 1:
            *came, _, metric = lax.optimization_barrier((*came, taken, metric))
        elif number == CROSS_AFTER:
            *came, crossing = lax.optimization_barrier((*came, crossing))
        begun = hold is not None
        ahead = [w for w in ((2, 3) if number == 1 else (number + 2,)) if w < ROUNDS]
        operands = [table, stream] + ([hold] if begun else []) + came + (swapped if begun else [])
        hold, *going = pl.pallas_call(
            functools.partial(
                step_kernel,
                size,
                stretch,
                own,
                0 if number == 1 else number,
                None if not begun else (0 if number == 2 else number - 1),
                ahead,
            ),
            in_specs=[SMEM, ANY] + ([ANY] if begun else []) + [IN_VMEM] * (4 if begun else 2),
            out_specs=[ANY] + [IN_VMEM] * (2 * len(ahead)),
            out_shape=[hold_shape] + [piece] * (2 * len(ahead)),
            input_output_aliases={2: 0} if begun else {},
            scratch_shapes=[pltpu.SemaphoreType.DMA((2,)), pltpu.SemaphoreType.DMA((2,)), pltpu.SemaphoreType.DMA],
            compiler_params=params(),
            cost_estimate=pl.CostEstimate(flops=0, bytes_accessed=12 * size * UNIT * columns * 2, transcendentals=0),
        )(*operands)
        swapped = swapping
        if number in PARTS:
            buffers = [mine, other, hold] + ([crossing] if number >= CROSS_AFTER else [])
            acc, hold = couple(lists, metric, acc, buffers, done, number, 2)
            done = number
            if number == PARTS[-1]:
                *going, acc = lax.optimization_barrier((*going, acc))
        for i, window in enumerate(ahead):
            sends[window] = going[2 * i : 2 * i + 2]
    hold = pl.pallas_call(
        functools.partial(close_kernel, size, stretch, ROUNDS - 1),
        in_specs=[IN_VMEM] * 2 + [ANY],
        out_specs=ANY,
        out_shape=hold_shape,
        input_output_aliases={2: 0},
        scratch_shapes=[pltpu.SemaphoreType.DMA((2,))],
        compiler_params=params(),
    )(*swapped, hold)
    [acc] = couple(lists, metric, acc, [mine, other, hold, crossing], done, ROUNDS)
    return acc


def shards(
    pno,
    amplitudes,
    pno_count,
    pao_coupling,
    row_owner,
    row_pair,
    row_target,
    row_coef,
    column_owner,
    column_pair,
    column_target,
    column_coef,
):
    pairs, depth, width = pno.shape
    tasks, crossings = row_pair.shape[0], column_pair.shape[0]
    members, groups = lax.axis_size("mem"), lax.axis_size("grp")
    member, group = lax.axis_index("mem"), lax.axis_index("grp")
    row_cap = max(2, 2 * tasks // members)
    col_cap = max(2, 2 * crossings // groups)
    chips = members // 2
    row_owner, column_owner = row_owner[:, 0], column_owner[:, 0]
    row_code = row_owner * pairs + row_pair
    col_code = column_owner * pairs + column_pair
    tell = jnp.concatenate([row_code, col_code, pno_count])
    told = lax.all_to_all(
        jnp.broadcast_to(tell, (groups * members, tell.shape[0])), ("grp", "mem"), split_axis=0, concat_axis=0, tiled=True
    )
    told = told.reshape(groups, members, -1)
    code, cols, count = told[..., :tasks], told[..., tasks : tasks + crossings], told[..., tasks + crossings :]
    blocks = blocks_of(pno, amplitudes, pno_count)
    ids = jnp.arange(members * pairs, dtype=jnp.int32)
    here = pick(count, group).reshape(-1)
    row_count = jnp.sum(jnp.where(row_code[:, None] == ids, here, 0), axis=1)
    beside = lax.dynamic_index_in_dim(count, member, 1, keepdims=False).reshape(-1)
    col_ids = jnp.arange(groups * pairs, dtype=jnp.int32)
    col_count = jnp.sum(jnp.where(col_code[:, None] == col_ids, beside, 0), axis=1)
    ask = lax.dynamic_index_in_dim(cols, member, 1, keepdims=False)
    asked = wanted_from(ask // pairs, ask % pairs, group, col_cap)
    col_row = (column_owner * col_cap + ranks_of(column_owner)) * width

    def metric_of(blocks):
        return metric_blocks(blocks, pao_coupling).reshape(pairs, width, depth)

    def cross_take(blocks):
        return take(blocks, asked.reshape(-1), width, 1)[0]

    def crossed(sent):
        return lax.all_to_all(sent, "grp", split_axis=0, concat_axis=0, tiled=True)

    def lists_of(location, when, first):
        col_location = col_row + (first << ROW_BITS)
        none = jnp.zeros((1,), jnp.int32)
        return (
            jnp.concatenate([location, col_location, none]),
            jnp.concatenate([when, jnp.full_like(col_location, CROSS_AFTER), none]),
            jnp.concatenate([row_count, col_count, none]),
            jnp.concatenate([row_target, column_target, none]),
            jnp.concatenate([row_coef, column_coef, none.astype(jnp.float32)]),
        )

    def plain(*_):
        want = wanted_from(pick(code, group) // pairs, pick(code, group) % pairs, member, row_cap)
        [sent] = take(blocks, want.reshape(-1), width, 1)
        got = lax.all_to_all(sent, "mem", split_axis=0, concat_axis=0, tiled=True)
        location = (row_owner * row_cap + ranks_of(row_owner)) * width + (1 << ROW_BITS)
        lists = lists_of(location, jnp.zeros_like(location), 2)
        [acc] = couple(lists, metric_of(blocks), None, [blocks, got, crossed(cross_take(blocks))], -1, ROUNDS)
        return acc

    if members % 2 or chips < 2 or chips > 4:
        return plain()
    other = lax.ppermute(blocks, "mem", [(i, i ^ 1) for i in range(members)])
    branch, table, place, need, location, when = relay_plan(code, count, group, member, (row_code, width))
    core = (member % 2).reshape(1).astype(jnp.int32)

    lists = lists_of(location, when, 3)

    def relayed(size):
        return relay(size, chips, pairs, width, table, place, need, core, lists, blocks, other, metric_of, cross_take, crossed)

    return lax.switch(branch, [functools.partial(relayed, size) for size in SIZES] + [plain])


def solution(mesh):
    in_specs = (
        P(("grp", "mem"), None, None),
        P(("grp", "mem"), None, None),
        P(("grp", "mem")),
        P(),
        P(("grp", "mem"), None),
        P(("grp", "mem")),
        P(("grp", "mem")),
        P(("grp", "mem")),
        P(("grp", "mem"), None),
        P(("grp", "mem")),
        P(("grp", "mem")),
        P(("grp", "mem")),
    )
    out_specs = P(("grp", "mem"), None, None)
    return jax.shard_map(shards, mesh=mesh, in_specs=in_specs, out_specs=out_specs, check_vma=False)
```

```python
import functools

import jax
import jax.numpy as jnp
from jax import lax
from jax.experimental import pallas as pl
from jax.experimental.pallas import tpu as pltpu
from jax.sharding import PartitionSpec as P

UNIT = 16
PLANS = ((8, 35), (8, 37), (9, 35), (9, 37))
VMEM = 48 * 2**20
CROSS_AFTER = 5
ROW_BITS = 20
MANY = 8
ANY = pl.BlockSpec(memory_space=pl.ANY)
SMEM = pl.BlockSpec(memory_space=pltpu.SMEM)
IN_VMEM = pl.BlockSpec(memory_space=pltpu.VMEM)


def params():
    return pltpu.CompilerParams(vmem_limit_bytes=VMEM)


def block_kernel(count_ref, pno_ref, amp_ref, out_ref):
    step = pl.program_id(0)
    many, depth, width = pno_ref.shape
    for i in range(many):
        count = count_ref[step * many + i]
        rows = lax.broadcasted_iota(jnp.int32, (width, depth), 0)
        turned = pno_ref[i].T
        out_ref[pl.ds(i * width, width), pl.ds(0, depth)] = jnp.where(rows < count, turned, jnp.zeros_like(turned))
        down = lax.broadcasted_iota(jnp.int32, (width, width), 0)
        across = lax.broadcasted_iota(jnp.int32, (width, width), 1)
        amp = amp_ref[i]
        live = (down < count) & (across < count)
        out_ref[pl.ds(i * width, width), pl.ds(depth, width)] = jnp.where(live, amp, jnp.zeros_like(amp))


def blocks_of(pno, amplitudes, pno_count):
    pairs, depth, width = pno.shape
    many = 4
    return pl.pallas_call(
        block_kernel,
        grid=(pairs // many,),
        in_specs=[
            SMEM,
            pl.BlockSpec((many, depth, width), lambda i: (i, 0, 0)),
            pl.BlockSpec((many, width, width), lambda i: (i, 0, 0)),
        ],
        out_specs=pl.BlockSpec((many * width, depth + width), lambda i: (i, 0)),
        out_shape=jax.ShapeDtypeStruct((pairs * width, depth + width), pno.dtype),
        compiler_params=pltpu.CompilerParams(vmem_limit_bytes=60 * 2**20),
    )(pno_count, pno, amplitudes)


def metric_kernel(depth, block_ref, coupling_ref, out_ref):
    live = block_ref[:, pl.ds(0, depth)]
    mixed = jnp.dot(live, coupling_ref[...], preferred_element_type=jnp.float32)
    out_ref[...] = (live.astype(jnp.float32) + mixed).astype(out_ref.dtype)


def metric_blocks(blocks, pao_coupling):
    rows, columns = blocks.shape
    depth = pao_coupling.shape[0]
    tile = 512
    return pl.pallas_call(
        functools.partial(metric_kernel, depth),
        grid=(rows // tile,),
        in_specs=[pl.BlockSpec((tile, columns), lambda i: (i, 0)), pl.BlockSpec((depth, depth), lambda i: (0, 0))],
        out_specs=pl.BlockSpec((tile, depth), lambda i: (i, 0)),
        out_shape=jax.ShapeDtypeStruct((rows, depth), blocks.dtype),
        compiler_params=params(),
        cost_estimate=pl.CostEstimate(flops=0, bytes_accessed=20_000_000, transcendentals=0),
    )(blocks, pao_coupling)


def pick(array, index):
    return lax.dynamic_index_in_dim(array, index, 0, keepdims=False)


def starts_of(lengths, chips, delay):
    starts, ends = {}, []
    for c in range(chips - 1):
        at = jnp.zeros_like(lengths[0][chips - 1])
        for f in range(chips - 1, c, -1):
            for o in range(c, -1, -1):
                if o < c:
                    at = jnp.where(lengths[o][f] > 0, jnp.maximum(at, starts[o, f, c - 1] + delay), at)
                starts[o, f, c] = at
                at = at + lengths[o][f]
        ends.append(at)
    return starts, functools.reduce(jnp.maximum, ends)


def relay_plan(code, count, group, member, mine):
    groups, members, _ = code.shape
    pairs = count.shape[2]
    chips, items = members // 2, 2 * pairs
    chip, core = member // 2, member % 2
    ids = jnp.arange(members * pairs, dtype=jnp.int32)
    asked = jnp.any(code[..., None, :] == ids[:, None], axis=-1)
    asked = jnp.any(asked.reshape(groups, chips, 2, chips, items), axis=2)
    asked = jnp.stack([asked, asked[:, ::-1, ::-1]])
    line = jnp.arange(chips, dtype=jnp.int32)
    later = (line[:, None] > line[None, :])[:, :, None]
    far = jnp.max(jnp.where(asked & later, line[:, None, None], 0), axis=2)
    units = ((count + UNIT - 1) // UNIT).reshape(groups, chips, items)
    units = jnp.stack([units, units[:, ::-1]])
    order = far * items + (items - 1 - jnp.arange(items, dtype=jnp.int32))
    before = (order[..., None, :] > order[..., :, None]) & (far[..., None, :] > 0)
    lane = jnp.sum(before.astype(jnp.int32), axis=-1) & 1
    kind = far * 2 + lane
    ahead = before & (kind[..., None, :] == kind[..., :, None])
    prefix = jnp.sum(jnp.where(ahead, units[..., None, :], 0), axis=-1)
    kinds = jnp.arange(2 * chips, dtype=jnp.int32)
    total = jnp.sum(jnp.where(kind[..., None, :] == kinds[:, None], units[..., None, :], 0), axis=-1)
    total = total.reshape(2, groups, chips, chips, 2)
    lengths = [[total[:, :, o, f] for f in range(chips)] for o in range(chips)]
    branch, size, span = jnp.int32(len(PLANS)), jnp.int32(PLANS[-1][1]), jnp.int32(PLANS[-1][0] * PLANS[-1][1])
    for b, (rounds, width) in reversed(list(enumerate(PLANS))):
        fits = jnp.max(starts_of(lengths, chips, 2 * width)[1]) <= rounds * width
        branch, size, span = (jnp.where(fits, x, y) for x, y in ((b, branch), (width, size), (rounds * width, span)))

    def own_group(x):
        return lax.dynamic_index_in_dim(x, group, 1, keepdims=False)

    far, lane, prefix, units, total = (own_group(x) for x in (far, lane, prefix, units, total))
    lengths = [[total[:, o, f] for f in range(chips)] for o in range(chips)]
    starts = starts_of(lengths, chips, 2 * size)[0]
    none = jnp.zeros_like(lengths[0][0])
    runs = []
    most = max(c * (chips - 1 - c) for c in range(chips))
    for c in range(chips):
        own = [(starts[c, f, c], lengths[c][f], none) if f > c else (none, none, none) for f in range(1, chips)]
        passed = [(starts[o, f, c], lengths[o][f], starts[o, f, c - 1]) for o in range(c) for f in range(c + 1, chips)]
        passed += [(none, none, none)] * (most - len(passed))
        runs.append(jnp.stack([jnp.stack(r) for r in own + passed]))
    runs = jnp.stack(runs)
    outgo = jnp.stack([jnp.stack([starts[c, f, c] if f > c else none for f in range(chips)]) for c in range(chips)])
    income = jnp.stack(
        [
            jnp.stack([jnp.stack([starts[o, f, c - 1] if o < c <= f else none for f in range(chips)]) for o in range(chips)])
            for c in range(chips)
        ]
    )
    table, place, need, spot, side = [], [], [], [], []
    for d in range(2):
        at = chip if d == 0 else chips - 1 - chip
        table.append(lax.dynamic_index_in_dim(pick(runs, at)[..., d, :], core, 2, keepdims=False))
        home = pick(far[d], at)
        chosen = lax.dynamic_index_in_dim(pick(outgo, at)[:, d, :], core, 1, keepdims=False)
        first = jnp.sum(jnp.where(home[:, None] == line, chosen, 0), axis=1)
        place.append(first + pick(prefix[d], at))
        need.append(jnp.where((home > 0) & (pick(lane[d], at) == core), pick(units[d], at), 0))
        came = pick(income, at)[:, :, d, :]
        hit = (far[d][:, :, None, None] == line[:, None]) & (lane[d][:, :, None, None] == jnp.arange(2, dtype=jnp.int32))
        where = prefix[d] + jnp.sum(jnp.where(hit, came[:, None], 0), axis=(2, 3))
        spot.append(where if d == 0 else where[::-1])
        side.append(lane[d] if d == 0 else lane[d][::-1])
    stretch = span + 8
    origin = line[:, None]
    item = jnp.arange(items, dtype=jnp.int32)[None, :]
    width = mine[1]
    down = (origin > chip).astype(jnp.int32)
    lies = jnp.where(down == 1, spot[1], spot[0])
    on = jnp.where(down == 1, side[1], side[0])
    far_row = ((2 * down + (on != core)) * stretch + lies) * UNIT + (2 << ROW_BITS)
    near_row = (item % pairs) * width + ((item // pairs != core).astype(jnp.int32) << ROW_BITS)
    rows = jnp.where(origin == chip, near_row, far_row).reshape(-1)
    last = lies + units[0] - 1
    passed = sum((last >= r * size).astype(jnp.int32) for r in range(1, max(rounds for rounds, _ in PLANS)))
    ready = jnp.where(origin == chip, 0, passed + (on != core)).reshape(-1)
    found = mine[0][:, None] == ids
    location = jnp.sum(jnp.where(found, rows, 0), axis=1)
    when = jnp.sum(jnp.where(found, ready, 0), axis=1)
    return branch, jnp.stack(table), jnp.stack(place), jnp.stack(need), location, when


def ranks_of(owner):
    spots = jnp.arange(owner.shape[-1], dtype=jnp.int32)
    ahead = (owner[..., None, :] == owner[..., :, None]) & (spots[None, :] < spots[:, None])
    return jnp.sum(ahead.astype(jnp.int32), axis=-1)


def wanted_from(owner, pair, me, capacity):
    slot = jnp.where(owner == me, ranks_of(owner), capacity)
    hit = slot[:, None, :] == jnp.arange(capacity, dtype=jnp.int32)[:, None]
    return jnp.sum(jnp.where(hit, pair[:, None, :], 0), axis=-1)


def load_all(source, scratch, sem, parts=8):
    rows = source.shape[0] // parts
    return [
        pltpu.make_async_copy(source.at[pl.ds(i * rows, rows)], scratch.at[pl.ds(i * rows, rows)], sem) for i in range(parts)
    ]


def take_kernel(width, index_ref, blocks_ref, *refs):
    outs, (scratch, load, sem) = refs[:-3], refs[-3:]
    slots = outs[0].shape[0] // width
    loads = load_all(blocks_ref, scratch, load)
    for c in loads:
        c.start()
    for c in loads:
        c.wait()

    def copies(i):
        for k, out in enumerate(outs):
            row = pl.multiple_of(index_ref[k * slots + i] * width, UNIT)
            yield pltpu.make_async_copy(
                scratch.at[pl.ds(row, width)], out.at[pl.ds(pl.multiple_of(i * width, UNIT), width)], sem
            )

    @pl.loop(0, slots)
    def _(i):
        for c in copies(i):
            c.start()

    @pl.loop(0, slots)
    def _(i):
        for c in copies(i):
            c.wait()


def take(blocks, index, width, parts):
    slots = index.shape[0] // parts
    shape = jax.ShapeDtypeStruct((slots * width, blocks.shape[1]), blocks.dtype)
    return pl.pallas_call(
        functools.partial(take_kernel, width),
        in_specs=[SMEM, ANY],
        out_specs=[ANY] * parts,
        out_shape=[shape] * parts,
        scratch_shapes=[pltpu.VMEM(blocks.shape, blocks.dtype), pltpu.SemaphoreType.DMA, pltpu.SemaphoreType.DMA],
        compiler_params=params(),
        cost_estimate=pl.CostEstimate(flops=0, bytes_accessed=2 * parts * slots * width * blocks.shape[1] * 2, transcendentals=0),
    )(index, blocks)


def run_copies(runs_ref, d, r, window, size, source, base, out, sem, shift):
    first, length, back = runs_ref[d, r, 0], runs_ref[d, r, 1], runs_ref[d, r, 2]
    low = jnp.maximum(first, window * size)
    high = jnp.minimum(first + length, (window + 1) * size)
    taken = jnp.maximum(high - low, 0)
    begin = back + low - first if shift else low
    rows = taken * UNIT
    return taken, pltpu.make_async_copy(
        source.at[pl.ds(pl.multiple_of((base + jnp.maximum(begin, 0)) * UNIT, UNIT), rows)],
        out.at[pl.ds(pl.multiple_of((low - window * size) * UNIT, UNIT), rows)],
        sem,
    )


def windows(runs_ref, picks, window, size, source, bases, outs, sem, shift, act):
    for d in range(2):
        for r in picks:
            taken, copy = run_copies(runs_ref, d, r, window, size, source, bases[d], outs[d], sem, shift)

            @pl.when(taken > 0)
            def _():
                getattr(copy, act)()


def items_of(pairs, core_ref, sources, visit):
    for half, source in enumerate(sources):

        @pl.loop(0, pairs)
        def _(i):
            for d in range(2):
                visit(source, i, d, (core_ref[0] ^ half) * pairs + i)


def open_kernel(size, span, pairs, width, own, place_ref, need_ref, runs_ref, core_ref, mine_ref, other_ref, stream_ref, *refs):
    outs, (near, beside, load, sem) = refs[:-4], refs[-4:]
    loads = load_all(mine_ref, near, load) + load_all(other_ref, beside, load)
    for c in loads:
        c.start()
    for c in loads:
        c.wait()
    straight = (0, span)

    def visit(source, i, d, item):
        units = need_ref[d, item]

        @pl.when(units > 0)
        def _():
            pltpu.make_async_copy(
                source.at[pl.ds(pl.multiple_of(i * width, UNIT), units * UNIT)],
                stream_ref.at[pl.ds(pl.multiple_of((straight[d] + place_ref[d, item]) * UNIT, UNIT), units * UNIT)],
                sem,
            ).start()

    items_of(pairs, core_ref, (near, beside), visit)
    for d in range(2):
        total = sum(runs_ref[d, r, 1] for r in range(own)) * UNIT

        @pl.when(total > 0)
        def _():
            pltpu.make_async_copy(near.at[pl.ds(0, total)], stream_ref.at[pl.ds(0, total)], sem).wait()

    for act in ("start", "wait"):
        for window in range(2):
            part = [out.at[pl.ds(window * size * UNIT, size * UNIT)] for out in outs]
            windows(runs_ref, range(own), window, size, stream_ref, straight, part, sem, False, act)


def step_kernel(size, stretch, own, at, other_at, next_windows, runs_ref, stream_ref, *refs):
    refs = list(refs)
    if other_at is not None:
        refs.pop(0)
    came = [refs.pop(0), refs.pop(0)]
    other = [refs.pop(0), refs.pop(0)] if other_at is not None else []
    hold = refs.pop(0)
    arrive, rest, lay = refs[-3:]
    outs = refs[:-3]
    rows = size * UNIT

    def filed(piece, section, number, sem):
        return pltpu.make_async_copy(
            piece, hold.at[pl.ds(section * stretch * UNIT + number * rows, piece.shape[0])], sem
        )

    first = [filed(c, 2 * d, at, arrive.at[d]) for d, c in enumerate(came)]
    second = [filed(c, 2 * d + 1, other_at, rest.at[d]) for d, c in enumerate(other)]
    for c in first + second:
        c.start()
    straight, through = (0, stretch - 8), (0, 2 * stretch)

    def lay_out(passed, act):
        picks = range(own, runs_ref.shape[1]) if passed else range(own)
        for i, window in enumerate(next_windows):
            source, bases = (hold, through) if passed else (stream_ref, straight)
            windows(runs_ref, picks, window, size, source, bases, outs[2 * i : 2 * i + 2], lay, passed, act)

    lay_out(False, "start")
    for c in first:
        c.wait()
    lay_out(True, "start")
    lay_out(False, "wait")
    lay_out(True, "wait")
    for c in second:
        c.wait()


def close_kernel(size, stretch, number, came_up, came_down, held_ref, hold, sem):
    del held_ref
    rows = size * UNIT
    copies = [
        pltpu.make_async_copy(c, hold.at[pl.ds((2 * d + 1) * stretch * UNIT + number * rows, rows)], sem.at[d])
        for d, c in enumerate((came_up, came_down))
    ]
    for c in copies:
        c.start()
    for c in copies:
        c.wait()


def couple_kernel(width, depth, many, low, high, begun, threads, loc_ref, when_ref, count_ref, target_ref, coef_ref, metric_ref, *refs):
    refs = list(refs)
    tasks = loc_ref.shape[0] - 1
    acc_ref = refs.pop(0) if begun else None
    line, slots, sems = refs[-3:]
    out_ref = refs[-5] if threads else refs[-4]
    buffers = refs[: -5 if threads else -4]
    out_ref[...] = acc_ref[...] if begun else jnp.zeros_like(out_ref)

    def gather(t, found):
        line[found] = t
        return found + ((when_ref[t] > low) & (when_ref[t] <= high)).astype(jnp.int32)

    found = lax.fori_loop(0, tasks, gather, jnp.int32(0))
    for u in range(many):
        line[found + u] = tasks
    groups = lax.div(found + (many - 1), jnp.int32(many))

    def fetch(group, phase):
        for u in range(many):
            code = loc_ref[line[group * many + u]]
            row = pl.multiple_of(code & ((1 << ROW_BITS) - 1), UNIT)
            for b, source in enumerate(buffers):

                @pl.when((code >> ROW_BITS) == b)
                def _():
                    pltpu.make_async_copy(source.at[pl.ds(row, width)], slots.at[phase, u], sems.at[phase, u]).start()

    @pl.when(groups > 0)
    def _():
        fetch(0, 0)

    @pl.loop(0, groups)
    def _(group):
        phase = lax.rem(group, 2)

        @pl.when(group + 1 < groups)
        def _():
            fetch(group + 1, 1 - phase)

        for u in range(many):
            pltpu.make_async_copy(buffers[0].at[pl.ds(0, width)], slots.at[phase, u], sems.at[phase, u]).wait()
        crossed, amps = [], []
        for u in range(many):
            t = line[group * many + u]
            live = lax.broadcasted_iota(jnp.int32, (width, width), 0) < count_ref[t]
            turned = lax.dot_general(
                slots[phase, u, :, pl.ds(0, depth)],
                metric_ref[target_ref[t]],
                (((1,), (1,)), ((), ())),
                preferred_element_type=jnp.float32,
            )
            crossed.append(jnp.where(live, turned, 0.0).astype(jnp.bfloat16))
            amp = slots[phase, u, :, pl.ds(depth, width)]
            amps.append(jnp.where(live, amp, jnp.zeros_like(amp)))
        halves = [
            lax.dot_general(turned, amp, (((0,), (0,)), ((), ())), preferred_element_type=jnp.float32).astype(jnp.bfloat16)
            for turned, amp in zip(crossed, amps)
        ]
        terms = [
            coef_ref[line[group * many + u]] * jnp.dot(halves[u], crossed[u], preferred_element_type=jnp.float32)
            for u in range(many)
        ]
        for u in range(many):
            target = target_ref[line[group * many + u]]
            out_ref[target] = out_ref[target] - terms[u]


def couple(lists, metric, acc, buffers, low, high, threaded=None):
    tasks, (pairs, width, depth) = lists[0].shape[0] - 1, metric.shape
    many = MANY
    operands = list(lists) + [metric] + ([] if acc is None else [acc]) + buffers
    out_shape = [jax.ShapeDtypeStruct((pairs, width, width), jnp.float32)]
    out_specs, aliases = [IN_VMEM], {}
    if threaded is not None:
        at = len(operands) - len(buffers) + threaded
        aliases = {at: 1}
        out_shape.append(jax.ShapeDtypeStruct(operands[at].shape, operands[at].dtype))
        out_specs.append(ANY)
    return pl.pallas_call(
        functools.partial(couple_kernel, width, depth, many, low, high, acc is not None, threaded is not None),
        in_specs=[SMEM] * 5 + [IN_VMEM] * (1 if acc is None else 2) + [ANY] * len(buffers),
        out_specs=out_specs,
        out_shape=out_shape,
        input_output_aliases=aliases,
        scratch_shapes=[
            pltpu.SMEM((tasks + many,), jnp.int32),
            pltpu.VMEM((2, many, width, depth + width), jnp.bfloat16),
            pltpu.SemaphoreType.DMA((2, many)),
        ],
        compiler_params=params(),
        cost_estimate=pl.CostEstimate(flops=0, bytes_accessed=20_000_000, transcendentals=0),
    )(*operands)


def relay(rounds, size, chips, pairs, width, table, place, need, core, lists, mine, other, metric_of, cross_take, crossed):
    columns = mine.shape[1]
    stretch = rounds * size + 8
    parts = (2, 4, rounds - 3)
    own = chips - 1
    piece = jax.ShapeDtypeStruct((size * UNIT, columns), mine.dtype)
    double = jax.ShapeDtypeStruct((2 * size * UNIT, columns), mine.dtype)
    stream_shape = jax.ShapeDtypeStruct((2 * rounds * size * UNIT, columns), mine.dtype)
    hold_shape = jax.ShapeDtypeStruct((4 * stretch * UNIT, columns), mine.dtype)
    members = 2 * chips
    ways = [
        [(i, i + 2) for i in range(members - 2)],
        [(i + 2, i) for i in range(members - 2)],
    ]
    across = [(i, i ^ 1) for i in range(members)]
    stream, *opened = pl.pallas_call(
        functools.partial(open_kernel, size, rounds * size, pairs, width, own),
        in_specs=[SMEM] * 4 + [ANY] * 2,
        out_specs=[ANY] + [IN_VMEM] * 2,
        out_shape=[stream_shape] + [double] * 2,
        scratch_shapes=[pltpu.VMEM(mine.shape, mine.dtype)] * 2 + [pltpu.SemaphoreType.DMA] * 2,
        compiler_params=params(),
        cost_estimate=pl.CostEstimate(flops=0, bytes_accessed=6 * mine.size * 2, transcendentals=0),
    )(place, need, table, core, mine, other)
    sends = {1: opened}
    stream, after = lax.optimization_barrier((stream, mine))
    taken = cross_take(after)
    metric, crossing = metric_of(after), crossed(taken)
    hold, swapped, acc, done = None, None, None, -1
    for number in range(1, rounds):
        came = [lax.ppermute(sends[number][d], "mem", ways[d]) for d in range(2)]
        if number == 1:
            *came, _, metric = lax.optimization_barrier((*came, taken, metric))
        swapping = [lax.ppermute(came[d], "mem", across) for d in range(2)]
        if number == CROSS_AFTER:
            *came, crossing = lax.optimization_barrier((*came, crossing))
        begun = hold is not None
        ahead = [w for w in ((2, 3) if number == 1 else (number + 2,)) if w < rounds]
        operands = [table, stream] + ([hold] if begun else []) + came + (swapped if begun else [])
        hold, *going = pl.pallas_call(
            functools.partial(
                step_kernel,
                size,
                stretch,
                own,
                0 if number == 1 else number,
                None if not begun else (0 if number == 2 else number - 1),
                ahead,
            ),
            in_specs=[SMEM, ANY] + ([ANY] if begun else []) + [IN_VMEM] * (4 if begun else 2),
            out_specs=[ANY] + [IN_VMEM] * (2 * len(ahead)),
            out_shape=[hold_shape] + [piece] * (2 * len(ahead)),
            input_output_aliases={2: 0} if begun else {},
            scratch_shapes=[pltpu.SemaphoreType.DMA((2,)), pltpu.SemaphoreType.DMA((2,)), pltpu.SemaphoreType.DMA],
            compiler_params=params(),
            cost_estimate=pl.CostEstimate(flops=0, bytes_accessed=12 * size * UNIT * columns * 2, transcendentals=0),
        )(*operands)
        swapped = swapping
        if number in parts:
            buffers = [mine, other, hold] + ([crossing] if number >= CROSS_AFTER else [])
            acc, hold = couple(lists, metric, acc, buffers, done, number, 2)
            done = number
            if number == parts[-1]:
                *going, acc = lax.optimization_barrier((*going, acc))
        for i, window in enumerate(ahead):
            sends[window] = going[2 * i : 2 * i + 2]
    hold = pl.pallas_call(
        functools.partial(close_kernel, size, stretch, rounds - 1),
        in_specs=[IN_VMEM] * 2 + [ANY],
        out_specs=ANY,
        out_shape=hold_shape,
        input_output_aliases={2: 0},
        scratch_shapes=[pltpu.SemaphoreType.DMA((2,))],
        compiler_params=params(),
    )(*swapped, hold)
    [acc] = couple(lists, metric, acc, [mine, other, hold, crossing], done, rounds)
    return acc


def shards(
    pno,
    amplitudes,
    pno_count,
    pao_coupling,
    row_owner,
    row_pair,
    row_target,
    row_coef,
    column_owner,
    column_pair,
    column_target,
    column_coef,
):
    pairs, depth, width = pno.shape
    tasks, crossings = row_pair.shape[0], column_pair.shape[0]
    members, groups = lax.axis_size("mem"), lax.axis_size("grp")
    member, group = lax.axis_index("mem"), lax.axis_index("grp")
    row_cap = max(2, 2 * tasks // members)
    col_cap = max(2, 2 * crossings // groups)
    chips = members // 2
    row_owner, column_owner = row_owner[:, 0], column_owner[:, 0]
    row_code = row_owner * pairs + row_pair
    col_code = column_owner * pairs + column_pair
    tell = jnp.concatenate([row_code, col_code, pno_count])
    told = lax.all_to_all(
        jnp.broadcast_to(tell, (groups * members, tell.shape[0])), ("grp", "mem"), split_axis=0, concat_axis=0, tiled=True
    )
    told = told.reshape(groups, members, -1)
    code, cols, count = told[..., :tasks], told[..., tasks : tasks + crossings], told[..., tasks + crossings :]
    blocks = blocks_of(pno, amplitudes, pno_count)
    ids = jnp.arange(members * pairs, dtype=jnp.int32)
    here = pick(count, group).reshape(-1)
    row_count = jnp.sum(jnp.where(row_code[:, None] == ids, here, 0), axis=1)
    beside = lax.dynamic_index_in_dim(count, member, 1, keepdims=False).reshape(-1)
    col_ids = jnp.arange(groups * pairs, dtype=jnp.int32)
    col_count = jnp.sum(jnp.where(col_code[:, None] == col_ids, beside, 0), axis=1)
    ask = lax.dynamic_index_in_dim(cols, member, 1, keepdims=False)
    asked = wanted_from(ask // pairs, ask % pairs, group, col_cap)
    col_row = (column_owner * col_cap + ranks_of(column_owner)) * width

    def metric_of(blocks):
        return metric_blocks(blocks, pao_coupling).reshape(pairs, width, depth)

    def cross_take(blocks):
        return take(blocks, asked.reshape(-1), width, 1)[0]

    def crossed(sent):
        return lax.all_to_all(sent, "grp", split_axis=0, concat_axis=0, tiled=True)

    def lists_of(location, when, first):
        col_location = col_row + (first << ROW_BITS)
        none = jnp.zeros((1,), jnp.int32)
        return (
            jnp.concatenate([location, col_location, none]),
            jnp.concatenate([when, jnp.full_like(col_location, CROSS_AFTER), none]),
            jnp.concatenate([row_count, col_count, none]),
            jnp.concatenate([row_target, column_target, none]),
            jnp.concatenate([row_coef, column_coef, none.astype(jnp.float32)]),
        )

    def plain(*_):
        want = wanted_from(pick(code, group) // pairs, pick(code, group) % pairs, member, row_cap)
        [sent] = take(blocks, want.reshape(-1), width, 1)
        got = lax.all_to_all(sent, "mem", split_axis=0, concat_axis=0, tiled=True)
        location = (row_owner * row_cap + ranks_of(row_owner)) * width + (1 << ROW_BITS)
        lists = lists_of(location, jnp.zeros_like(location), 2)
        [acc] = couple(lists, metric_of(blocks), None, [blocks, got, crossed(cross_take(blocks))], -1, CROSS_AFTER)
        return acc

    if members % 2 or chips < 2 or chips > 4:
        return plain()
    other = lax.ppermute(blocks, "mem", [(i, i ^ 1) for i in range(members)])
    branch, table, place, need, location, when = relay_plan(code, count, group, member, (row_code, width))
    core = (member % 2).reshape(1).astype(jnp.int32)

    lists = lists_of(location, when, 3)

    def relayed(rounds, size):
        return relay(rounds, size, chips, pairs, width, table, place, need, core, lists, blocks, other, metric_of, cross_take, crossed)

    return lax.switch(branch, [functools.partial(relayed, *p) for p in PLANS] + [plain])


def solution(mesh):
    in_specs = (
        P(("grp", "mem"), None, None),
        P(("grp", "mem"), None, None),
        P(("grp", "mem")),
        P(),
        P(("grp", "mem"), None),
        P(("grp", "mem")),
        P(("grp", "mem")),
        P(("grp", "mem")),
        P(("grp", "mem"), None),
        P(("grp", "mem")),
        P(("grp", "mem")),
        P(("grp", "mem")),
    )
    out_specs = P(("grp", "mem"), None, None)
    return jax.shard_map(shards, mesh=mesh, in_specs=in_specs, out_specs=out_specs, check_vma=False)
```

```python
import functools

import jax
import jax.numpy as jnp
from jax import lax
from jax.experimental import pallas as pl
from jax.experimental.pallas import tpu as pltpu
from jax.sharding import PartitionSpec as P

UNIT = 16
PLANS = ((8, 35), (8, 37), (9, 35), (9, 37))
VMEM = 48 * 2**20
CROSS_AFTER = 5
ROW_BITS = 20
MANY = 8
ANY = pl.BlockSpec(memory_space=pl.ANY)
SMEM = pl.BlockSpec(memory_space=pltpu.SMEM)
IN_VMEM = pl.BlockSpec(memory_space=pltpu.VMEM)


def params():
    return pltpu.CompilerParams(vmem_limit_bytes=VMEM)


def block_kernel(count_ref, pno_ref, amp_ref, out_ref):
    step = pl.program_id(0)
    many, depth, width = pno_ref.shape
    for i in range(many):
        count = count_ref[step * many + i]
        rows = lax.broadcasted_iota(jnp.int32, (width, depth), 0)
        turned = pno_ref[i].T
        out_ref[pl.ds(i * width, width), pl.ds(0, depth)] = jnp.where(rows < count, turned, jnp.zeros_like(turned))
        down = lax.broadcasted_iota(jnp.int32, (width, width), 0)
        across = lax.broadcasted_iota(jnp.int32, (width, width), 1)
        amp = amp_ref[i]
        live = (down < count) & (across < count)
        out_ref[pl.ds(i * width, width), pl.ds(depth, width)] = jnp.where(live, amp, jnp.zeros_like(amp))


def blocks_of(pno, amplitudes, pno_count):
    pairs, depth, width = pno.shape
    many = 4
    return pl.pallas_call(
        block_kernel,
        grid=(pairs // many,),
        in_specs=[
            SMEM,
            pl.BlockSpec((many, depth, width), lambda i: (i, 0, 0)),
            pl.BlockSpec((many, width, width), lambda i: (i, 0, 0)),
        ],
        out_specs=pl.BlockSpec((many * width, depth + width), lambda i: (i, 0)),
        out_shape=jax.ShapeDtypeStruct((pairs * width, depth + width), pno.dtype),
        compiler_params=pltpu.CompilerParams(vmem_limit_bytes=60 * 2**20),
    )(pno_count, pno, amplitudes)


def metric_kernel(depth, block_ref, coupling_ref, out_ref):
    live = block_ref[:, pl.ds(0, depth)]
    mixed = jnp.dot(live, coupling_ref[...], preferred_element_type=jnp.float32)
    out_ref[...] = (live.astype(jnp.float32) + mixed).astype(out_ref.dtype)


def metric_blocks(blocks, pao_coupling):
    rows, columns = blocks.shape
    depth = pao_coupling.shape[0]
    tile = 512
    return pl.pallas_call(
        functools.partial(metric_kernel, depth),
        grid=(rows // tile,),
        in_specs=[pl.BlockSpec((tile, columns), lambda i: (i, 0)), pl.BlockSpec((depth, depth), lambda i: (0, 0))],
        out_specs=pl.BlockSpec((tile, depth), lambda i: (i, 0)),
        out_shape=jax.ShapeDtypeStruct((rows, depth), blocks.dtype),
        compiler_params=params(),
        cost_estimate=pl.CostEstimate(flops=0, bytes_accessed=20_000_000, transcendentals=0),
    )(blocks, pao_coupling)


def pick(array, index):
    return lax.dynamic_index_in_dim(array, index, 0, keepdims=False)


def starts_of(lengths, chips, delay):
    starts, ends = {}, []
    for c in range(chips - 1):
        at = jnp.zeros_like(lengths[0][chips - 1])
        for f in range(chips - 1, c, -1):
            for o in range(c, -1, -1):
                if o < c:
                    at = jnp.where(lengths[o][f] > 0, jnp.maximum(at, starts[o, f, c - 1] + delay), at)
                starts[o, f, c] = at
                at = at + lengths[o][f]
        ends.append(at)
    return starts, functools.reduce(jnp.maximum, ends)


def relay_plan(code, count, group, member, mine):
    groups, members, _ = code.shape
    pairs = count.shape[2]
    chips, items = members // 2, 2 * pairs
    chip, core = member // 2, member % 2
    ids = jnp.arange(members * pairs, dtype=jnp.int32)
    asked = jnp.any(code[..., None, :] == ids[:, None], axis=-1)
    asked = jnp.any(asked.reshape(groups, chips, 2, chips, items), axis=2)
    asked = jnp.stack([asked, asked[:, ::-1, ::-1]])
    line = jnp.arange(chips, dtype=jnp.int32)
    later = (line[:, None] > line[None, :])[:, :, None]
    far = jnp.max(jnp.where(asked & later, line[:, None, None], 0), axis=2)
    units = ((count + UNIT - 1) // UNIT).reshape(groups, chips, items)
    units = jnp.stack([units, units[:, ::-1]])
    order = far * items + (items - 1 - jnp.arange(items, dtype=jnp.int32))
    before = (order[..., None, :] > order[..., :, None]) & (far[..., None, :] > 0)
    lane = jnp.sum(before.astype(jnp.int32), axis=-1) & 1
    kind = far * 2 + lane
    ahead = before & (kind[..., None, :] == kind[..., :, None])
    prefix = jnp.sum(jnp.where(ahead, units[..., None, :], 0), axis=-1)
    kinds = jnp.arange(2 * chips, dtype=jnp.int32)
    total = jnp.sum(jnp.where(kind[..., None, :] == kinds[:, None], units[..., None, :], 0), axis=-1)
    total = total.reshape(2, groups, chips, chips, 2)
    lengths = [[total[:, :, o, f] for f in range(chips)] for o in range(chips)]
    branch, size, span = jnp.int32(len(PLANS)), jnp.int32(PLANS[-1][1]), jnp.int32(PLANS[-1][0] * PLANS[-1][1])
    for b, (rounds, width) in reversed(list(enumerate(PLANS))):
        fits = jnp.max(starts_of(lengths, chips, 2 * width)[1]) <= rounds * width
        branch, size, span = (jnp.where(fits, x, y) for x, y in ((b, branch), (width, size), (rounds * width, span)))

    def own_group(x):
        return lax.dynamic_index_in_dim(x, group, 1, keepdims=False)

    far, lane, prefix, units, total = (own_group(x) for x in (far, lane, prefix, units, total))
    lengths = [[total[:, o, f] for f in range(chips)] for o in range(chips)]
    starts = starts_of(lengths, chips, 2 * size)[0]
    none = jnp.zeros_like(lengths[0][0])
    runs = []
    most = max(c * (chips - 1 - c) for c in range(chips))
    for c in range(chips):
        own = [(starts[c, f, c], lengths[c][f], none) if f > c else (none, none, none) for f in range(1, chips)]
        passed = [(starts[o, f, c], lengths[o][f], starts[o, f, c - 1]) for o in range(c) for f in range(c + 1, chips)]
        passed += [(none, none, none)] * (most - len(passed))
        runs.append(jnp.stack([jnp.stack(r) for r in own + passed]))
    runs = jnp.stack(runs)
    outgo = jnp.stack([jnp.stack([starts[c, f, c] if f > c else none for f in range(chips)]) for c in range(chips)])
    income = jnp.stack(
        [
            jnp.stack([jnp.stack([starts[o, f, c - 1] if o < c <= f else none for f in range(chips)]) for o in range(chips)])
            for c in range(chips)
        ]
    )
    table, place, need, spot, side = [], [], [], [], []
    for d in range(2):
        at = chip if d == 0 else chips - 1 - chip
        table.append(lax.dynamic_index_in_dim(pick(runs, at)[..., d, :], core, 2, keepdims=False))
        home = pick(far[d], at)
        chosen = lax.dynamic_index_in_dim(pick(outgo, at)[:, d, :], core, 1, keepdims=False)
        first = jnp.sum(jnp.where(home[:, None] == line, chosen, 0), axis=1)
        place.append(first + pick(prefix[d], at))
        need.append(jnp.where((home > 0) & (pick(lane[d], at) == core), pick(units[d], at), 0))
        came = pick(income, at)[:, :, d, :]
        hit = (far[d][:, :, None, None] == line[:, None]) & (lane[d][:, :, None, None] == jnp.arange(2, dtype=jnp.int32))
        where = prefix[d] + jnp.sum(jnp.where(hit, came[:, None], 0), axis=(2, 3))
        spot.append(where if d == 0 else where[::-1])
        side.append(lane[d] if d == 0 else lane[d][::-1])
    stretch = span + 8
    origin = line[:, None]
    item = jnp.arange(items, dtype=jnp.int32)[None, :]
    width = mine[1]
    down = (origin > chip).astype(jnp.int32)
    lies = jnp.where(down == 1, spot[1], spot[0])
    on = jnp.where(down == 1, side[1], side[0])
    far_row = ((2 * down + (on != core)) * stretch + lies) * UNIT + (2 << ROW_BITS)
    near_row = (item % pairs) * width + ((item // pairs != core).astype(jnp.int32) << ROW_BITS)
    rows = jnp.where(origin == chip, near_row, far_row).reshape(-1)
    last = lies + units[0] - 1
    passed = sum((last >= r * size).astype(jnp.int32) for r in range(1, max(rounds for rounds, _ in PLANS)))
    ready = jnp.where(origin == chip, 0, passed + (on != core)).reshape(-1)
    found = mine[0][:, None] == ids
    location = jnp.sum(jnp.where(found, rows, 0), axis=1)
    when = jnp.sum(jnp.where(found, ready, 0), axis=1)
    return branch, jnp.stack(table), jnp.stack(place), jnp.stack(need), location, when


def ranks_of(owner):
    spots = jnp.arange(owner.shape[-1], dtype=jnp.int32)
    ahead = (owner[..., None, :] == owner[..., :, None]) & (spots[None, :] < spots[:, None])
    return jnp.sum(ahead.astype(jnp.int32), axis=-1)


def wanted_from(owner, pair, me, capacity):
    slot = jnp.where(owner == me, ranks_of(owner), capacity)
    hit = slot[:, None, :] == jnp.arange(capacity, dtype=jnp.int32)[:, None]
    return jnp.sum(jnp.where(hit, pair[:, None, :], 0), axis=-1)


def load_all(source, scratch, sem, parts=8):
    rows = source.shape[0] // parts
    return [
        pltpu.make_async_copy(source.at[pl.ds(i * rows, rows)], scratch.at[pl.ds(i * rows, rows)], sem) for i in range(parts)
    ]


def take_kernel(width, index_ref, blocks_ref, *refs):
    outs, (scratch, load, sem) = refs[:-3], refs[-3:]
    slots = outs[0].shape[0] // width
    loads = load_all(blocks_ref, scratch, load)
    for c in loads:
        c.start()
    for c in loads:
        c.wait()

    def copies(i):
        for k, out in enumerate(outs):
            row = pl.multiple_of(index_ref[k * slots + i] * width, UNIT)
            yield pltpu.make_async_copy(
                scratch.at[pl.ds(row, width)], out.at[pl.ds(pl.multiple_of(i * width, UNIT), width)], sem
            )

    @pl.loop(0, slots)
    def _(i):
        for c in copies(i):
            c.start()

    @pl.loop(0, slots)
    def _(i):
        for c in copies(i):
            c.wait()


def take(blocks, index, width, parts):
    slots = index.shape[0] // parts
    shape = jax.ShapeDtypeStruct((slots * width, blocks.shape[1]), blocks.dtype)
    return pl.pallas_call(
        functools.partial(take_kernel, width),
        in_specs=[SMEM, ANY],
        out_specs=[ANY] * parts,
        out_shape=[shape] * parts,
        scratch_shapes=[pltpu.VMEM(blocks.shape, blocks.dtype), pltpu.SemaphoreType.DMA, pltpu.SemaphoreType.DMA],
        compiler_params=params(),
        cost_estimate=pl.CostEstimate(flops=0, bytes_accessed=2 * parts * slots * width * blocks.shape[1] * 2, transcendentals=0),
    )(index, blocks)


def run_copies(runs_ref, d, r, window, size, source, base, out, sem, shift):
    first, length, back = runs_ref[d, r, 0], runs_ref[d, r, 1], runs_ref[d, r, 2]
    low = jnp.maximum(first, window * size)
    high = jnp.minimum(first + length, (window + 1) * size)
    taken = jnp.maximum(high - low, 0)
    begin = back + low - first if shift else low
    rows = taken * UNIT
    return taken, pltpu.make_async_copy(
        source.at[pl.ds(pl.multiple_of((base + jnp.maximum(begin, 0)) * UNIT, UNIT), rows)],
        out.at[pl.ds(pl.multiple_of((low - window * size) * UNIT, UNIT), rows)],
        sem,
    )


def windows(runs_ref, picks, window, size, source, bases, outs, sem, shift, act):
    for d in range(2):
        for r in picks:
            taken, copy = run_copies(runs_ref, d, r, window, size, source, bases[d], outs[d], sem, shift)

            @pl.when(taken > 0)
            def _():
                getattr(copy, act)()


def items_of(pairs, core_ref, sources, visit):
    for half, source in enumerate(sources):

        @pl.loop(0, pairs)
        def _(i):
            for d in range(2):
                visit(source, i, d, (core_ref[0] ^ half) * pairs + i)


def open_kernel(size, span, pairs, width, own, place_ref, need_ref, runs_ref, core_ref, mine_ref, other_ref, stream_ref, *refs):
    outs, (near, beside, load, sem) = refs[:-4], refs[-4:]
    loads = load_all(mine_ref, near, load) + load_all(other_ref, beside, load)
    for c in loads:
        c.start()
    for c in loads:
        c.wait()
    straight = (0, span)

    def visit(source, i, d, item):
        units = need_ref[d, item]

        @pl.when(units > 0)
        def _():
            pltpu.make_async_copy(
                source.at[pl.ds(pl.multiple_of(i * width, UNIT), units * UNIT)],
                stream_ref.at[pl.ds(pl.multiple_of((straight[d] + place_ref[d, item]) * UNIT, UNIT), units * UNIT)],
                sem,
            ).start()

    items_of(pairs, core_ref, (near, beside), visit)
    for d in range(2):
        total = sum(runs_ref[d, r, 1] for r in range(own)) * UNIT

        @pl.when(total > 0)
        def _():
            pltpu.make_async_copy(near.at[pl.ds(0, total)], stream_ref.at[pl.ds(0, total)], sem).wait()

    for act in ("start", "wait"):
        for window in range(2):
            part = [out.at[pl.ds(window * size * UNIT, size * UNIT)] for out in outs]
            windows(runs_ref, range(own), window, size, stream_ref, straight, part, sem, False, act)


def step_kernel(size, stretch, own, at, other_at, next_windows, runs_ref, stream_ref, *refs):
    refs = list(refs)
    if other_at is not None:
        refs.pop(0)
    came = [refs.pop(0), refs.pop(0)]
    other = [refs.pop(0), refs.pop(0)] if other_at is not None else []
    hold = refs.pop(0)
    arrive, rest, lay = refs[-3:]
    outs = refs[:-3]
    rows = size * UNIT

    def filed(piece, section, number, sem):
        return pltpu.make_async_copy(
            piece, hold.at[pl.ds(section * stretch * UNIT + number * rows, piece.shape[0])], sem
        )

    first = [filed(c, 2 * d, at, arrive.at[d]) for d, c in enumerate(came)]
    second = [filed(c, 2 * d + 1, other_at, rest.at[d]) for d, c in enumerate(other)]
    for c in first + second:
        c.start()
    straight, through = (0, stretch - 8), (0, 2 * stretch)

    def lay_out(passed, act):
        picks = range(own, runs_ref.shape[1]) if passed else range(own)
        for i, window in enumerate(next_windows):
            source, bases = (hold, through) if passed else (stream_ref, straight)
            windows(runs_ref, picks, window, size, source, bases, outs[2 * i : 2 * i + 2], lay, passed, act)

    lay_out(False, "start")
    for c in first:
        c.wait()
    lay_out(True, "start")
    lay_out(False, "wait")
    lay_out(True, "wait")
    for c in second:
        c.wait()


def close_kernel(size, stretch, number, came_up, came_down, held_ref, hold, sem):
    del held_ref
    rows = size * UNIT
    copies = [
        pltpu.make_async_copy(c, hold.at[pl.ds((2 * d + 1) * stretch * UNIT + number * rows, rows)], sem.at[d])
        for d, c in enumerate((came_up, came_down))
    ]
    for c in copies:
        c.start()
    for c in copies:
        c.wait()


def couple_kernel(width, depth, many, low, high, begun, threads, loc_ref, when_ref, count_ref, target_ref, coef_ref, metric_ref, *refs):
    refs = list(refs)
    tasks = loc_ref.shape[0] - 1
    acc_ref = refs.pop(0) if begun else None
    line, slots, sems = refs[-3:]
    out_ref = refs[-5] if threads else refs[-4]
    buffers = refs[: -5 if threads else -4]
    out_ref[...] = acc_ref[...] if begun else jnp.zeros_like(out_ref)

    def gather(t, found):
        line[found] = t
        return found + ((when_ref[t] > low) & (when_ref[t] <= high)).astype(jnp.int32)

    found = lax.fori_loop(0, tasks, gather, jnp.int32(0))
    for u in range(many):
        line[found + u] = tasks
    groups = lax.div(found + (many - 1), jnp.int32(many))

    def fetch(group, phase):
        for u in range(many):
            code = loc_ref[line[group * many + u]]
            row = pl.multiple_of(code & ((1 << ROW_BITS) - 1), UNIT)
            for b, source in enumerate(buffers):

                @pl.when((code >> ROW_BITS) == b)
                def _():
                    pltpu.make_async_copy(source.at[pl.ds(row, width)], slots.at[phase, u], sems.at[phase, u]).start()

    @pl.when(groups > 0)
    def _():
        fetch(0, 0)

    @pl.loop(0, groups)
    def _(group):
        phase = lax.rem(group, 2)

        @pl.when(group + 1 < groups)
        def _():
            fetch(group + 1, 1 - phase)

        for u in range(many):
            pltpu.make_async_copy(buffers[0].at[pl.ds(0, width)], slots.at[phase, u], sems.at[phase, u]).wait()
        crossed, amps = [], []
        for u in range(many):
            t = line[group * many + u]
            live = lax.broadcasted_iota(jnp.int32, (width, width), 0) < count_ref[t]
            turned = lax.dot_general(
                slots[phase, u, :, pl.ds(0, depth)],
                metric_ref[target_ref[t]],
                (((1,), (1,)), ((), ())),
                preferred_element_type=jnp.float32,
            )
            crossed.append(jnp.where(live, turned, 0.0).astype(jnp.bfloat16))
            amp = slots[phase, u, :, pl.ds(depth, width)]
            amps.append(jnp.where(live, amp, jnp.zeros_like(amp)))
        halves = [
            lax.dot_general(turned, amp, (((0,), (0,)), ((), ())), preferred_element_type=jnp.float32).astype(jnp.bfloat16)
            for turned, amp in zip(crossed, amps)
        ]
        terms = [
            coef_ref[line[group * many + u]] * jnp.dot(halves[u], crossed[u], preferred_element_type=jnp.float32)
            for u in range(many)
        ]
        for u in range(many):
            target = target_ref[line[group * many + u]]
            out_ref[target] = out_ref[target] - terms[u]


def couple(lists, metric, acc, buffers, low, high, threaded=None):
    tasks, (pairs, width, depth) = lists[0].shape[0] - 1, metric.shape
    many = MANY
    operands = list(lists) + [metric] + ([] if acc is None else [acc]) + buffers
    out_shape = [jax.ShapeDtypeStruct((pairs, width, width), jnp.float32)]
    out_specs, aliases = [IN_VMEM], {}
    if threaded is not None:
        at = len(operands) - len(buffers) + threaded
        aliases = {at: 1}
        out_shape.append(jax.ShapeDtypeStruct(operands[at].shape, operands[at].dtype))
        out_specs.append(ANY)
    return pl.pallas_call(
        functools.partial(couple_kernel, width, depth, many, low, high, acc is not None, threaded is not None),
        in_specs=[SMEM] * 5 + [IN_VMEM] * (1 if acc is None else 2) + [ANY] * len(buffers),
        out_specs=out_specs,
        out_shape=out_shape,
        input_output_aliases=aliases,
        scratch_shapes=[
            pltpu.SMEM((tasks + many,), jnp.int32),
            pltpu.VMEM((2, many, width, depth + width), jnp.bfloat16),
            pltpu.SemaphoreType.DMA((2, many)),
        ],
        compiler_params=params(),
        cost_estimate=pl.CostEstimate(flops=0, bytes_accessed=20_000_000, transcendentals=0),
    )(*operands)


def relay(rounds, size, chips, pairs, width, table, place, need, core, lists, mine, other, metric_of, cross_take, crossed):
    columns = mine.shape[1]
    stretch = rounds * size + 8
    parts = (2, 4, rounds - 3, rounds - 2)
    own = chips - 1
    piece = jax.ShapeDtypeStruct((size * UNIT, columns), mine.dtype)
    double = jax.ShapeDtypeStruct((2 * size * UNIT, columns), mine.dtype)
    stream_shape = jax.ShapeDtypeStruct((2 * rounds * size * UNIT, columns), mine.dtype)
    hold_shape = jax.ShapeDtypeStruct((4 * stretch * UNIT, columns), mine.dtype)
    members = 2 * chips
    ways = [
        [(i, i + 2) for i in range(members - 2)],
        [(i + 2, i) for i in range(members - 2)],
    ]
    across = [(i, i ^ 1) for i in range(members)]
    stream, *opened = pl.pallas_call(
        functools.partial(open_kernel, size, rounds * size, pairs, width, own),
        in_specs=[SMEM] * 4 + [ANY] * 2,
        out_specs=[ANY] + [IN_VMEM] * 2,
        out_shape=[stream_shape] + [double] * 2,
        scratch_shapes=[pltpu.VMEM(mine.shape, mine.dtype)] * 2 + [pltpu.SemaphoreType.DMA] * 2,
        compiler_params=params(),
        cost_estimate=pl.CostEstimate(flops=0, bytes_accessed=6 * mine.size * 2, transcendentals=0),
    )(place, need, table, core, mine, other)
    sends = {1: opened}
    stream, after = lax.optimization_barrier((stream, mine))
    taken = cross_take(after)
    metric, crossing = metric_of(after), crossed(taken)
    hold, swapped, acc, done = None, None, None, -1
    for number in range(1, rounds):
        came = [lax.ppermute(sends[number][d], "mem", ways[d]) for d in range(2)]
        if number == 1:
            *came, _, metric = lax.optimization_barrier((*came, taken, metric))
        else:
            *came, hold = lax.optimization_barrier((*came, hold))
        swapping = [lax.ppermute(came[d], "mem", across) for d in range(2)]
        if number == rounds - 3:
            *came, crossing = lax.optimization_barrier((*came, crossing))
        begun = hold is not None
        ahead = [w for w in ((2, 3) if number == 1 else (number + 2,)) if w < rounds]
        operands = [table, stream] + ([hold] if begun else []) + came + (swapped if begun else [])
        hold, *going = pl.pallas_call(
            functools.partial(
                step_kernel,
                size,
                stretch,
                own,
                0 if number == 1 else number,
                None if not begun else (0 if number == 2 else number - 1),
                ahead,
            ),
            in_specs=[SMEM, ANY] + ([ANY] if begun else []) + [IN_VMEM] * (4 if begun else 2),
            out_specs=[ANY] + [IN_VMEM] * (2 * len(ahead)),
            out_shape=[hold_shape] + [piece] * (2 * len(ahead)),
            input_output_aliases={2: 0} if begun else {},
            scratch_shapes=[pltpu.SemaphoreType.DMA((2,)), pltpu.SemaphoreType.DMA((2,)), pltpu.SemaphoreType.DMA],
            compiler_params=params(),
            cost_estimate=pl.CostEstimate(flops=0, bytes_accessed=12 * size * UNIT * columns * 2, transcendentals=0),
        )(*operands)
        swapped = swapping
        if number in parts:
            buffers = [mine, other, hold] + ([crossing] if number >= rounds - 3 else [])
            acc, hold = couple(lists, metric, acc, buffers, done, number, 2)
            done = number
        for i, window in enumerate(ahead):
            sends[window] = going[2 * i : 2 * i + 2]
    hold = pl.pallas_call(
        functools.partial(close_kernel, size, stretch, rounds - 1),
        in_specs=[IN_VMEM] * 2 + [ANY],
        out_specs=ANY,
        out_shape=hold_shape,
        input_output_aliases={2: 0},
        scratch_shapes=[pltpu.SemaphoreType.DMA((2,))],
        compiler_params=params(),
    )(*swapped, hold)
    [acc] = couple(lists, metric, acc, [mine, other, hold, crossing], done, rounds)
    return acc


def shards(
    pno,
    amplitudes,
    pno_count,
    pao_coupling,
    row_owner,
    row_pair,
    row_target,
    row_coef,
    column_owner,
    column_pair,
    column_target,
    column_coef,
):
    pairs, depth, width = pno.shape
    tasks, crossings = row_pair.shape[0], column_pair.shape[0]
    members, groups = lax.axis_size("mem"), lax.axis_size("grp")
    member, group = lax.axis_index("mem"), lax.axis_index("grp")
    row_cap = max(2, 2 * tasks // members)
    col_cap = max(2, 2 * crossings // groups)
    chips = members // 2
    row_owner, column_owner = row_owner[:, 0], column_owner[:, 0]
    row_code = row_owner * pairs + row_pair
    col_code = column_owner * pairs + column_pair
    tell = jnp.concatenate([row_code, col_code, pno_count])
    told = lax.all_to_all(
        jnp.broadcast_to(tell, (groups * members, tell.shape[0])), ("grp", "mem"), split_axis=0, concat_axis=0, tiled=True
    )
    told = told.reshape(groups, members, -1)
    code, cols, count = told[..., :tasks], told[..., tasks : tasks + crossings], told[..., tasks + crossings :]
    blocks = blocks_of(pno, amplitudes, pno_count)
    ids = jnp.arange(members * pairs, dtype=jnp.int32)
    here = pick(count, group).reshape(-1)
    row_count = jnp.sum(jnp.where(row_code[:, None] == ids, here, 0), axis=1)
    beside = lax.dynamic_index_in_dim(count, member, 1, keepdims=False).reshape(-1)
    col_ids = jnp.arange(groups * pairs, dtype=jnp.int32)
    col_count = jnp.sum(jnp.where(col_code[:, None] == col_ids, beside, 0), axis=1)
    ask = lax.dynamic_index_in_dim(cols, member, 1, keepdims=False)
    asked = wanted_from(ask // pairs, ask % pairs, group, col_cap)
    col_row = (column_owner * col_cap + ranks_of(column_owner)) * width

    def metric_of(blocks):
        return metric_blocks(blocks, pao_coupling).reshape(pairs, width, depth)

    def cross_take(blocks):
        return take(blocks, asked.reshape(-1), width, 1)[0]

    def crossed(sent):
        return lax.all_to_all(sent, "grp", split_axis=0, concat_axis=0, tiled=True)

    def lists_of(location, when, first):
        col_location = col_row + (first << ROW_BITS)
        none = jnp.zeros((1,), jnp.int32)
        return (
            jnp.concatenate([location, col_location, none]),
            jnp.concatenate([when, jnp.full_like(col_location, CROSS_AFTER), none]),
            jnp.concatenate([row_count, col_count, none]),
            jnp.concatenate([row_target, column_target, none]),
            jnp.concatenate([row_coef, column_coef, none.astype(jnp.float32)]),
        )

    def plain(*_):
        want = wanted_from(pick(code, group) // pairs, pick(code, group) % pairs, member, row_cap)
        [sent] = take(blocks, want.reshape(-1), width, 1)
        got = lax.all_to_all(sent, "mem", split_axis=0, concat_axis=0, tiled=True)
        location = (row_owner * row_cap + ranks_of(row_owner)) * width + (1 << ROW_BITS)
        lists = lists_of(location, jnp.zeros_like(location), 2)
        [acc] = couple(lists, metric_of(blocks), None, [blocks, got, crossed(cross_take(blocks))], -1, CROSS_AFTER)
        return acc

    if members % 2 or chips < 2 or chips > 4:
        return plain()
    other = lax.ppermute(blocks, "mem", [(i, i ^ 1) for i in range(members)])
    branch, table, place, need, location, when = relay_plan(code, count, group, member, (row_code, width))
    core = (member % 2).reshape(1).astype(jnp.int32)

    lists = lists_of(location, when, 3)

    def relayed(rounds, size):
        return relay(rounds, size, chips, pairs, width, table, place, need, core, lists, blocks, other, metric_of, cross_take, crossed)

    return lax.switch(branch, [functools.partial(relayed, *p) for p in PLANS] + [plain])


def solution(mesh):
    in_specs = (
        P(("grp", "mem"), None, None),
        P(("grp", "mem"), None, None),
        P(("grp", "mem")),
        P(),
        P(("grp", "mem"), None),
        P(("grp", "mem")),
        P(("grp", "mem")),
        P(("grp", "mem")),
        P(("grp", "mem"), None),
        P(("grp", "mem")),
        P(("grp", "mem")),
        P(("grp", "mem")),
    )
    out_specs = P(("grp", "mem"), None, None)
    return jax.shard_map(shards, mesh=mesh, in_specs=in_specs, out_specs=out_specs, check_vma=False)
```

```python
import functools

import jax
import jax.numpy as jnp
from jax import lax
from jax.experimental import pallas as pl
from jax.experimental.pallas import tpu as pltpu
from jax.sharding import PartitionSpec as P

UNIT = 16
PLANS = ((8, 35), (8, 37), (9, 35), (9, 37))
VMEM = 48 * 2**20
CROSS_AFTER = 5
ROW_BITS = 20
MANY = 8
ANY = pl.BlockSpec(memory_space=pl.ANY)
SMEM = pl.BlockSpec(memory_space=pltpu.SMEM)
IN_VMEM = pl.BlockSpec(memory_space=pltpu.VMEM)


def params():
    return pltpu.CompilerParams(vmem_limit_bytes=VMEM)


def block_kernel(count_ref, pno_ref, amp_ref, out_ref):
    step = pl.program_id(0)
    many, depth, width = pno_ref.shape
    for i in range(many):
        count = count_ref[step * many + i]
        rows = lax.broadcasted_iota(jnp.int32, (width, depth), 0)
        turned = pno_ref[i].T
        out_ref[pl.ds(i * width, width), pl.ds(0, depth)] = jnp.where(rows < count, turned, jnp.zeros_like(turned))
        down = lax.broadcasted_iota(jnp.int32, (width, width), 0)
        across = lax.broadcasted_iota(jnp.int32, (width, width), 1)
        amp = amp_ref[i]
        live = (down < count) & (across < count)
        out_ref[pl.ds(i * width, width), pl.ds(depth, width)] = jnp.where(live, amp, jnp.zeros_like(amp))


def blocks_of(pno, amplitudes, pno_count):
    pairs, depth, width = pno.shape
    many = 4
    return pl.pallas_call(
        block_kernel,
        grid=(pairs // many,),
        in_specs=[
            SMEM,
            pl.BlockSpec((many, depth, width), lambda i: (i, 0, 0)),
            pl.BlockSpec((many, width, width), lambda i: (i, 0, 0)),
        ],
        out_specs=pl.BlockSpec((many * width, depth + width), lambda i: (i, 0)),
        out_shape=jax.ShapeDtypeStruct((pairs * width, depth + width), pno.dtype),
        compiler_params=pltpu.CompilerParams(vmem_limit_bytes=60 * 2**20),
    )(pno_count, pno, amplitudes)


def metric_kernel(depth, block_ref, coupling_ref, out_ref):
    live = block_ref[:, pl.ds(0, depth)]
    mixed = jnp.dot(live, coupling_ref[...], preferred_element_type=jnp.float32)
    out_ref[...] = (live.astype(jnp.float32) + mixed).astype(out_ref.dtype)


def metric_blocks(blocks, pao_coupling):
    rows, columns = blocks.shape
    depth = pao_coupling.shape[0]
    tile = 512
    return pl.pallas_call(
        functools.partial(metric_kernel, depth),
        grid=(rows // tile,),
        in_specs=[pl.BlockSpec((tile, columns), lambda i: (i, 0)), pl.BlockSpec((depth, depth), lambda i: (0, 0))],
        out_specs=pl.BlockSpec((tile, depth), lambda i: (i, 0)),
        out_shape=jax.ShapeDtypeStruct((rows, depth), blocks.dtype),
        compiler_params=params(),
        cost_estimate=pl.CostEstimate(flops=0, bytes_accessed=20_000_000, transcendentals=0),
    )(blocks, pao_coupling)


def pick(array, index):
    return lax.dynamic_index_in_dim(array, index, 0, keepdims=False)


def starts_of(lengths, chips, delay):
    starts, ends = {}, []
    for c in range(chips - 1):
        at = jnp.zeros_like(lengths[0][chips - 1])
        for f in range(chips - 1, c, -1):
            for o in range(c, -1, -1):
                if o < c:
                    at = jnp.where(lengths[o][f] > 0, jnp.maximum(at, starts[o, f, c - 1] + delay), at)
                starts[o, f, c] = at
                at = at + lengths[o][f]
        ends.append(at)
    return starts, functools.reduce(jnp.maximum, ends)


def relay_plan(code, count, group, member, mine):
    groups, members, _ = code.shape
    pairs = count.shape[2]
    chips, items = members // 2, 2 * pairs
    chip, core = member // 2, member % 2
    ids = jnp.arange(members * pairs, dtype=jnp.int32)
    asked = jnp.any(code[..., None, :] == ids[:, None], axis=-1)
    asked = jnp.any(asked.reshape(groups, chips, 2, chips, items), axis=2)
    asked = jnp.stack([asked, asked[:, ::-1, ::-1]])
    line = jnp.arange(chips, dtype=jnp.int32)
    later = (line[:, None] > line[None, :])[:, :, None]
    far = jnp.max(jnp.where(asked & later, line[:, None, None], 0), axis=2)
    units = ((count + UNIT - 1) // UNIT).reshape(groups, chips, items)
    units = jnp.stack([units, units[:, ::-1]])
    order = far * items + (items - 1 - jnp.arange(items, dtype=jnp.int32))
    before = (order[..., None, :] > order[..., :, None]) & (far[..., None, :] > 0)
    lane = jnp.sum(before.astype(jnp.int32), axis=-1) & 1
    kind = far * 2 + lane
    ahead = before & (kind[..., None, :] == kind[..., :, None])
    prefix = jnp.sum(jnp.where(ahead, units[..., None, :], 0), axis=-1)
    kinds = jnp.arange(2 * chips, dtype=jnp.int32)
    total = jnp.sum(jnp.where(kind[..., None, :] == kinds[:, None], units[..., None, :], 0), axis=-1)
    total = total.reshape(2, groups, chips, chips, 2)
    lengths = [[total[:, :, o, f] for f in range(chips)] for o in range(chips)]
    branch, size, span = jnp.int32(len(PLANS)), jnp.int32(PLANS[-1][1]), jnp.int32(PLANS[-1][0] * PLANS[-1][1])
    for b, (rounds, width) in reversed(list(enumerate(PLANS))):
        fits = jnp.max(starts_of(lengths, chips, 2 * width)[1]) <= rounds * width
        branch, size, span = (jnp.where(fits, x, y) for x, y in ((b, branch), (width, size), (rounds * width, span)))

    def own_group(x):
        return lax.dynamic_index_in_dim(x, group, 1, keepdims=False)

    far, lane, prefix, units, total = (own_group(x) for x in (far, lane, prefix, units, total))
    lengths = [[total[:, o, f] for f in range(chips)] for o in range(chips)]
    starts = starts_of(lengths, chips, 2 * size)[0]
    none = jnp.zeros_like(lengths[0][0])
    runs = []
    most = max(c * (chips - 1 - c) for c in range(chips))
    for c in range(chips):
        own = [(starts[c, f, c], lengths[c][f], none) if f > c else (none, none, none) for f in range(1, chips)]
        passed = [(starts[o, f, c], lengths[o][f], starts[o, f, c - 1]) for o in range(c) for f in range(c + 1, chips)]
        passed += [(none, none, none)] * (most - len(passed))
        runs.append(jnp.stack([jnp.stack(r) for r in own + passed]))
    runs = jnp.stack(runs)
    outgo = jnp.stack([jnp.stack([starts[c, f, c] if f > c else none for f in range(chips)]) for c in range(chips)])
    income = jnp.stack(
        [
            jnp.stack([jnp.stack([starts[o, f, c - 1] if o < c <= f else none for f in range(chips)]) for o in range(chips)])
            for c in range(chips)
        ]
    )
    table, place, need, spot, side = [], [], [], [], []
    for d in range(2):
        at = chip if d == 0 else chips - 1 - chip
        table.append(lax.dynamic_index_in_dim(pick(runs, at)[..., d, :], core, 2, keepdims=False))
        home = pick(far[d], at)
        chosen = lax.dynamic_index_in_dim(pick(outgo, at)[:, d, :], core, 1, keepdims=False)
        first = jnp.sum(jnp.where(home[:, None] == line, chosen, 0), axis=1)
        place.append(first + pick(prefix[d], at))
        need.append(jnp.where((home > 0) & (pick(lane[d], at) == core), pick(units[d], at), 0))
        came = pick(income, at)[:, :, d, :]
        hit = (far[d][:, :, None, None] == line[:, None]) & (lane[d][:, :, None, None] == jnp.arange(2, dtype=jnp.int32))
        where = prefix[d] + jnp.sum(jnp.where(hit, came[:, None], 0), axis=(2, 3))
        spot.append(where if d == 0 else where[::-1])
        side.append(lane[d] if d == 0 else lane[d][::-1])
    stretch = span + 8
    origin = line[:, None]
    item = jnp.arange(items, dtype=jnp.int32)[None, :]
    width = mine[1]
    down = (origin > chip).astype(jnp.int32)
    lies = jnp.where(down == 1, spot[1], spot[0])
    on = jnp.where(down == 1, side[1], side[0])
    far_row = ((2 * down + (on != core)) * stretch + lies) * UNIT + (2 << ROW_BITS)
    near_row = (item % pairs) * width + ((item // pairs != core).astype(jnp.int32) << ROW_BITS)
    rows = jnp.where(origin == chip, near_row, far_row).reshape(-1)
    last = lies + units[0] - 1
    passed = sum((last >= r * size).astype(jnp.int32) for r in range(1, max(rounds for rounds, _ in PLANS)))
    ready = jnp.where(origin == chip, 0, passed).reshape(-1)
    found = mine[0][:, None] == ids
    location = jnp.sum(jnp.where(found, rows, 0), axis=1)
    when = jnp.sum(jnp.where(found, ready, 0), axis=1)
    return branch, jnp.stack(table), jnp.stack(place), jnp.stack(need), location, when


def ranks_of(owner):
    spots = jnp.arange(owner.shape[-1], dtype=jnp.int32)
    ahead = (owner[..., None, :] == owner[..., :, None]) & (spots[None, :] < spots[:, None])
    return jnp.sum(ahead.astype(jnp.int32), axis=-1)


def wanted_from(owner, pair, me, capacity):
    slot = jnp.where(owner == me, ranks_of(owner), capacity)
    hit = slot[:, None, :] == jnp.arange(capacity, dtype=jnp.int32)[:, None]
    return jnp.sum(jnp.where(hit, pair[:, None, :], 0), axis=-1)


def load_all(source, scratch, sem, parts=8):
    rows = source.shape[0] // parts
    return [
        pltpu.make_async_copy(source.at[pl.ds(i * rows, rows)], scratch.at[pl.ds(i * rows, rows)], sem) for i in range(parts)
    ]


def take_kernel(width, index_ref, blocks_ref, *refs):
    outs, (scratch, load, sem) = refs[:-3], refs[-3:]
    slots = outs[0].shape[0] // width
    loads = load_all(blocks_ref, scratch, load)
    for c in loads:
        c.start()
    for c in loads:
        c.wait()

    def copies(i):
        for k, out in enumerate(outs):
            row = pl.multiple_of(index_ref[k * slots + i] * width, UNIT)
            yield pltpu.make_async_copy(
                scratch.at[pl.ds(row, width)], out.at[pl.ds(pl.multiple_of(i * width, UNIT), width)], sem
            )

    @pl.loop(0, slots)
    def _(i):
        for c in copies(i):
            c.start()

    @pl.loop(0, slots)
    def _(i):
        for c in copies(i):
            c.wait()


def take(blocks, index, width, parts):
    slots = index.shape[0] // parts
    shape = jax.ShapeDtypeStruct((slots * width, blocks.shape[1]), blocks.dtype)
    return pl.pallas_call(
        functools.partial(take_kernel, width),
        in_specs=[SMEM, ANY],
        out_specs=[ANY] * parts,
        out_shape=[shape] * parts,
        scratch_shapes=[pltpu.VMEM(blocks.shape, blocks.dtype), pltpu.SemaphoreType.DMA, pltpu.SemaphoreType.DMA],
        compiler_params=params(),
        cost_estimate=pl.CostEstimate(flops=0, bytes_accessed=2 * parts * slots * width * blocks.shape[1] * 2, transcendentals=0),
    )(index, blocks)


def run_copies(runs_ref, d, r, window, size, source, base, out, sem, shift):
    first, length, back = runs_ref[d, r, 0], runs_ref[d, r, 1], runs_ref[d, r, 2]
    low = jnp.maximum(first, window * size)
    high = jnp.minimum(first + length, (window + 1) * size)
    taken = jnp.maximum(high - low, 0)
    begin = back + low - first if shift else low
    rows = taken * UNIT
    return taken, pltpu.make_async_copy(
        source.at[pl.ds(pl.multiple_of((base + jnp.maximum(begin, 0)) * UNIT, UNIT), rows)],
        out.at[pl.ds(pl.multiple_of((low - window * size) * UNIT, UNIT), rows)],
        sem,
    )


def windows(runs_ref, picks, window, size, source, bases, outs, sem, shift, act):
    for d in range(2):
        for r in picks:
            taken, copy = run_copies(runs_ref, d, r, window, size, source, bases[d], outs[d], sem, shift)

            @pl.when(taken > 0)
            def _():
                getattr(copy, act)()


def items_of(pairs, core_ref, sources, visit):
    for half, source in enumerate(sources):

        @pl.loop(0, pairs)
        def _(i):
            for d in range(2):
                visit(source, i, d, (core_ref[0] ^ half) * pairs + i)


def open_kernel(size, span, pairs, width, own, place_ref, need_ref, runs_ref, core_ref, mine_ref, other_ref, stream_ref, *refs):
    outs, (near, beside, load, sem) = refs[:-4], refs[-4:]
    loads = load_all(mine_ref, near, load) + load_all(other_ref, beside, load)
    for c in loads:
        c.start()
    for c in loads:
        c.wait()
    straight = (0, span)

    def visit(source, i, d, item):
        units = need_ref[d, item]

        @pl.when(units > 0)
        def _():
            pltpu.make_async_copy(
                source.at[pl.ds(pl.multiple_of(i * width, UNIT), units * UNIT)],
                stream_ref.at[pl.ds(pl.multiple_of((straight[d] + place_ref[d, item]) * UNIT, UNIT), units * UNIT)],
                sem,
            ).start()

    items_of(pairs, core_ref, (near, beside), visit)
    for d in range(2):
        total = sum(runs_ref[d, r, 1] for r in range(own)) * UNIT

        @pl.when(total > 0)
        def _():
            pltpu.make_async_copy(near.at[pl.ds(0, total)], stream_ref.at[pl.ds(0, total)], sem).wait()

    for act in ("start", "wait"):
        for window in range(2):
            part = [out.at[pl.ds(window * size * UNIT, size * UNIT)] for out in outs]
            windows(runs_ref, range(own), window, size, stream_ref, straight, part, sem, False, act)


def step_kernel(size, stretch, own, begun, at, next_windows, runs_ref, stream_ref, *refs):
    refs = list(refs)
    if begun:
        refs.pop(0)
    came = [refs.pop(0), refs.pop(0)]
    other = [refs.pop(0), refs.pop(0)]
    hold = refs.pop(0)
    arrive, rest, lay = refs[-3:]
    outs = refs[:-3]
    rows = size * UNIT

    def filed(piece, section, sem):
        return pltpu.make_async_copy(
            piece, hold.at[pl.ds(section * stretch * UNIT + at * rows, piece.shape[0])], sem
        )

    first = [filed(c, 2 * d, arrive.at[d]) for d, c in enumerate(came)]
    second = [filed(c, 2 * d + 1, rest.at[d]) for d, c in enumerate(other)]
    for c in first + second:
        c.start()
    straight, through = (0, stretch - 8), (0, 2 * stretch)

    def lay_out(passed, act):
        picks = range(own, runs_ref.shape[1]) if passed else range(own)
        for i, window in enumerate(next_windows):
            source, bases = (hold, through) if passed else (stream_ref, straight)
            windows(runs_ref, picks, window, size, source, bases, outs[2 * i : 2 * i + 2], lay, passed, act)

    lay_out(False, "start")
    for c in first:
        c.wait()
    lay_out(True, "start")
    lay_out(False, "wait")
    lay_out(True, "wait")
    for c in second:
        c.wait()


def couple_kernel(width, depth, many, low, high, begun, threads, loc_ref, when_ref, count_ref, target_ref, coef_ref, metric_ref, *refs):
    refs = list(refs)
    tasks = loc_ref.shape[0] - 1
    acc_ref = refs.pop(0) if begun else None
    line, slots, sems = refs[-3:]
    out_ref = refs[-5] if threads else refs[-4]
    buffers = refs[: -5 if threads else -4]
    out_ref[...] = acc_ref[...] if begun else jnp.zeros_like(out_ref)

    def gather(t, found):
        line[found] = t
        return found + ((when_ref[t] > low) & (when_ref[t] <= high)).astype(jnp.int32)

    found = lax.fori_loop(0, tasks, gather, jnp.int32(0))
    for u in range(many):
        line[found + u] = tasks
    groups = lax.div(found + (many - 1), jnp.int32(many))

    def fetch(group, phase):
        for u in range(many):
            code = loc_ref[line[group * many + u]]
            row = pl.multiple_of(code & ((1 << ROW_BITS) - 1), UNIT)
            for b, source in enumerate(buffers):

                @pl.when((code >> ROW_BITS) == b)
                def _():
                    pltpu.make_async_copy(source.at[pl.ds(row, width)], slots.at[phase, u], sems.at[phase, u]).start()

    @pl.when(groups > 0)
    def _():
        fetch(0, 0)

    @pl.loop(0, groups)
    def _(group):
        phase = lax.rem(group, 2)

        @pl.when(group + 1 < groups)
        def _():
            fetch(group + 1, 1 - phase)

        for u in range(many):
            pltpu.make_async_copy(buffers[0].at[pl.ds(0, width)], slots.at[phase, u], sems.at[phase, u]).wait()
        crossed, amps = [], []
        for u in range(many):
            t = line[group * many + u]
            live = lax.broadcasted_iota(jnp.int32, (width, width), 0) < count_ref[t]
            turned = lax.dot_general(
                slots[phase, u, :, pl.ds(0, depth)],
                metric_ref[target_ref[t]],
                (((1,), (1,)), ((), ())),
                preferred_element_type=jnp.float32,
            )
            crossed.append(jnp.where(live, turned, 0.0).astype(jnp.bfloat16))
            amp = slots[phase, u, :, pl.ds(depth, width)]
            amps.append(jnp.where(live, amp, jnp.zeros_like(amp)))
        halves = [
            lax.dot_general(turned, amp, (((0,), (0,)), ((), ())), preferred_element_type=jnp.float32).astype(jnp.bfloat16)
            for turned, amp in zip(crossed, amps)
        ]
        terms = [
            coef_ref[line[group * many + u]] * jnp.dot(halves[u], crossed[u], preferred_element_type=jnp.float32)
            for u in range(many)
        ]
        for u in range(many):
            target = target_ref[line[group * many + u]]
            out_ref[target] = out_ref[target] - terms[u]


def couple(lists, metric, acc, buffers, low, high, threaded=None):
    tasks, (pairs, width, depth) = lists[0].shape[0] - 1, metric.shape
    many = MANY
    operands = list(lists) + [metric] + ([] if acc is None else [acc]) + buffers
    out_shape = [jax.ShapeDtypeStruct((pairs, width, width), jnp.float32)]
    out_specs, aliases = [IN_VMEM], {}
    if threaded is not None:
        at = len(operands) - len(buffers) + threaded
        aliases = {at: 1}
        out_shape.append(jax.ShapeDtypeStruct(operands[at].shape, operands[at].dtype))
        out_specs.append(ANY)
    return pl.pallas_call(
        functools.partial(couple_kernel, width, depth, many, low, high, acc is not None, threaded is not None),
        in_specs=[SMEM] * 5 + [IN_VMEM] * (1 if acc is None else 2) + [ANY] * len(buffers),
        out_specs=out_specs,
        out_shape=out_shape,
        input_output_aliases=aliases,
        scratch_shapes=[
            pltpu.SMEM((tasks + many,), jnp.int32),
            pltpu.VMEM((2, many, width, depth + width), jnp.bfloat16),
            pltpu.SemaphoreType.DMA((2, many)),
        ],
        compiler_params=params(),
        cost_estimate=pl.CostEstimate(flops=0, bytes_accessed=20_000_000, transcendentals=0),
    )(*operands)


def relay(rounds, size, chips, pairs, width, table, place, need, core, lists, mine, other, metric_of, cross_take, crossed):
    columns = mine.shape[1]
    stretch = rounds * size + 8
    parts = (2, 4, rounds - 3, rounds - 2)
    own = chips - 1
    piece = jax.ShapeDtypeStruct((size * UNIT, columns), mine.dtype)
    double = jax.ShapeDtypeStruct((2 * size * UNIT, columns), mine.dtype)
    stream_shape = jax.ShapeDtypeStruct((2 * rounds * size * UNIT, columns), mine.dtype)
    hold_shape = jax.ShapeDtypeStruct((4 * stretch * UNIT, columns), mine.dtype)
    members = 2 * chips
    ways = [
        [(i, i + 2) for i in range(members - 2)],
        [(i + 2, i) for i in range(members - 2)],
    ]
    across = [(i, i ^ 1) for i in range(members)]
    stream, *opened = pl.pallas_call(
        functools.partial(open_kernel, size, rounds * size, pairs, width, own),
        in_specs=[SMEM] * 4 + [ANY] * 2,
        out_specs=[ANY] + [IN_VMEM] * 2,
        out_shape=[stream_shape] + [double] * 2,
        scratch_shapes=[pltpu.VMEM(mine.shape, mine.dtype)] * 2 + [pltpu.SemaphoreType.DMA] * 2,
        compiler_params=params(),
        cost_estimate=pl.CostEstimate(flops=0, bytes_accessed=6 * mine.size * 2, transcendentals=0),
    )(place, need, table, core, mine, other)
    sends = {1: opened}
    stream, after = lax.optimization_barrier((stream, mine))
    taken = cross_take(after)
    metric, crossing = metric_of(after), crossed(taken)
    hold, acc, done = None, None, -1
    for number in range(1, rounds):
        came = [lax.ppermute(sends[number][d], "mem", ways[d]) for d in range(2)]
        if number == 1:
            *came, _, metric = lax.optimization_barrier((*came, taken, metric))
        else:
            *came, hold = lax.optimization_barrier((*came, hold))
        swapping = [lax.ppermute(came[d], "mem", across) for d in range(2)]
        if number == CROSS_AFTER - 1:
            *came, crossing = lax.optimization_barrier((*came, crossing))
        begun = hold is not None
        ahead = [w for w in ((2, 3) if number == 1 else (number + 2,)) if w < rounds]
        operands = [table, stream] + ([hold] if begun else []) + came + swapping
        hold, *going = pl.pallas_call(
            functools.partial(
                step_kernel,
                size,
                stretch,
                own,
                begun,
                0 if number == 1 else number,
                ahead,
            ),
            in_specs=[SMEM, ANY] + ([ANY] if begun else []) + [IN_VMEM] * 4,
            out_specs=[ANY] + [IN_VMEM] * (2 * len(ahead)),
            out_shape=[hold_shape] + [piece] * (2 * len(ahead)),
            input_output_aliases={2: 0} if begun else {},
            scratch_shapes=[pltpu.SemaphoreType.DMA((2,)), pltpu.SemaphoreType.DMA((2,)), pltpu.SemaphoreType.DMA],
            compiler_params=params(),
            cost_estimate=pl.CostEstimate(flops=0, bytes_accessed=12 * size * UNIT * columns * 2, transcendentals=0),
        )(*operands)
        if number in parts:
            buffers = [mine, other, hold] + ([crossing] if number >= rounds - 3 else [])
            acc, hold = couple(lists, metric, acc, buffers, done, number, 2)
            done = number
        for i, window in enumerate(ahead):
            sends[window] = going[2 * i : 2 * i + 2]
    [acc] = couple(lists, metric, acc, [mine, other, hold, crossing], done, rounds)
    return acc


def shards(
    pno,
    amplitudes,
    pno_count,
    pao_coupling,
    row_owner,
    row_pair,
    row_target,
    row_coef,
    column_owner,
    column_pair,
    column_target,
    column_coef,
):
    pairs, depth, width = pno.shape
    tasks, crossings = row_pair.shape[0], column_pair.shape[0]
    members, groups = lax.axis_size("mem"), lax.axis_size("grp")
    member, group = lax.axis_index("mem"), lax.axis_index("grp")
    row_cap = max(2, 2 * tasks // members)
    col_cap = max(2, 2 * crossings // groups)
    chips = members // 2
    row_owner, column_owner = row_owner[:, 0], column_owner[:, 0]
    row_code = row_owner * pairs + row_pair
    col_code = column_owner * pairs + column_pair
    tell = jnp.concatenate([row_code, col_code, pno_count])
    told = lax.all_to_all(
        jnp.broadcast_to(tell, (groups * members, tell.shape[0])), ("grp", "mem"), split_axis=0, concat_axis=0, tiled=True
    )
    told = told.reshape(groups, members, -1)
    code, cols, count = told[..., :tasks], told[..., tasks : tasks + crossings], told[..., tasks + crossings :]
    blocks = blocks_of(pno, amplitudes, pno_count)
    ids = jnp.arange(members * pairs, dtype=jnp.int32)
    here = pick(count, group).reshape(-1)
    row_count = jnp.sum(jnp.where(row_code[:, None] == ids, here, 0), axis=1)
    beside = lax.dynamic_index_in_dim(count, member, 1, keepdims=False).reshape(-1)
    col_ids = jnp.arange(groups * pairs, dtype=jnp.int32)
    col_count = jnp.sum(jnp.where(col_code[:, None] == col_ids, beside, 0), axis=1)
    ask = lax.dynamic_index_in_dim(cols, member, 1, keepdims=False)
    asked = wanted_from(ask // pairs, ask % pairs, group, col_cap)
    col_row = (column_owner * col_cap + ranks_of(column_owner)) * width

    def metric_of(blocks):
        return metric_blocks(blocks, pao_coupling).reshape(pairs, width, depth)

    def cross_take(blocks):
        return take(blocks, asked.reshape(-1), width, 1)[0]

    def crossed(sent):
        return lax.all_to_all(sent, "grp", split_axis=0, concat_axis=0, tiled=True)

    def lists_of(location, when, first):
        col_location = col_row + (first << ROW_BITS)
        none = jnp.zeros((1,), jnp.int32)
        return (
            jnp.concatenate([location, col_location, none]),
            jnp.concatenate([when, jnp.full_like(col_location, CROSS_AFTER), none]),
            jnp.concatenate([row_count, col_count, none]),
            jnp.concatenate([row_target, column_target, none]),
            jnp.concatenate([row_coef, column_coef, none.astype(jnp.float32)]),
        )

    def plain(*_):
        want = wanted_from(pick(code, group) // pairs, pick(code, group) % pairs, member, row_cap)
        [sent] = take(blocks, want.reshape(-1), width, 1)
        got = lax.all_to_all(sent, "mem", split_axis=0, concat_axis=0, tiled=True)
        location = (row_owner * row_cap + ranks_of(row_owner)) * width + (1 << ROW_BITS)
        lists = lists_of(location, jnp.zeros_like(location), 2)
        [acc] = couple(lists, metric_of(blocks), None, [blocks, got, crossed(cross_take(blocks))], -1, CROSS_AFTER)
        return acc

    if members % 2 or chips < 2 or chips > 4:
        return plain()
    other = lax.ppermute(blocks, "mem", [(i, i ^ 1) for i in range(members)])
    branch, table, place, need, location, when = relay_plan(code, count, group, member, (row_code, width))
    core = (member % 2).reshape(1).astype(jnp.int32)

    lists = lists_of(location, when, 3)

    def relayed(rounds, size):
        return relay(rounds, size, chips, pairs, width, table, place, need, core, lists, blocks, other, metric_of, cross_take, crossed)

    return lax.switch(branch, [functools.partial(relayed, *p) for p in PLANS] + [plain])


def solution(mesh):
    in_specs = (
        P(("grp", "mem"), None, None),
        P(("grp", "mem"), None, None),
        P(("grp", "mem")),
        P(),
        P(("grp", "mem"), None),
        P(("grp", "mem")),
        P(("grp", "mem")),
        P(("grp", "mem")),
        P(("grp", "mem"), None),
        P(("grp", "mem")),
        P(("grp", "mem")),
        P(("grp", "mem")),
    )
    out_specs = P(("grp", "mem"), None, None)
    return jax.shard_map(shards, mesh=mesh, in_specs=in_specs, out_specs=out_specs, check_vma=False)
```

```python
import functools

import jax
import jax.numpy as jnp
from jax import lax
from jax.experimental import pallas as pl
from jax.experimental.pallas import tpu as pltpu
from jax.sharding import PartitionSpec as P

UNIT = 16
PLANS = ((8, 35), (8, 37), (9, 35), (9, 37))
VMEM = 48 * 2**20
CROSS_AFTER = 5
ROW_BITS = 20
MANY = 8
ANY = pl.BlockSpec(memory_space=pl.ANY)
SMEM = pl.BlockSpec(memory_space=pltpu.SMEM)
IN_VMEM = pl.BlockSpec(memory_space=pltpu.VMEM)


def params():
    return pltpu.CompilerParams(vmem_limit_bytes=VMEM)


def block_kernel(count_ref, pno_ref, amp_ref, out_ref):
    step = pl.program_id(0)
    many, depth, width = pno_ref.shape
    for i in range(many):
        count = count_ref[step * many + i]
        rows = lax.broadcasted_iota(jnp.int32, (width, depth), 0)
        turned = pno_ref[i].T
        out_ref[pl.ds(i * width, width), pl.ds(0, depth)] = jnp.where(rows < count, turned, jnp.zeros_like(turned))
        down = lax.broadcasted_iota(jnp.int32, (width, width), 0)
        across = lax.broadcasted_iota(jnp.int32, (width, width), 1)
        amp = amp_ref[i]
        live = (down < count) & (across < count)
        out_ref[pl.ds(i * width, width), pl.ds(depth, width)] = jnp.where(live, amp, jnp.zeros_like(amp))


def blocks_of(pno, amplitudes, pno_count):
    pairs, depth, width = pno.shape
    many = 4
    return pl.pallas_call(
        block_kernel,
        grid=(pairs // many,),
        in_specs=[
            SMEM,
            pl.BlockSpec((many, depth, width), lambda i: (i, 0, 0)),
            pl.BlockSpec((many, width, width), lambda i: (i, 0, 0)),
        ],
        out_specs=pl.BlockSpec((many * width, depth + width), lambda i: (i, 0)),
        out_shape=jax.ShapeDtypeStruct((pairs * width, depth + width), pno.dtype),
        compiler_params=pltpu.CompilerParams(vmem_limit_bytes=60 * 2**20),
    )(pno_count, pno, amplitudes)


def metric_kernel(depth, block_ref, coupling_ref, out_ref):
    live = block_ref[:, pl.ds(0, depth)]
    mixed = jnp.dot(live, coupling_ref[...], preferred_element_type=jnp.float32)
    out_ref[...] = (live.astype(jnp.float32) + mixed).astype(out_ref.dtype)


def metric_blocks(blocks, pao_coupling):
    rows, columns = blocks.shape
    depth = pao_coupling.shape[0]
    tile = 512
    return pl.pallas_call(
        functools.partial(metric_kernel, depth),
        grid=(rows // tile,),
        in_specs=[pl.BlockSpec((tile, columns), lambda i: (i, 0)), pl.BlockSpec((depth, depth), lambda i: (0, 0))],
        out_specs=pl.BlockSpec((tile, depth), lambda i: (i, 0)),
        out_shape=jax.ShapeDtypeStruct((rows, depth), blocks.dtype),
        compiler_params=params(),
        cost_estimate=pl.CostEstimate(flops=0, bytes_accessed=20_000_000, transcendentals=0),
    )(blocks, pao_coupling)


def pick(array, index):
    return lax.dynamic_index_in_dim(array, index, 0, keepdims=False)


def starts_of(lengths, chips, delay):
    starts, ends = {}, []
    for c in range(chips - 1):
        at = jnp.zeros_like(lengths[0][chips - 1])
        for f in range(chips - 1, c, -1):
            for o in range(c, -1, -1):
                if o < c:
                    at = jnp.where(lengths[o][f] > 0, jnp.maximum(at, starts[o, f, c - 1] + delay), at)
                starts[o, f, c] = at
                at = at + lengths[o][f]
        ends.append(at)
    return starts, functools.reduce(jnp.maximum, ends)


def relay_plan(code, count, group, member, mine):
    groups, members, _ = code.shape
    pairs = count.shape[2]
    chips, items = members // 2, 2 * pairs
    chip, core = member // 2, member % 2
    ids = jnp.arange(members * pairs, dtype=jnp.int32)
    asked = jnp.any(code[..., None, :] == ids[:, None], axis=-1)
    asked = jnp.any(asked.reshape(groups, chips, 2, chips, items), axis=2)
    asked = jnp.stack([asked, asked[:, ::-1, ::-1]])
    line = jnp.arange(chips, dtype=jnp.int32)
    later = (line[:, None] > line[None, :])[:, :, None]
    far = jnp.max(jnp.where(asked & later, line[:, None, None], 0), axis=2)
    units = ((count + UNIT - 1) // UNIT).reshape(groups, chips, items)
    units = jnp.stack([units, units[:, ::-1]])
    order = far * items + (items - 1 - jnp.arange(items, dtype=jnp.int32))
    before = (order[..., None, :] > order[..., :, None]) & (far[..., None, :] > 0)
    lane = jnp.sum(before.astype(jnp.int32), axis=-1) & 1
    kind = far * 2 + lane
    ahead = before & (kind[..., None, :] == kind[..., :, None])
    prefix = jnp.sum(jnp.where(ahead, units[..., None, :], 0), axis=-1)
    kinds = jnp.arange(2 * chips, dtype=jnp.int32)
    total = jnp.sum(jnp.where(kind[..., None, :] == kinds[:, None], units[..., None, :], 0), axis=-1)
    total = total.reshape(2, groups, chips, chips, 2)
    lengths = [[total[:, :, o, f] for f in range(chips)] for o in range(chips)]
    branch, size, span = jnp.int32(len(PLANS)), jnp.int32(PLANS[-1][1]), jnp.int32(PLANS[-1][0] * PLANS[-1][1])
    for b, (rounds, width) in reversed(list(enumerate(PLANS))):
        fits = jnp.max(starts_of(lengths, chips, 2 * width)[1]) <= rounds * width
        branch, size, span = (jnp.where(fits, x, y) for x, y in ((b, branch), (width, size), (rounds * width, span)))

    def own_group(x):
        return lax.dynamic_index_in_dim(x, group, 1, keepdims=False)

    far, lane, prefix, units, total = (own_group(x) for x in (far, lane, prefix, units, total))
    lengths = [[total[:, o, f] for f in range(chips)] for o in range(chips)]
    starts = starts_of(lengths, chips, 2 * size)[0]
    none = jnp.zeros_like(lengths[0][0])
    runs = []
    most = max(c * (chips - 1 - c) for c in range(chips))
    for c in range(chips):
        own = [(starts[c, f, c], lengths[c][f], none) if f > c else (none, none, none) for f in range(1, chips)]
        passed = [(starts[o, f, c], lengths[o][f], starts[o, f, c - 1]) for o in range(c) for f in range(c + 1, chips)]
        passed += [(none, none, none)] * (most - len(passed))
        runs.append(jnp.stack([jnp.stack(r) for r in own + passed]))
    runs = jnp.stack(runs)
    outgo = jnp.stack([jnp.stack([starts[c, f, c] if f > c else none for f in range(chips)]) for c in range(chips)])
    income = jnp.stack(
        [
            jnp.stack([jnp.stack([starts[o, f, c - 1] if o < c <= f else none for f in range(chips)]) for o in range(chips)])
            for c in range(chips)
        ]
    )
    table, place, need, spot, side = [], [], [], [], []
    for d in range(2):
        at = chip if d == 0 else chips - 1 - chip
        table.append(lax.dynamic_index_in_dim(pick(runs, at)[..., d, :], core, 2, keepdims=False))
        home = pick(far[d], at)
        chosen = lax.dynamic_index_in_dim(pick(outgo, at)[:, d, :], core, 1, keepdims=False)
        first = jnp.sum(jnp.where(home[:, None] == line, chosen, 0), axis=1)
        place.append(first + pick(prefix[d], at))
        need.append(jnp.where((home > 0) & (pick(lane[d], at) == core), pick(units[d], at), 0))
        came = pick(income, at)[:, :, d, :]
        hit = (far[d][:, :, None, None] == line[:, None]) & (lane[d][:, :, None, None] == jnp.arange(2, dtype=jnp.int32))
        where = prefix[d] + jnp.sum(jnp.where(hit, came[:, None], 0), axis=(2, 3))
        spot.append(where if d == 0 else where[::-1])
        side.append(lane[d] if d == 0 else lane[d][::-1])
    stretch = span + 8
    origin = line[:, None]
    item = jnp.arange(items, dtype=jnp.int32)[None, :]
    width = mine[1]
    down = (origin > chip).astype(jnp.int32)
    lies = jnp.where(down == 1, spot[1], spot[0])
    on = jnp.where(down == 1, side[1], side[0])
    far_row = ((2 * down + (on != core)) * stretch + lies) * UNIT + (2 << ROW_BITS)
    near_row = (item % pairs) * width + ((item // pairs != core).astype(jnp.int32) << ROW_BITS)
    rows = jnp.where(origin == chip, near_row, far_row).reshape(-1)
    last = lies + units[0] - 1
    passed = sum((last >= r * size).astype(jnp.int32) for r in range(1, max(rounds for rounds, _ in PLANS)))
    ready = jnp.where(origin == chip, 0, passed + (on != core)).reshape(-1)
    found = mine[0][:, None] == ids
    location = jnp.sum(jnp.where(found, rows, 0), axis=1)
    when = jnp.sum(jnp.where(found, ready, 0), axis=1)
    return branch, jnp.stack(table), jnp.stack(place), jnp.stack(need), location, when


def ranks_of(owner):
    spots = jnp.arange(owner.shape[-1], dtype=jnp.int32)
    ahead = (owner[..., None, :] == owner[..., :, None]) & (spots[None, :] < spots[:, None])
    return jnp.sum(ahead.astype(jnp.int32), axis=-1)


def wanted_from(owner, pair, me, capacity):
    slot = jnp.where(owner == me, ranks_of(owner), capacity)
    hit = slot[:, None, :] == jnp.arange(capacity, dtype=jnp.int32)[:, None]
    return jnp.sum(jnp.where(hit, pair[:, None, :], 0), axis=-1)


def load_all(source, scratch, sem, parts=8):
    rows = source.shape[0] // parts
    return [
        pltpu.make_async_copy(source.at[pl.ds(i * rows, rows)], scratch.at[pl.ds(i * rows, rows)], sem) for i in range(parts)
    ]


def take_kernel(width, index_ref, blocks_ref, *refs):
    outs, (scratch, load, sem) = refs[:-3], refs[-3:]
    slots = outs[0].shape[0] // width
    loads = load_all(blocks_ref, scratch, load)
    for c in loads:
        c.start()
    for c in loads:
        c.wait()

    def copies(i):
        for k, out in enumerate(outs):
            row = pl.multiple_of(index_ref[k * slots + i] * width, UNIT)
            yield pltpu.make_async_copy(
                scratch.at[pl.ds(row, width)], out.at[pl.ds(pl.multiple_of(i * width, UNIT), width)], sem
            )

    @pl.loop(0, slots)
    def _(i):
        for c in copies(i):
            c.start()

    @pl.loop(0, slots)
    def _(i):
        for c in copies(i):
            c.wait()


def take(blocks, index, width, parts):
    slots = index.shape[0] // parts
    shape = jax.ShapeDtypeStruct((slots * width, blocks.shape[1]), blocks.dtype)
    return pl.pallas_call(
        functools.partial(take_kernel, width),
        in_specs=[SMEM, ANY],
        out_specs=[ANY] * parts,
        out_shape=[shape] * parts,
        scratch_shapes=[pltpu.VMEM(blocks.shape, blocks.dtype), pltpu.SemaphoreType.DMA, pltpu.SemaphoreType.DMA],
        compiler_params=params(),
        cost_estimate=pl.CostEstimate(flops=0, bytes_accessed=2 * parts * slots * width * blocks.shape[1] * 2, transcendentals=0),
    )(index, blocks)


def run_copies(runs_ref, d, r, window, size, source, base, out, sem, shift):
    first, length, back = runs_ref[d, r, 0], runs_ref[d, r, 1], runs_ref[d, r, 2]
    low = jnp.maximum(first, window * size)
    high = jnp.minimum(first + length, (window + 1) * size)
    taken = jnp.maximum(high - low, 0)
    begin = back + low - first if shift else low
    rows = taken * UNIT
    return taken, pltpu.make_async_copy(
        source.at[pl.ds(pl.multiple_of((base + jnp.maximum(begin, 0)) * UNIT, UNIT), rows)],
        out.at[pl.ds(pl.multiple_of((low - window * size) * UNIT, UNIT), rows)],
        sem,
    )


def windows(runs_ref, picks, window, size, source, bases, outs, sem, shift, act):
    for d in range(2):
        for r in picks:
            taken, copy = run_copies(runs_ref, d, r, window, size, source, bases[d], outs[d], sem, shift)

            @pl.when(taken > 0)
            def _():
                getattr(copy, act)()


def items_of(pairs, core_ref, sources, visit):
    for half, source in enumerate(sources):

        @pl.loop(0, pairs)
        def _(i):
            for d in range(2):
                visit(source, i, d, (core_ref[0] ^ half) * pairs + i)


def open_kernel(size, span, pairs, width, own, place_ref, need_ref, runs_ref, core_ref, mine_ref, other_ref, stream_ref, *refs):
    outs, (near, beside, load, sem) = refs[:-4], refs[-4:]
    loads = load_all(mine_ref, near, load) + load_all(other_ref, beside, load)
    for c in loads:
        c.start()
    for c in loads:
        c.wait()
    straight = (0, span)

    def visit(source, i, d, item):
        units = need_ref[d, item]

        @pl.when(units > 0)
        def _():
            pltpu.make_async_copy(
                source.at[pl.ds(pl.multiple_of(i * width, UNIT), units * UNIT)],
                stream_ref.at[pl.ds(pl.multiple_of((straight[d] + place_ref[d, item]) * UNIT, UNIT), units * UNIT)],
                sem,
            ).start()

    items_of(pairs, core_ref, (near, beside), visit)
    for d in range(2):
        total = sum(runs_ref[d, r, 1] for r in range(own)) * UNIT

        @pl.when(total > 0)
        def _():
            pltpu.make_async_copy(near.at[pl.ds(0, total)], stream_ref.at[pl.ds(0, total)], sem).wait()

    for act in ("start", "wait"):
        for window in range(2):
            part = [out.at[pl.ds(window * size * UNIT, size * UNIT)] for out in outs]
            windows(runs_ref, range(own), window, size, stream_ref, straight, part, sem, False, act)


def step_kernel(size, stretch, own, at, other_at, next_windows, runs_ref, stream_ref, *refs):
    refs = list(refs)
    if other_at is not None:
        refs.pop(0)
    came = [refs.pop(0), refs.pop(0)]
    other = [refs.pop(0), refs.pop(0)] if other_at is not None else []
    hold = refs.pop(0)
    arrive, rest, lay = refs[-3:]
    outs = refs[:-3]
    rows = size * UNIT

    def filed(piece, section, number, sem):
        return pltpu.make_async_copy(
            piece, hold.at[pl.ds(section * stretch * UNIT + number * rows, piece.shape[0])], sem
        )

    first = [filed(c, 2 * d, at, arrive.at[d]) for d, c in enumerate(came)]
    second = [filed(c, 2 * d + 1, other_at, rest.at[d]) for d, c in enumerate(other)]
    for c in first + second:
        c.start()
    straight, through = (0, stretch - 8), (0, 2 * stretch)

    def lay_out(passed, act):
        picks = range(own, runs_ref.shape[1]) if passed else range(own)
        for i, window in enumerate(next_windows):
            source, bases = (hold, through) if passed else (stream_ref, straight)
            windows(runs_ref, picks, window, size, source, bases, outs[2 * i : 2 * i + 2], lay, passed, act)

    lay_out(False, "start")
    for c in first:
        c.wait()
    lay_out(True, "start")
    lay_out(False, "wait")
    lay_out(True, "wait")
    for c in second:
        c.wait()


def close_kernel(size, stretch, number, came_up, came_down, held_ref, hold, sem):
    del held_ref
    rows = size * UNIT
    copies = [
        pltpu.make_async_copy(c, hold.at[pl.ds((2 * d + 1) * stretch * UNIT + number * rows, rows)], sem.at[d])
        for d, c in enumerate((came_up, came_down))
    ]
    for c in copies:
        c.start()
    for c in copies:
        c.wait()


def couple_kernel(width, depth, many, low, high, begun, threads, loc_ref, when_ref, count_ref, target_ref, coef_ref, metric_ref, *refs):
    refs = list(refs)
    tasks = loc_ref.shape[0] - 1
    acc_ref = refs.pop(0) if begun else None
    line, slots, sems = refs[-3:]
    out_ref = refs[-5] if threads else refs[-4]
    buffers = refs[: -5 if threads else -4]
    out_ref[...] = acc_ref[...] if begun else jnp.zeros_like(out_ref)

    def gather(t, found):
        line[found] = t
        return found + ((when_ref[t] > low) & (when_ref[t] <= high)).astype(jnp.int32)

    found = lax.fori_loop(0, tasks, gather, jnp.int32(0))
    for u in range(many):
        line[found + u] = tasks
    groups = lax.div(found + (many - 1), jnp.int32(many))

    def fetch(group, phase):
        for u in range(many):
            code = loc_ref[line[group * many + u]]
            row = pl.multiple_of(code & ((1 << ROW_BITS) - 1), UNIT)
            for b, source in enumerate(buffers):

                @pl.when((code >> ROW_BITS) == b)
                def _():
                    pltpu.make_async_copy(source.at[pl.ds(row, width)], slots.at[phase, u], sems.at[phase, u]).start()

    @pl.when(groups > 0)
    def _():
        fetch(0, 0)

    @pl.loop(0, groups)
    def _(group):
        phase = lax.rem(group, 2)

        @pl.when(group + 1 < groups)
        def _():
            fetch(group + 1, 1 - phase)

        for u in range(many):
            pltpu.make_async_copy(buffers[0].at[pl.ds(0, width)], slots.at[phase, u], sems.at[phase, u]).wait()
        crossed, amps = [], []
        for u in range(many):
            t = line[group * many + u]
            live = lax.broadcasted_iota(jnp.int32, (width, width), 0) < count_ref[t]
            turned = lax.dot_general(
                slots[phase, u, :, pl.ds(0, depth)],
                metric_ref[target_ref[t]],
                (((1,), (1,)), ((), ())),
                preferred_element_type=jnp.float32,
            )
            crossed.append(jnp.where(live, turned, 0.0).astype(jnp.bfloat16))
            amp = slots[phase, u, :, pl.ds(depth, width)]
            amps.append(jnp.where(live, amp, jnp.zeros_like(amp)))
        halves = [
            lax.dot_general(turned, amp, (((0,), (0,)), ((), ())), preferred_element_type=jnp.float32).astype(jnp.bfloat16)
            for turned, amp in zip(crossed, amps)
        ]
        terms = [
            coef_ref[line[group * many + u]] * jnp.dot(halves[u], crossed[u], preferred_element_type=jnp.float32)
            for u in range(many)
        ]
        for u in range(many):
            target = target_ref[line[group * many + u]]
            out_ref[target] = out_ref[target] - terms[u]


def couple(lists, metric, acc, buffers, low, high, threaded=None):
    tasks, (pairs, width, depth) = lists[0].shape[0] - 1, metric.shape
    many = MANY
    operands = list(lists) + [metric] + ([] if acc is None else [acc]) + buffers
    out_shape = [jax.ShapeDtypeStruct((pairs, width, width), jnp.float32)]
    out_specs, aliases = [IN_VMEM], {}
    if threaded is not None:
        at = len(operands) - len(buffers) + threaded
        aliases = {at: 1}
        out_shape.append(jax.ShapeDtypeStruct(operands[at].shape, operands[at].dtype))
        out_specs.append(ANY)
    return pl.pallas_call(
        functools.partial(couple_kernel, width, depth, many, low, high, acc is not None, threaded is not None),
        in_specs=[SMEM] * 5 + [IN_VMEM] * (1 if acc is None else 2) + [ANY] * len(buffers),
        out_specs=out_specs,
        out_shape=out_shape,
        input_output_aliases=aliases,
        scratch_shapes=[
            pltpu.SMEM((tasks + many,), jnp.int32),
            pltpu.VMEM((2, many, width, depth + width), jnp.bfloat16),
            pltpu.SemaphoreType.DMA((2, many)),
        ],
        compiler_params=params(),
        cost_estimate=pl.CostEstimate(flops=0, bytes_accessed=20_000_000, transcendentals=0),
    )(*operands)


def relay(rounds, size, chips, pairs, width, table, place, need, core, lists, mine, other, metric_of, cross_take, crossed):
    columns = mine.shape[1]
    stretch = rounds * size + 8
    parts = (2, 4, rounds - 3, rounds - 2)
    own = chips - 1
    piece = jax.ShapeDtypeStruct((size * UNIT, columns), mine.dtype)
    double = jax.ShapeDtypeStruct((2 * size * UNIT, columns), mine.dtype)
    stream_shape = jax.ShapeDtypeStruct((2 * rounds * size * UNIT, columns), mine.dtype)
    hold_shape = jax.ShapeDtypeStruct((4 * stretch * UNIT, columns), mine.dtype)
    members = 2 * chips
    ways = [
        [(i, i + 2) for i in range(members - 2)],
        [(i + 2, i) for i in range(members - 2)],
    ]
    across = [(i, i ^ 1) for i in range(members)]
    stream, *opened = pl.pallas_call(
        functools.partial(open_kernel, size, rounds * size, pairs, width, own),
        in_specs=[SMEM] * 4 + [ANY] * 2,
        out_specs=[ANY] + [IN_VMEM] * 2,
        out_shape=[stream_shape] + [double] * 2,
        scratch_shapes=[pltpu.VMEM(mine.shape, mine.dtype)] * 2 + [pltpu.SemaphoreType.DMA] * 2,
        compiler_params=params(),
        cost_estimate=pl.CostEstimate(flops=0, bytes_accessed=6 * mine.size * 2, transcendentals=0),
    )(place, need, table, core, mine, other)
    sends = {1: opened}
    stream, after = lax.optimization_barrier((stream, mine))
    taken = cross_take(after)
    metric, crossing = metric_of(after), crossed(taken)
    hold, swapped, acc, done = None, None, None, -1
    for number in range(1, rounds):
        came = [lax.ppermute(sends[number][d], "mem", ways[d]) for d in range(2)]
        if number == 1:
            *came, _, metric = lax.optimization_barrier((*came, taken, metric))
        else:
            if number - 1 in parts:
                came[0], hold = lax.optimization_barrier((came[0], hold))
                buffers = [mine, other, hold] + ([crossing] if number - 1 >= rounds - 3 else [])
                acc, hold = couple(lists, metric, acc, buffers, done, number - 1, 2)
                done = number - 1
            *came, hold = lax.optimization_barrier((*came, hold))
        swapping = [lax.ppermute(came[d], "mem", across) for d in range(2)]
        if number == rounds - 3:
            *came, crossing = lax.optimization_barrier((*came, crossing))
        begun = hold is not None
        ahead = [w for w in ((2, 3) if number == 1 else (number + 2,)) if w < rounds]
        operands = [table, stream] + ([hold] if begun else []) + came + (swapped if begun else [])
        hold, *going = pl.pallas_call(
            functools.partial(
                step_kernel,
                size,
                stretch,
                own,
                0 if number == 1 else number,
                None if not begun else (0 if number == 2 else number - 1),
                ahead,
            ),
            in_specs=[SMEM, ANY] + ([ANY] if begun else []) + [IN_VMEM] * (4 if begun else 2),
            out_specs=[ANY] + [IN_VMEM] * (2 * len(ahead)),
            out_shape=[hold_shape] + [piece] * (2 * len(ahead)),
            input_output_aliases={2: 0} if begun else {},
            scratch_shapes=[pltpu.SemaphoreType.DMA((2,)), pltpu.SemaphoreType.DMA((2,)), pltpu.SemaphoreType.DMA],
            compiler_params=params(),
            cost_estimate=pl.CostEstimate(flops=0, bytes_accessed=12 * size * UNIT * columns * 2, transcendentals=0),
        )(*operands)
        swapped = swapping
        for i, window in enumerate(ahead):
            sends[window] = going[2 * i : 2 * i + 2]
    hold = pl.pallas_call(
        functools.partial(close_kernel, size, stretch, rounds - 1),
        in_specs=[IN_VMEM] * 2 + [ANY],
        out_specs=ANY,
        out_shape=hold_shape,
        input_output_aliases={2: 0},
        scratch_shapes=[pltpu.SemaphoreType.DMA((2,))],
        compiler_params=params(),
    )(*swapped, hold)
    [acc] = couple(lists, metric, acc, [mine, other, hold, crossing], done, rounds)
    return acc


def shards(
    pno,
    amplitudes,
    pno_count,
    pao_coupling,
    row_owner,
    row_pair,
    row_target,
    row_coef,
    column_owner,
    column_pair,
    column_target,
    column_coef,
):
    pairs, depth, width = pno.shape
    tasks, crossings = row_pair.shape[0], column_pair.shape[0]
    members, groups = lax.axis_size("mem"), lax.axis_size("grp")
    member, group = lax.axis_index("mem"), lax.axis_index("grp")
    row_cap = max(2, 2 * tasks // members)
    col_cap = max(2, 2 * crossings // groups)
    chips = members // 2
    row_owner, column_owner = row_owner[:, 0], column_owner[:, 0]
    row_code = row_owner * pairs + row_pair
    col_code = column_owner * pairs + column_pair
    tell = jnp.concatenate([row_code, col_code, pno_count])
    told = lax.all_to_all(
        jnp.broadcast_to(tell, (groups * members, tell.shape[0])), ("grp", "mem"), split_axis=0, concat_axis=0, tiled=True
    )
    told = told.reshape(groups, members, -1)
    code, cols, count = told[..., :tasks], told[..., tasks : tasks + crossings], told[..., tasks + crossings :]
    blocks = blocks_of(pno, amplitudes, pno_count)
    ids = jnp.arange(members * pairs, dtype=jnp.int32)
    here = pick(count, group).reshape(-1)
    row_count = jnp.sum(jnp.where(row_code[:, None] == ids, here, 0), axis=1)
    beside = lax.dynamic_index_in_dim(count, member, 1, keepdims=False).reshape(-1)
    col_ids = jnp.arange(groups * pairs, dtype=jnp.int32)
    col_count = jnp.sum(jnp.where(col_code[:, None] == col_ids, beside, 0), axis=1)
    ask = lax.dynamic_index_in_dim(cols, member, 1, keepdims=False)
    asked = wanted_from(ask // pairs, ask % pairs, group, col_cap)
    col_row = (column_owner * col_cap + ranks_of(column_owner)) * width

    def metric_of(blocks):
        return metric_blocks(blocks, pao_coupling).reshape(pairs, width, depth)

    def cross_take(blocks):
        return take(blocks, asked.reshape(-1), width, 1)[0]

    def crossed(sent):
        return lax.all_to_all(sent, "grp", split_axis=0, concat_axis=0, tiled=True)

    def lists_of(location, when, first):
        col_location = col_row + (first << ROW_BITS)
        none = jnp.zeros((1,), jnp.int32)
        return (
            jnp.concatenate([location, col_location, none]),
            jnp.concatenate([when, jnp.full_like(col_location, CROSS_AFTER), none]),
            jnp.concatenate([row_count, col_count, none]),
            jnp.concatenate([row_target, column_target, none]),
            jnp.concatenate([row_coef, column_coef, none.astype(jnp.float32)]),
        )

    def plain(*_):
        want = wanted_from(pick(code, group) // pairs, pick(code, group) % pairs, member, row_cap)
        [sent] = take(blocks, want.reshape(-1), width, 1)
        got = lax.all_to_all(sent, "mem", split_axis=0, concat_axis=0, tiled=True)
        location = (row_owner * row_cap + ranks_of(row_owner)) * width + (1 << ROW_BITS)
        lists = lists_of(location, jnp.zeros_like(location), 2)
        [acc] = couple(lists, metric_of(blocks), None, [blocks, got, crossed(cross_take(blocks))], -1, CROSS_AFTER)
        return acc

    if members % 2 or chips < 2 or chips > 4:
        return plain()
    other = lax.ppermute(blocks, "mem", [(i, i ^ 1) for i in range(members)])
    branch, table, place, need, location, when = relay_plan(code, count, group, member, (row_code, width))
    core = (member % 2).reshape(1).astype(jnp.int32)

    lists = lists_of(location, when, 3)

    def relayed(rounds, size):
        return relay(rounds, size, chips, pairs, width, table, place, need, core, lists, blocks, other, metric_of, cross_take, crossed)

    return lax.switch(branch, [functools.partial(relayed, *p) for p in PLANS] + [plain])


def solution(mesh):
    in_specs = (
        P(("grp", "mem"), None, None),
        P(("grp", "mem"), None, None),
        P(("grp", "mem")),
        P(),
        P(("grp", "mem"), None),
        P(("grp", "mem")),
        P(("grp", "mem")),
        P(("grp", "mem")),
        P(("grp", "mem"), None),
        P(("grp", "mem")),
        P(("grp", "mem")),
        P(("grp", "mem")),
    )
    out_specs = P(("grp", "mem"), None, None)
    return jax.shard_map(shards, mesh=mesh, in_specs=in_specs, out_specs=out_specs, check_vma=False)
```

```python
import functools

import jax
import jax.numpy as jnp
from jax import lax
from jax.experimental import pallas as pl
from jax.experimental.pallas import tpu as pltpu
from jax.sharding import PartitionSpec as P

UNIT = 16
PLANS = ((8, 35), (8, 37), (9, 36))
VMEM = 48 * 2**20
CROSS_AFTER = 5
ROW_BITS = 20
MANY = 8
ANY = pl.BlockSpec(memory_space=pl.ANY)
SMEM = pl.BlockSpec(memory_space=pltpu.SMEM)
IN_VMEM = pl.BlockSpec(memory_space=pltpu.VMEM)


def params():
    return pltpu.CompilerParams(vmem_limit_bytes=VMEM)


def block_kernel(count_ref, pno_ref, amp_ref, out_ref):
    step = pl.program_id(0)
    many, depth, width = pno_ref.shape
    for i in range(many):
        count = count_ref[step * many + i]
        rows = lax.broadcasted_iota(jnp.int32, (width, depth), 0)
        turned = pno_ref[i].T
        out_ref[pl.ds(i * width, width), pl.ds(0, depth)] = jnp.where(rows < count, turned, jnp.zeros_like(turned))
        down = lax.broadcasted_iota(jnp.int32, (width, width), 0)
        across = lax.broadcasted_iota(jnp.int32, (width, width), 1)
        amp = amp_ref[i]
        live = (down < count) & (across < count)
        out_ref[pl.ds(i * width, width), pl.ds(depth, width)] = jnp.where(live, amp, jnp.zeros_like(amp))


def blocks_of(pno, amplitudes, pno_count):
    pairs, depth, width = pno.shape
    many = 4
    return pl.pallas_call(
        block_kernel,
        grid=(pairs // many,),
        in_specs=[
            SMEM,
            pl.BlockSpec((many, depth, width), lambda i: (i, 0, 0)),
            pl.BlockSpec((many, width, width), lambda i: (i, 0, 0)),
        ],
        out_specs=pl.BlockSpec((many * width, depth + width), lambda i: (i, 0)),
        out_shape=jax.ShapeDtypeStruct((pairs * width, depth + width), pno.dtype),
        compiler_params=pltpu.CompilerParams(vmem_limit_bytes=60 * 2**20),
    )(pno_count, pno, amplitudes)


def metric_kernel(depth, block_ref, coupling_ref, out_ref):
    live = block_ref[:, pl.ds(0, depth)]
    mixed = jnp.dot(live, coupling_ref[...], preferred_element_type=jnp.float32)
    out_ref[...] = (live.astype(jnp.float32) + mixed).astype(out_ref.dtype)


def metric_blocks(blocks, pao_coupling):
    rows, columns = blocks.shape
    depth = pao_coupling.shape[0]
    tile = 512
    return pl.pallas_call(
        functools.partial(metric_kernel, depth),
        grid=(rows // tile,),
        in_specs=[pl.BlockSpec((tile, columns), lambda i: (i, 0)), pl.BlockSpec((depth, depth), lambda i: (0, 0))],
        out_specs=pl.BlockSpec((tile, depth), lambda i: (i, 0)),
        out_shape=jax.ShapeDtypeStruct((rows, depth), blocks.dtype),
        compiler_params=params(),
        cost_estimate=pl.CostEstimate(flops=0, bytes_accessed=20_000_000, transcendentals=0),
    )(blocks, pao_coupling)


def pick(array, index):
    return lax.dynamic_index_in_dim(array, index, 0, keepdims=False)


def starts_of(lengths, chips, delay):
    starts, ends = {}, []
    for c in range(chips - 1):
        at = jnp.zeros_like(lengths[0][chips - 1])
        for f in range(chips - 1, c, -1):
            for o in range(c, -1, -1):
                if o < c:
                    at = jnp.where(lengths[o][f] > 0, jnp.maximum(at, starts[o, f, c - 1] + delay), at)
                starts[o, f, c] = at
                at = at + lengths[o][f]
        ends.append(at)
    return starts, functools.reduce(jnp.maximum, ends)


def relay_plan(code, count, group, member, mine):
    groups, members, _ = code.shape
    pairs = count.shape[2]
    chips, items = members // 2, 2 * pairs
    chip, core = member // 2, member % 2
    ids = jnp.arange(members * pairs, dtype=jnp.int32)
    asked = jnp.any(code[..., None, :] == ids[:, None], axis=-1)
    asked = jnp.any(asked.reshape(groups, chips, 2, chips, items), axis=2)
    asked = jnp.stack([asked, asked[:, ::-1, ::-1]])
    line = jnp.arange(chips, dtype=jnp.int32)
    later = (line[:, None] > line[None, :])[:, :, None]
    far = jnp.max(jnp.where(asked & later, line[:, None, None], 0), axis=2)
    units = ((count + UNIT - 1) // UNIT).reshape(groups, chips, items)
    units = jnp.stack([units, units[:, ::-1]])
    order = far * items + (items - 1 - jnp.arange(items, dtype=jnp.int32))
    before = (order[..., None, :] > order[..., :, None]) & (far[..., None, :] > 0)
    lane = jnp.sum(before.astype(jnp.int32), axis=-1) & 1
    kind = far * 2 + lane
    ahead = before & (kind[..., None, :] == kind[..., :, None])
    prefix = jnp.sum(jnp.where(ahead, units[..., None, :], 0), axis=-1)
    kinds = jnp.arange(2 * chips, dtype=jnp.int32)
    total = jnp.sum(jnp.where(kind[..., None, :] == kinds[:, None], units[..., None, :], 0), axis=-1)
    total = total.reshape(2, groups, chips, chips, 2)
    lengths = [[total[:, :, o, f] for f in range(chips)] for o in range(chips)]
    branch, size, span = jnp.int32(len(PLANS)), jnp.int32(PLANS[-1][1]), jnp.int32(PLANS[-1][0] * PLANS[-1][1])
    for b, (rounds, width) in reversed(list(enumerate(PLANS))):
        fits = jnp.max(starts_of(lengths, chips, 2 * width)[1]) <= rounds * width
        branch, size, span = (jnp.where(fits, x, y) for x, y in ((b, branch), (width, size), (rounds * width, span)))

    def own_group(x):
        return lax.dynamic_index_in_dim(x, group, 1, keepdims=False)

    far, lane, prefix, units, total = (own_group(x) for x in (far, lane, prefix, units, total))
    lengths = [[total[:, o, f] for f in range(chips)] for o in range(chips)]
    starts = starts_of(lengths, chips, 2 * size)[0]
    none = jnp.zeros_like(lengths[0][0])
    runs = []
    most = max(c * (chips - 1 - c) for c in range(chips))
    for c in range(chips):
        own = [(starts[c, f, c], lengths[c][f], none) if f > c else (none, none, none) for f in range(1, chips)]
        passed = [(starts[o, f, c], lengths[o][f], starts[o, f, c - 1]) for o in range(c) for f in range(c + 1, chips)]
        passed += [(none, none, none)] * (most - len(passed))
        runs.append(jnp.stack([jnp.stack(r) for r in own + passed]))
    runs = jnp.stack(runs)
    outgo = jnp.stack([jnp.stack([starts[c, f, c] if f > c else none for f in range(chips)]) for c in range(chips)])
    income = jnp.stack(
        [
            jnp.stack([jnp.stack([starts[o, f, c - 1] if o < c <= f else none for f in range(chips)]) for o in range(chips)])
            for c in range(chips)
        ]
    )
    table, place, need, spot, side = [], [], [], [], []
    for d in range(2):
        at = chip if d == 0 else chips - 1 - chip
        table.append(lax.dynamic_index_in_dim(pick(runs, at)[..., d, :], core, 2, keepdims=False))
        home = pick(far[d], at)
        chosen = lax.dynamic_index_in_dim(pick(outgo, at)[:, d, :], core, 1, keepdims=False)
        first = jnp.sum(jnp.where(home[:, None] == line, chosen, 0), axis=1)
        place.append(first + pick(prefix[d], at))
        need.append(jnp.where((home > 0) & (pick(lane[d], at) == core), pick(units[d], at), 0))
        came = pick(income, at)[:, :, d, :]
        hit = (far[d][:, :, None, None] == line[:, None]) & (lane[d][:, :, None, None] == jnp.arange(2, dtype=jnp.int32))
        where = prefix[d] + jnp.sum(jnp.where(hit, came[:, None], 0), axis=(2, 3))
        spot.append(where if d == 0 else where[::-1])
        side.append(lane[d] if d == 0 else lane[d][::-1])
    stretch = span + 8
    origin = line[:, None]
    item = jnp.arange(items, dtype=jnp.int32)[None, :]
    width = mine[1]
    down = (origin > chip).astype(jnp.int32)
    lies = jnp.where(down == 1, spot[1], spot[0])
    on = jnp.where(down == 1, side[1], side[0])
    far_row = ((2 * down + (on != core)) * stretch + lies) * UNIT + (2 << ROW_BITS)
    near_row = (item % pairs) * width + ((item // pairs != core).astype(jnp.int32) << ROW_BITS)
    rows = jnp.where(origin == chip, near_row, far_row).reshape(-1)
    last = lies + units[0] - 1
    passed = sum((last >= r * size).astype(jnp.int32) for r in range(1, max(rounds for rounds, _ in PLANS)))
    ready = jnp.where(origin == chip, 0, passed + (on != core)).reshape(-1)
    found = mine[0][:, None] == ids
    location = jnp.sum(jnp.where(found, rows, 0), axis=1)
    when = jnp.sum(jnp.where(found, ready, 0), axis=1)
    return branch, jnp.stack(table), jnp.stack(place), jnp.stack(need), location, when


def ranks_of(owner):
    spots = jnp.arange(owner.shape[-1], dtype=jnp.int32)
    ahead = (owner[..., None, :] == owner[..., :, None]) & (spots[None, :] < spots[:, None])
    return jnp.sum(ahead.astype(jnp.int32), axis=-1)


def wanted_from(owner, pair, me, capacity):
    slot = jnp.where(owner == me, ranks_of(owner), capacity)
    hit = slot[:, None, :] == jnp.arange(capacity, dtype=jnp.int32)[:, None]
    return jnp.sum(jnp.where(hit, pair[:, None, :], 0), axis=-1)


def load_all(source, scratch, sem, parts=8):
    rows = source.shape[0] // parts
    return [
        pltpu.make_async_copy(source.at[pl.ds(i * rows, rows)], scratch.at[pl.ds(i * rows, rows)], sem) for i in range(parts)
    ]


def take_kernel(width, index_ref, blocks_ref, *refs):
    outs, (scratch, load, sem) = refs[:-3], refs[-3:]
    slots = outs[0].shape[0] // width
    loads = load_all(blocks_ref, scratch, load)
    for c in loads:
        c.start()
    for c in loads:
        c.wait()

    def copies(i):
        for k, out in enumerate(outs):
            row = pl.multiple_of(index_ref[k * slots + i] * width, UNIT)
            yield pltpu.make_async_copy(
                scratch.at[pl.ds(row, width)], out.at[pl.ds(pl.multiple_of(i * width, UNIT), width)], sem
            )

    @pl.loop(0, slots)
    def _(i):
        for c in copies(i):
            c.start()

    @pl.loop(0, slots)
    def _(i):
        for c in copies(i):
            c.wait()


def take(blocks, index, width, parts):
    slots = index.shape[0] // parts
    shape = jax.ShapeDtypeStruct((slots * width, blocks.shape[1]), blocks.dtype)
    return pl.pallas_call(
        functools.partial(take_kernel, width),
        in_specs=[SMEM, ANY],
        out_specs=[ANY] * parts,
        out_shape=[shape] * parts,
        scratch_shapes=[pltpu.VMEM(blocks.shape, blocks.dtype), pltpu.SemaphoreType.DMA, pltpu.SemaphoreType.DMA],
        compiler_params=params(),
        cost_estimate=pl.CostEstimate(flops=0, bytes_accessed=2 * parts * slots * width * blocks.shape[1] * 2, transcendentals=0),
    )(index, blocks)


def run_copies(runs_ref, d, r, window, size, source, base, out, sem, shift):
    first, length, back = runs_ref[d, r, 0], runs_ref[d, r, 1], runs_ref[d, r, 2]
    low = jnp.maximum(first, window * size)
    high = jnp.minimum(first + length, (window + 1) * size)
    taken = jnp.maximum(high - low, 0)
    begin = back + low - first if shift else low
    rows = taken * UNIT
    return taken, pltpu.make_async_copy(
        source.at[pl.ds(pl.multiple_of((base + jnp.maximum(begin, 0)) * UNIT, UNIT), rows)],
        out.at[pl.ds(pl.multiple_of((low - window * size) * UNIT, UNIT), rows)],
        sem,
    )


def windows(runs_ref, picks, window, size, source, bases, outs, sem, shift, act):
    for d in range(2):
        for r in picks:
            taken, copy = run_copies(runs_ref, d, r, window, size, source, bases[d], outs[d], sem, shift)

            @pl.when(taken > 0)
            def _():
                getattr(copy, act)()


def items_of(pairs, core_ref, sources, visit):
    for half, source in enumerate(sources):

        @pl.loop(0, pairs)
        def _(i):
            for d in range(2):
                visit(source, i, d, (core_ref[0] ^ half) * pairs + i)


def open_kernel(size, span, pairs, width, own, place_ref, need_ref, runs_ref, core_ref, mine_ref, other_ref, stream_ref, *refs):
    outs, (near, beside, load, sem) = refs[:-4], refs[-4:]
    loads = load_all(mine_ref, near, load) + load_all(other_ref, beside, load)
    for c in loads:
        c.start()
    for c in loads:
        c.wait()
    straight = (0, span)

    def visit(source, i, d, item):
        units = need_ref[d, item]

        @pl.when(units > 0)
        def _():
            pltpu.make_async_copy(
                source.at[pl.ds(pl.multiple_of(i * width, UNIT), units * UNIT)],
                stream_ref.at[pl.ds(pl.multiple_of((straight[d] + place_ref[d, item]) * UNIT, UNIT), units * UNIT)],
                sem,
            ).start()

    items_of(pairs, core_ref, (near, beside), visit)
    for d in range(2):
        total = sum(runs_ref[d, r, 1] for r in range(own)) * UNIT

        @pl.when(total > 0)
        def _():
            pltpu.make_async_copy(near.at[pl.ds(0, total)], stream_ref.at[pl.ds(0, total)], sem).wait()

    for act in ("start", "wait"):
        for window in range(2):
            part = [out.at[pl.ds(window * size * UNIT, size * UNIT)] for out in outs]
            windows(runs_ref, range(own), window, size, stream_ref, straight, part, sem, False, act)


def step_kernel(size, stretch, own, at, other_at, next_windows, runs_ref, stream_ref, *refs):
    refs = list(refs)
    if other_at is not None:
        refs.pop(0)
    came = [refs.pop(0), refs.pop(0)]
    other = [refs.pop(0), refs.pop(0)] if other_at is not None else []
    hold = refs.pop(0)
    arrive, rest, lay = refs[-3:]
    outs = refs[:-3]
    rows = size * UNIT

    def filed(piece, section, number, sem):
        return pltpu.make_async_copy(
            piece, hold.at[pl.ds(section * stretch * UNIT + number * rows, piece.shape[0])], sem
        )

    first = [filed(c, 2 * d, at, arrive.at[d]) for d, c in enumerate(came)]
    second = [filed(c, 2 * d + 1, other_at, rest.at[d]) for d, c in enumerate(other)]
    for c in first + second:
        c.start()
    straight, through = (0, stretch - 8), (0, 2 * stretch)

    def lay_out(passed, act):
        picks = range(own, runs_ref.shape[1]) if passed else range(own)
        for i, window in enumerate(next_windows):
            source, bases = (hold, through) if passed else (stream_ref, straight)
            windows(runs_ref, picks, window, size, source, bases, outs[2 * i : 2 * i + 2], lay, passed, act)

    lay_out(False, "start")
    for c in first:
        c.wait()
    lay_out(True, "start")
    lay_out(False, "wait")
    lay_out(True, "wait")
    for c in second:
        c.wait()


def close_kernel(size, stretch, number, came_up, came_down, held_ref, hold, sem):
    del held_ref
    rows = size * UNIT
    copies = [
        pltpu.make_async_copy(c, hold.at[pl.ds((2 * d + 1) * stretch * UNIT + number * rows, rows)], sem.at[d])
        for d, c in enumerate((came_up, came_down))
    ]
    for c in copies:
        c.start()
    for c in copies:
        c.wait()


def couple_kernel(width, depth, many, low, high, begun, threads, loc_ref, when_ref, count_ref, target_ref, coef_ref, metric_ref, *refs):
    refs = list(refs)
    tasks = loc_ref.shape[0] - 1
    acc_ref = refs.pop(0) if begun else None
    line, slots, sems = refs[-3:]
    out_ref = refs[-5] if threads else refs[-4]
    buffers = refs[: -5 if threads else -4]
    out_ref[...] = acc_ref[...] if begun else jnp.zeros_like(out_ref)

    def gather(t, found):
        line[found] = t
        return found + ((when_ref[t] > low) & (when_ref[t] <= high)).astype(jnp.int32)

    found = lax.fori_loop(0, tasks, gather, jnp.int32(0))
    for u in range(many):
        line[found + u] = tasks
    groups = lax.div(found + (many - 1), jnp.int32(many))

    def fetch(group, phase):
        for u in range(many):
            code = loc_ref[line[group * many + u]]
            row = pl.multiple_of(code & ((1 << ROW_BITS) - 1), UNIT)
            for b, source in enumerate(buffers):

                @pl.when((code >> ROW_BITS) == b)
                def _():
                    pltpu.make_async_copy(source.at[pl.ds(row, width)], slots.at[phase, u], sems.at[phase, u]).start()

    @pl.when(groups > 0)
    def _():
        fetch(0, 0)

    @pl.loop(0, groups)
    def _(group):
        phase = lax.rem(group, 2)

        @pl.when(group + 1 < groups)
        def _():
            fetch(group + 1, 1 - phase)

        for u in range(many):
            pltpu.make_async_copy(buffers[0].at[pl.ds(0, width)], slots.at[phase, u], sems.at[phase, u]).wait()
        crossed, amps = [], []
        for u in range(many):
            t = line[group * many + u]
            live = lax.broadcasted_iota(jnp.int32, (width, width), 0) < count_ref[t]
            turned = lax.dot_general(
                slots[phase, u, :, pl.ds(0, depth)],
                metric_ref[target_ref[t]],
                (((1,), (1,)), ((), ())),
                preferred_element_type=jnp.float32,
            )
            crossed.append(jnp.where(live, turned, 0.0).astype(jnp.bfloat16))
            amp = slots[phase, u, :, pl.ds(depth, width)]
            amps.append(jnp.where(live, amp, jnp.zeros_like(amp)))
        halves = [
            lax.dot_general(turned, amp, (((0,), (0,)), ((), ())), preferred_element_type=jnp.float32).astype(jnp.bfloat16)
            for turned, amp in zip(crossed, amps)
        ]
        terms = [
            coef_ref[line[group * many + u]] * jnp.dot(halves[u], crossed[u], preferred_element_type=jnp.float32)
            for u in range(many)
        ]
        for u in range(many):
            target = target_ref[line[group * many + u]]
            out_ref[target] = out_ref[target] - terms[u]


def couple(lists, metric, acc, buffers, low, high, threaded=None):
    tasks, (pairs, width, depth) = lists[0].shape[0] - 1, metric.shape
    many = MANY
    operands = list(lists) + [metric] + ([] if acc is None else [acc]) + buffers
    out_shape = [jax.ShapeDtypeStruct((pairs, width, width), jnp.float32)]
    out_specs, aliases = [IN_VMEM], {}
    if threaded is not None:
        at = len(operands) - len(buffers) + threaded
        aliases = {at: 1}
        out_shape.append(jax.ShapeDtypeStruct(operands[at].shape, operands[at].dtype))
        out_specs.append(ANY)
    return pl.pallas_call(
        functools.partial(couple_kernel, width, depth, many, low, high, acc is not None, threaded is not None),
        in_specs=[SMEM] * 5 + [IN_VMEM] * (1 if acc is None else 2) + [ANY] * len(buffers),
        out_specs=out_specs,
        out_shape=out_shape,
        input_output_aliases=aliases,
        scratch_shapes=[
            pltpu.SMEM((tasks + many,), jnp.int32),
            pltpu.VMEM((2, many, width, depth + width), jnp.bfloat16),
            pltpu.SemaphoreType.DMA((2, many)),
        ],
        compiler_params=params(),
        cost_estimate=pl.CostEstimate(flops=0, bytes_accessed=20_000_000, transcendentals=0),
    )(*operands)


def relay(rounds, size, chips, pairs, width, table, place, need, core, lists, mine, other, metric_of, cross_take, crossed):
    columns = mine.shape[1]
    stretch = rounds * size + 8
    parts = (2, 4, rounds - 3, rounds - 2)
    own = chips - 1
    piece = jax.ShapeDtypeStruct((size * UNIT, columns), mine.dtype)
    double = jax.ShapeDtypeStruct((2 * size * UNIT, columns), mine.dtype)
    stream_shape = jax.ShapeDtypeStruct((2 * rounds * size * UNIT, columns), mine.dtype)
    hold_shape = jax.ShapeDtypeStruct((4 * stretch * UNIT, columns), mine.dtype)
    members = 2 * chips
    ways = [
        [(i, i + 2) for i in range(members - 2)],
        [(i + 2, i) for i in range(members - 2)],
    ]
    across = [(i, i ^ 1) for i in range(members)]
    stream, *opened = pl.pallas_call(
        functools.partial(open_kernel, size, rounds * size, pairs, width, own),
        in_specs=[SMEM] * 4 + [ANY] * 2,
        out_specs=[ANY] + [IN_VMEM] * 2,
        out_shape=[stream_shape] + [double] * 2,
        scratch_shapes=[pltpu.VMEM(mine.shape, mine.dtype)] * 2 + [pltpu.SemaphoreType.DMA] * 2,
        compiler_params=params(),
        cost_estimate=pl.CostEstimate(flops=0, bytes_accessed=6 * mine.size * 2, transcendentals=0),
    )(place, need, table, core, mine, other)
    sends = {1: opened}
    stream, after = lax.optimization_barrier((stream, mine))
    taken = cross_take(after)
    metric, crossing = metric_of(after), crossed(taken)
    hold, swapped, acc, done = None, None, None, -1
    for number in range(1, rounds):
        came = [lax.ppermute(sends[number][d], "mem", ways[d]) for d in range(2)]
        if number == 1:
            *came, _, metric = lax.optimization_barrier((*came, taken, metric))
        else:
            *came, hold = lax.optimization_barrier((*came, hold))
        swapping = [lax.ppermute(came[d], "mem", across) for d in range(2)]
        if number == rounds - 3:
            *came, crossing = lax.optimization_barrier((*came, crossing))
        begun = hold is not None
        ahead = [w for w in ((2, 3) if number == 1 else (number + 2,)) if w < rounds]
        operands = [table, stream] + ([hold] if begun else []) + came + (swapped if begun else [])
        hold, *going = pl.pallas_call(
            functools.partial(
                step_kernel,
                size,
                stretch,
                own,
                0 if number == 1 else number,
                None if not begun else (0 if number == 2 else number - 1),
                ahead,
            ),
            in_specs=[SMEM, ANY] + ([ANY] if begun else []) + [IN_VMEM] * (4 if begun else 2),
            out_specs=[ANY] + [IN_VMEM] * (2 * len(ahead)),
            out_shape=[hold_shape] + [piece] * (2 * len(ahead)),
            input_output_aliases={2: 0} if begun else {},
            scratch_shapes=[pltpu.SemaphoreType.DMA((2,)), pltpu.SemaphoreType.DMA((2,)), pltpu.SemaphoreType.DMA],
            compiler_params=params(),
            cost_estimate=pl.CostEstimate(flops=0, bytes_accessed=12 * size * UNIT * columns * 2, transcendentals=0),
        )(*operands)
        swapped = swapping
        if number in parts:
            buffers = [mine, other, hold] + ([crossing] if number >= rounds - 3 else [])
            acc, hold = couple(lists, metric, acc, buffers, done, number, 2)
            done = number
        for i, window in enumerate(ahead):
            sends[window] = going[2 * i : 2 * i + 2]
    hold = pl.pallas_call(
        functools.partial(close_kernel, size, stretch, rounds - 1),
        in_specs=[IN_VMEM] * 2 + [ANY],
        out_specs=ANY,
        out_shape=hold_shape,
        input_output_aliases={2: 0},
        scratch_shapes=[pltpu.SemaphoreType.DMA((2,))],
        compiler_params=params(),
    )(*swapped, hold)
    [acc] = couple(lists, metric, acc, [mine, other, hold, crossing], done, rounds)
    return acc


def shards(
    pno,
    amplitudes,
    pno_count,
    pao_coupling,
    row_owner,
    row_pair,
    row_target,
    row_coef,
    column_owner,
    column_pair,
    column_target,
    column_coef,
):
    pairs, depth, width = pno.shape
    tasks, crossings = row_pair.shape[0], column_pair.shape[0]
    members, groups = lax.axis_size("mem"), lax.axis_size("grp")
    member, group = lax.axis_index("mem"), lax.axis_index("grp")
    row_cap = max(2, 2 * tasks // members)
    col_cap = max(2, 2 * crossings // groups)
    chips = members // 2
    row_owner, column_owner = row_owner[:, 0], column_owner[:, 0]
    row_code = row_owner * pairs + row_pair
    col_code = column_owner * pairs + column_pair
    tell = jnp.concatenate([row_code, col_code, pno_count])
    told = lax.all_to_all(
        jnp.broadcast_to(tell, (groups * members, tell.shape[0])), ("grp", "mem"), split_axis=0, concat_axis=0, tiled=True
    )
    told = told.reshape(groups, members, -1)
    code, cols, count = told[..., :tasks], told[..., tasks : tasks + crossings], told[..., tasks + crossings :]
    blocks = blocks_of(pno, amplitudes, pno_count)
    ids = jnp.arange(members * pairs, dtype=jnp.int32)
    here = pick(count, group).reshape(-1)
    row_count = jnp.sum(jnp.where(row_code[:, None] == ids, here, 0), axis=1)
    beside = lax.dynamic_index_in_dim(count, member, 1, keepdims=False).reshape(-1)
    col_ids = jnp.arange(groups * pairs, dtype=jnp.int32)
    col_count = jnp.sum(jnp.where(col_code[:, None] == col_ids, beside, 0), axis=1)
    ask = lax.dynamic_index_in_dim(cols, member, 1, keepdims=False)
    asked = wanted_from(ask // pairs, ask % pairs, group, col_cap)
    col_row = (column_owner * col_cap + ranks_of(column_owner)) * width

    def metric_of(blocks):
        return metric_blocks(blocks, pao_coupling).reshape(pairs, width, depth)

    def cross_take(blocks):
        return take(blocks, asked.reshape(-1), width, 1)[0]

    def crossed(sent):
        return lax.all_to_all(sent, "grp", split_axis=0, concat_axis=0, tiled=True)

    def lists_of(location, when, first):
        col_location = col_row + (first << ROW_BITS)
        none = jnp.zeros((1,), jnp.int32)
        return (
            jnp.concatenate([location, col_location, none]),
            jnp.concatenate([when, jnp.full_like(col_location, CROSS_AFTER), none]),
            jnp.concatenate([row_count, col_count, none]),
            jnp.concatenate([row_target, column_target, none]),
            jnp.concatenate([row_coef, column_coef, none.astype(jnp.float32)]),
        )

    def plain(*_):
        want = wanted_from(pick(code, group) // pairs, pick(code, group) % pairs, member, row_cap)
        [sent] = take(blocks, want.reshape(-1), width, 1)
        got = lax.all_to_all(sent, "mem", split_axis=0, concat_axis=0, tiled=True)
        location = (row_owner * row_cap + ranks_of(row_owner)) * width + (1 << ROW_BITS)
        lists = lists_of(location, jnp.zeros_like(location), 2)
        [acc] = couple(lists, metric_of(blocks), None, [blocks, got, crossed(cross_take(blocks))], -1, CROSS_AFTER)
        return acc

    if members % 2 or chips < 2 or chips > 4:
        return plain()
    other = lax.ppermute(blocks, "mem", [(i, i ^ 1) for i in range(members)])
    branch, table, place, need, location, when = relay_plan(code, count, group, member, (row_code, width))
    core = (member % 2).reshape(1).astype(jnp.int32)

    lists = lists_of(location, when, 3)

    def relayed(rounds, size):
        return relay(rounds, size, chips, pairs, width, table, place, need, core, lists, blocks, other, metric_of, cross_take, crossed)

    return lax.switch(branch, [functools.partial(relayed, *p) for p in PLANS] + [plain])


def solution(mesh):
    in_specs = (
        P(("grp", "mem"), None, None),
        P(("grp", "mem"), None, None),
        P(("grp", "mem")),
        P(),
        P(("grp", "mem"), None),
        P(("grp", "mem")),
        P(("grp", "mem")),
        P(("grp", "mem")),
        P(("grp", "mem"), None),
        P(("grp", "mem")),
        P(("grp", "mem")),
        P(("grp", "mem")),
    )
    out_specs = P(("grp", "mem"), None, None)
    return jax.shard_map(shards, mesh=mesh, in_specs=in_specs, out_specs=out_specs, check_vma=False)
```

```python
import functools

import jax
import jax.numpy as jnp
from jax import lax
from jax.experimental import pallas as pl
from jax.experimental.pallas import tpu as pltpu
from jax.sharding import PartitionSpec as P

UNIT = 16
PLANS = ((8, 37), (9, 36))
VMEM = 48 * 2**20
CROSS_AFTER = 5
ROW_BITS = 20
MANY = 8
ANY = pl.BlockSpec(memory_space=pl.ANY)
SMEM = pl.BlockSpec(memory_space=pltpu.SMEM)
IN_VMEM = pl.BlockSpec(memory_space=pltpu.VMEM)


def params():
    return pltpu.CompilerParams(vmem_limit_bytes=VMEM)


def block_kernel(count_ref, pno_ref, amp_ref, out_ref):
    step = pl.program_id(0)
    many, depth, width = pno_ref.shape
    for i in range(many):
        count = count_ref[step * many + i]
        rows = lax.broadcasted_iota(jnp.int32, (width, depth), 0)
        turned = pno_ref[i].T
        out_ref[pl.ds(i * width, width), pl.ds(0, depth)] = jnp.where(rows < count, turned, jnp.zeros_like(turned))
        down = lax.broadcasted_iota(jnp.int32, (width, width), 0)
        across = lax.broadcasted_iota(jnp.int32, (width, width), 1)
        amp = amp_ref[i]
        live = (down < count) & (across < count)
        out_ref[pl.ds(i * width, width), pl.ds(depth, width)] = jnp.where(live, amp, jnp.zeros_like(amp))


def blocks_of(pno, amplitudes, pno_count):
    pairs, depth, width = pno.shape
    many = 4
    return pl.pallas_call(
        block_kernel,
        grid=(pairs // many,),
        in_specs=[
            SMEM,
            pl.BlockSpec((many, depth, width), lambda i: (i, 0, 0)),
            pl.BlockSpec((many, width, width), lambda i: (i, 0, 0)),
        ],
        out_specs=pl.BlockSpec((many * width, depth + width), lambda i: (i, 0)),
        out_shape=jax.ShapeDtypeStruct((pairs * width, depth + width), pno.dtype),
        compiler_params=pltpu.CompilerParams(vmem_limit_bytes=60 * 2**20),
    )(pno_count, pno, amplitudes)


def metric_kernel(depth, block_ref, coupling_ref, out_ref):
    live = block_ref[:, pl.ds(0, depth)]
    mixed = jnp.dot(live, coupling_ref[...], preferred_element_type=jnp.float32)
    out_ref[...] = (live.astype(jnp.float32) + mixed).astype(out_ref.dtype)


def metric_blocks(blocks, pao_coupling):
    rows, columns = blocks.shape
    depth = pao_coupling.shape[0]
    tile = 512
    return pl.pallas_call(
        functools.partial(metric_kernel, depth),
        grid=(rows // tile,),
        in_specs=[pl.BlockSpec((tile, columns), lambda i: (i, 0)), pl.BlockSpec((depth, depth), lambda i: (0, 0))],
        out_specs=pl.BlockSpec((tile, depth), lambda i: (i, 0)),
        out_shape=jax.ShapeDtypeStruct((rows, depth), blocks.dtype),
        compiler_params=params(),
        cost_estimate=pl.CostEstimate(flops=0, bytes_accessed=20_000_000, transcendentals=0),
    )(blocks, pao_coupling)


def pick(array, index):
    return lax.dynamic_index_in_dim(array, index, 0, keepdims=False)


def starts_of(lengths, chips, delay):
    starts, ends = {}, []
    for c in range(chips - 1):
        at = jnp.zeros_like(lengths[0][chips - 1])
        for f in range(chips - 1, c, -1):
            for o in range(c, -1, -1):
                if o < c:
                    at = jnp.where(lengths[o][f] > 0, jnp.maximum(at, starts[o, f, c - 1] + delay), at)
                starts[o, f, c] = at
                at = at + lengths[o][f]
        ends.append(at)
    return starts, functools.reduce(jnp.maximum, ends)


def relay_plan(code, count, group, member, mine):
    groups, members, _ = code.shape
    pairs = count.shape[2]
    chips, items = members // 2, 2 * pairs
    chip, core = member // 2, member % 2
    ids = jnp.arange(members * pairs, dtype=jnp.int32)
    asked = jnp.any(code[..., None, :] == ids[:, None], axis=-1)
    asked = jnp.any(asked.reshape(groups, chips, 2, chips, items), axis=2)
    asked = jnp.stack([asked, asked[:, ::-1, ::-1]])
    line = jnp.arange(chips, dtype=jnp.int32)
    later = (line[:, None] > line[None, :])[:, :, None]
    far = jnp.max(jnp.where(asked & later, line[:, None, None], 0), axis=2)
    units = ((count + UNIT - 1) // UNIT).reshape(groups, chips, items)
    units = jnp.stack([units, units[:, ::-1]])
    order = far * items + (items - 1 - jnp.arange(items, dtype=jnp.int32))
    before = (order[..., None, :] > order[..., :, None]) & (far[..., None, :] > 0)
    lane = jnp.sum(before.astype(jnp.int32), axis=-1) & 1
    kind = far * 2 + lane
    ahead = before & (kind[..., None, :] == kind[..., :, None])
    prefix = jnp.sum(jnp.where(ahead, units[..., None, :], 0), axis=-1)
    kinds = jnp.arange(2 * chips, dtype=jnp.int32)
    total = jnp.sum(jnp.where(kind[..., None, :] == kinds[:, None], units[..., None, :], 0), axis=-1)
    total = total.reshape(2, groups, chips, chips, 2)
    lengths = [[total[:, :, o, f] for f in range(chips)] for o in range(chips)]
    branch, size, span = jnp.int32(len(PLANS)), jnp.int32(PLANS[-1][1]), jnp.int32(PLANS[-1][0] * PLANS[-1][1])
    for b, (rounds, width) in reversed(list(enumerate(PLANS))):
        fits = jnp.max(starts_of(lengths, chips, 2 * width)[1]) <= rounds * width
        branch, size, span = (jnp.where(fits, x, y) for x, y in ((b, branch), (width, size), (rounds * width, span)))

    def own_group(x):
        return lax.dynamic_index_in_dim(x, group, 1, keepdims=False)

    far, lane, prefix, units, total = (own_group(x) for x in (far, lane, prefix, units, total))
    lengths = [[total[:, o, f] for f in range(chips)] for o in range(chips)]
    starts = starts_of(lengths, chips, 2 * size)[0]
    none = jnp.zeros_like(lengths[0][0])
    runs = []
    most = max(c * (chips - 1 - c) for c in range(chips))
    for c in range(chips):
        own = [(starts[c, f, c], lengths[c][f], none) if f > c else (none, none, none) for f in range(1, chips)]
        passed = [(starts[o, f, c], lengths[o][f], starts[o, f, c - 1]) for o in range(c) for f in range(c + 1, chips)]
        passed += [(none, none, none)] * (most - len(passed))
        runs.append(jnp.stack([jnp.stack(r) for r in own + passed]))
    runs = jnp.stack(runs)
    outgo = jnp.stack([jnp.stack([starts[c, f, c] if f > c else none for f in range(chips)]) for c in range(chips)])
    income = jnp.stack(
        [
            jnp.stack([jnp.stack([starts[o, f, c - 1] if o < c <= f else none for f in range(chips)]) for o in range(chips)])
            for c in range(chips)
        ]
    )
    table, place, need, spot, side = [], [], [], [], []
    for d in range(2):
        at = chip if d == 0 else chips - 1 - chip
        table.append(lax.dynamic_index_in_dim(pick(runs, at)[..., d, :], core, 2, keepdims=False))
        home = pick(far[d], at)
        chosen = lax.dynamic_index_in_dim(pick(outgo, at)[:, d, :], core, 1, keepdims=False)
        first = jnp.sum(jnp.where(home[:, None] == line, chosen, 0), axis=1)
        place.append(first + pick(prefix[d], at))
        need.append(jnp.where((home > 0) & (pick(lane[d], at) == core), pick(units[d], at), 0))
        came = pick(income, at)[:, :, d, :]
        hit = (far[d][:, :, None, None] == line[:, None]) & (lane[d][:, :, None, None] == jnp.arange(2, dtype=jnp.int32))
        where = prefix[d] + jnp.sum(jnp.where(hit, came[:, None], 0), axis=(2, 3))
        spot.append(where if d == 0 else where[::-1])
        side.append(lane[d] if d == 0 else lane[d][::-1])
    stretch = span + 8
    origin = line[:, None]
    item = jnp.arange(items, dtype=jnp.int32)[None, :]
    width = mine[1]
    down = (origin > chip).astype(jnp.int32)
    lies = jnp.where(down == 1, spot[1], spot[0])
    on = jnp.where(down == 1, side[1], side[0])
    far_row = ((2 * down + (on != core)) * stretch + lies) * UNIT + (2 << ROW_BITS)
    near_row = (item % pairs) * width + ((item // pairs != core).astype(jnp.int32) << ROW_BITS)
    rows = jnp.where(origin == chip, near_row, far_row).reshape(-1)
    last = lies + units[0] - 1
    passed = sum((last >= r * size).astype(jnp.int32) for r in range(1, max(rounds for rounds, _ in PLANS)))
    ready = jnp.where(origin == chip, 0, passed + (on != core)).reshape(-1)
    found = mine[0][:, None] == ids
    location = jnp.sum(jnp.where(found, rows, 0), axis=1)
    when = jnp.sum(jnp.where(found, ready, 0), axis=1)
    return branch, jnp.stack(table), jnp.stack(place), jnp.stack(need), location, when


def ranks_of(owner):
    spots = jnp.arange(owner.shape[-1], dtype=jnp.int32)
    ahead = (owner[..., None, :] == owner[..., :, None]) & (spots[None, :] < spots[:, None])
    return jnp.sum(ahead.astype(jnp.int32), axis=-1)


def wanted_from(owner, pair, me, capacity):
    slot = jnp.where(owner == me, ranks_of(owner), capacity)
    hit = slot[:, None, :] == jnp.arange(capacity, dtype=jnp.int32)[:, None]
    return jnp.sum(jnp.where(hit, pair[:, None, :], 0), axis=-1)


def load_all(source, scratch, sem, parts=8):
    rows = source.shape[0] // parts
    return [
        pltpu.make_async_copy(source.at[pl.ds(i * rows, rows)], scratch.at[pl.ds(i * rows, rows)], sem) for i in range(parts)
    ]


def take_kernel(width, index_ref, blocks_ref, *refs):
    outs, (scratch, load, sem) = refs[:-3], refs[-3:]
    slots = outs[0].shape[0] // width
    loads = load_all(blocks_ref, scratch, load)
    for c in loads:
        c.start()
    for c in loads:
        c.wait()

    def copies(i):
        for k, out in enumerate(outs):
            row = pl.multiple_of(index_ref[k * slots + i] * width, UNIT)
            yield pltpu.make_async_copy(
                scratch.at[pl.ds(row, width)], out.at[pl.ds(pl.multiple_of(i * width, UNIT), width)], sem
            )

    @pl.loop(0, slots)
    def _(i):
        for c in copies(i):
            c.start()

    @pl.loop(0, slots)
    def _(i):
        for c in copies(i):
            c.wait()


def take(blocks, index, width, parts):
    slots = index.shape[0] // parts
    shape = jax.ShapeDtypeStruct((slots * width, blocks.shape[1]), blocks.dtype)
    return pl.pallas_call(
        functools.partial(take_kernel, width),
        in_specs=[SMEM, ANY],
        out_specs=[ANY] * parts,
        out_shape=[shape] * parts,
        scratch_shapes=[pltpu.VMEM(blocks.shape, blocks.dtype), pltpu.SemaphoreType.DMA, pltpu.SemaphoreType.DMA],
        compiler_params=params(),
        cost_estimate=pl.CostEstimate(flops=0, bytes_accessed=2 * parts * slots * width * blocks.shape[1] * 2, transcendentals=0),
    )(index, blocks)


def run_copies(runs_ref, d, r, window, size, source, base, out, sem, shift):
    first, length, back = runs_ref[d, r, 0], runs_ref[d, r, 1], runs_ref[d, r, 2]
    low = jnp.maximum(first, window * size)
    high = jnp.minimum(first + length, (window + 1) * size)
    taken = jnp.maximum(high - low, 0)
    begin = back + low - first if shift else low
    rows = taken * UNIT
    return taken, pltpu.make_async_copy(
        source.at[pl.ds(pl.multiple_of((base + jnp.maximum(begin, 0)) * UNIT, UNIT), rows)],
        out.at[pl.ds(pl.multiple_of((low - window * size) * UNIT, UNIT), rows)],
        sem,
    )


def windows(runs_ref, picks, window, size, source, bases, outs, sem, shift, act):
    for d in range(2):
        for r in picks:
            taken, copy = run_copies(runs_ref, d, r, window, size, source, bases[d], outs[d], sem, shift)

            @pl.when(taken > 0)
            def _():
                getattr(copy, act)()


def items_of(pairs, core_ref, sources, visit):
    for half, source in enumerate(sources):

        @pl.loop(0, pairs)
        def _(i):
            for d in range(2):
                visit(source, i, d, (core_ref[0] ^ half) * pairs + i)


def open_kernel(size, span, pairs, width, own, place_ref, need_ref, runs_ref, core_ref, mine_ref, other_ref, stream_ref, *refs):
    outs, (near, beside, load, sem) = refs[:-4], refs[-4:]
    loads = load_all(mine_ref, near, load) + load_all(other_ref, beside, load)
    for c in loads:
        c.start()
    for c in loads:
        c.wait()
    straight = (0, span)

    def visit(source, i, d, item):
        units = need_ref[d, item]

        @pl.when(units > 0)
        def _():
            pltpu.make_async_copy(
                source.at[pl.ds(pl.multiple_of(i * width, UNIT), units * UNIT)],
                stream_ref.at[pl.ds(pl.multiple_of((straight[d] + place_ref[d, item]) * UNIT, UNIT), units * UNIT)],
                sem,
            ).start()

    items_of(pairs, core_ref, (near, beside), visit)
    for d in range(2):
        total = sum(runs_ref[d, r, 1] for r in range(own)) * UNIT

        @pl.when(total > 0)
        def _():
            pltpu.make_async_copy(near.at[pl.ds(0, total)], stream_ref.at[pl.ds(0, total)], sem).wait()

    for act in ("start", "wait"):
        for window in range(2):
            part = [out.at[pl.ds(window * size * UNIT, size * UNIT)] for out in outs]
            windows(runs_ref, range(own), window, size, stream_ref, straight, part, sem, False, act)


def step_kernel(size, stretch, own, at, other_at, next_windows, runs_ref, stream_ref, *refs):
    refs = list(refs)
    if other_at is not None:
        refs.pop(0)
    came = [refs.pop(0), refs.pop(0)]
    other = [refs.pop(0), refs.pop(0)] if other_at is not None else []
    hold = refs.pop(0)
    arrive, rest, lay = refs[-3:]
    outs = refs[:-3]
    rows = size * UNIT

    def filed(piece, section, number, sem):
        return pltpu.make_async_copy(
            piece, hold.at[pl.ds(section * stretch * UNIT + number * rows, piece.shape[0])], sem
        )

    first = [filed(c, 2 * d, at, arrive.at[d]) for d, c in enumerate(came)]
    second = [filed(c, 2 * d + 1, other_at, rest.at[d]) for d, c in enumerate(other)]
    for c in first + second:
        c.start()
    straight, through = (0, stretch - 8), (0, 2 * stretch)

    def lay_out(passed, act):
        picks = range(own, runs_ref.shape[1]) if passed else range(own)
        for i, window in enumerate(next_windows):
            source, bases = (hold, through) if passed else (stream_ref, straight)
            windows(runs_ref, picks, window, size, source, bases, outs[2 * i : 2 * i + 2], lay, passed, act)

    lay_out(False, "start")
    for c in first:
        c.wait()
    lay_out(True, "start")
    lay_out(False, "wait")
    lay_out(True, "wait")
    for c in second:
        c.wait()


def close_kernel(size, stretch, number, came_up, came_down, held_ref, hold, sem):
    del held_ref
    rows = size * UNIT
    copies = [
        pltpu.make_async_copy(c, hold.at[pl.ds((2 * d + 1) * stretch * UNIT + number * rows, rows)], sem.at[d])
        for d, c in enumerate((came_up, came_down))
    ]
    for c in copies:
        c.start()
    for c in copies:
        c.wait()


def couple_kernel(width, depth, many, low, high, begun, threads, loc_ref, when_ref, count_ref, target_ref, coef_ref, metric_ref, *refs):
    refs = list(refs)
    tasks = loc_ref.shape[0] - 1
    acc_ref = refs.pop(0) if begun else None
    line, slots, sems = refs[-3:]
    out_ref = refs[-5] if threads else refs[-4]
    buffers = refs[: -5 if threads else -4]
    out_ref[...] = acc_ref[...] if begun else jnp.zeros_like(out_ref)

    def gather(t, found):
        line[found] = t
        return found + ((when_ref[t] > low) & (when_ref[t] <= high)).astype(jnp.int32)

    found = lax.fori_loop(0, tasks, gather, jnp.int32(0))
    for u in range(many):
        line[found + u] = tasks
    groups = lax.div(found + (many - 1), jnp.int32(many))

    def fetch(group, phase):
        for u in range(many):
            code = loc_ref[line[group * many + u]]
            row = pl.multiple_of(code & ((1 << ROW_BITS) - 1), UNIT)
            for b, source in enumerate(buffers):

                @pl.when((code >> ROW_BITS) == b)
                def _():
                    pltpu.make_async_copy(source.at[pl.ds(row, width)], slots.at[phase, u], sems.at[phase, u]).start()

    @pl.when(groups > 0)
    def _():
        fetch(0, 0)

    @pl.loop(0, groups)
    def _(group):
        phase = lax.rem(group, 2)

        @pl.when(group + 1 < groups)
        def _():
            fetch(group + 1, 1 - phase)

        for u in range(many):
            pltpu.make_async_copy(buffers[0].at[pl.ds(0, width)], slots.at[phase, u], sems.at[phase, u]).wait()
        crossed, amps = [], []
        for u in range(many):
            t = line[group * many + u]
            live = lax.broadcasted_iota(jnp.int32, (width, width), 0) < count_ref[t]
            turned = lax.dot_general(
                slots[phase, u, :, pl.ds(0, depth)],
                metric_ref[target_ref[t]],
                (((1,), (1,)), ((), ())),
                preferred_element_type=jnp.float32,
            )
            crossed.append(jnp.where(live, turned, 0.0).astype(jnp.bfloat16))
            amp = slots[phase, u, :, pl.ds(depth, width)]
            amps.append(jnp.where(live, amp, jnp.zeros_like(amp)))
        halves = [
            lax.dot_general(turned, amp, (((0,), (0,)), ((), ())), preferred_element_type=jnp.float32).astype(jnp.bfloat16)
            for turned, amp in zip(crossed, amps)
        ]
        terms = [
            coef_ref[line[group * many + u]] * jnp.dot(halves[u], crossed[u], preferred_element_type=jnp.float32)
            for u in range(many)
        ]
        for u in range(many):
            target = target_ref[line[group * many + u]]
            out_ref[target] = out_ref[target] - terms[u]


def couple(lists, metric, acc, buffers, low, high, threaded=None):
    tasks, (pairs, width, depth) = lists[0].shape[0] - 1, metric.shape
    many = MANY
    operands = list(lists) + [metric] + ([] if acc is None else [acc]) + buffers
    out_shape = [jax.ShapeDtypeStruct((pairs, width, width), jnp.float32)]
    out_specs, aliases = [IN_VMEM], {}
    if threaded is not None:
        at = len(operands) - len(buffers) + threaded
        aliases = {at: 1}
        out_shape.append(jax.ShapeDtypeStruct(operands[at].shape, operands[at].dtype))
        out_specs.append(ANY)
    return pl.pallas_call(
        functools.partial(couple_kernel, width, depth, many, low, high, acc is not None, threaded is not None),
        in_specs=[SMEM] * 5 + [IN_VMEM] * (1 if acc is None else 2) + [ANY] * len(buffers),
        out_specs=out_specs,
        out_shape=out_shape,
        input_output_aliases=aliases,
        scratch_shapes=[
            pltpu.SMEM((tasks + many,), jnp.int32),
            pltpu.VMEM((2, many, width, depth + width), jnp.bfloat16),
            pltpu.SemaphoreType.DMA((2, many)),
        ],
        compiler_params=params(),
        cost_estimate=pl.CostEstimate(flops=0, bytes_accessed=20_000_000, transcendentals=0),
    )(*operands)


def relay(rounds, size, chips, pairs, width, table, place, need, core, lists, mine, other, metric_of, cross_take, crossed):
    columns = mine.shape[1]
    stretch = rounds * size + 8
    parts = (2, 4, rounds - 3, rounds - 2)
    own = chips - 1
    piece = jax.ShapeDtypeStruct((size * UNIT, columns), mine.dtype)
    double = jax.ShapeDtypeStruct((2 * size * UNIT, columns), mine.dtype)
    stream_shape = jax.ShapeDtypeStruct((2 * rounds * size * UNIT, columns), mine.dtype)
    hold_shape = jax.ShapeDtypeStruct((4 * stretch * UNIT, columns), mine.dtype)
    members = 2 * chips
    ways = [
        [(i, i + 2) for i in range(members - 2)],
        [(i + 2, i) for i in range(members - 2)],
    ]
    across = [(i, i ^ 1) for i in range(members)]
    stream, *opened = pl.pallas_call(
        functools.partial(open_kernel, size, rounds * size, pairs, width, own),
        in_specs=[SMEM] * 4 + [ANY] * 2,
        out_specs=[ANY] + [IN_VMEM] * 2,
        out_shape=[stream_shape] + [double] * 2,
        scratch_shapes=[pltpu.VMEM(mine.shape, mine.dtype)] * 2 + [pltpu.SemaphoreType.DMA] * 2,
        compiler_params=params(),
        cost_estimate=pl.CostEstimate(flops=0, bytes_accessed=6 * mine.size * 2, transcendentals=0),
    )(place, need, table, core, mine, other)
    sends = {1: opened}
    stream, after = lax.optimization_barrier((stream, mine))
    taken = cross_take(after)
    metric, crossing = metric_of(after), crossed(taken)
    hold, swapped, acc, done = None, None, None, -1
    for number in range(1, rounds):
        came = [lax.ppermute(sends[number][d], "mem", ways[d]) for d in range(2)]
        if number == 1:
            *came, _, metric = lax.optimization_barrier((*came, taken, metric))
        else:
            *came, hold = lax.optimization_barrier((*came, hold))
        swapping = [lax.ppermute(came[d], "mem", across) for d in range(2)]
        if number == rounds - 3:
            *came, crossing = lax.optimization_barrier((*came, crossing))
        begun = hold is not None
        ahead = [w for w in ((2, 3) if number == 1 else (number + 2,)) if w < rounds]
        operands = [table, stream] + ([hold] if begun else []) + came + (swapped if begun else [])
        hold, *going = pl.pallas_call(
            functools.partial(
                step_kernel,
                size,
                stretch,
                own,
                0 if number == 1 else number,
                None if not begun else (0 if number == 2 else number - 1),
                ahead,
            ),
            in_specs=[SMEM, ANY] + ([ANY] if begun else []) + [IN_VMEM] * (4 if begun else 2),
            out_specs=[ANY] + [IN_VMEM] * (2 * len(ahead)),
            out_shape=[hold_shape] + [piece] * (2 * len(ahead)),
            input_output_aliases={2: 0} if begun else {},
            scratch_shapes=[pltpu.SemaphoreType.DMA((2,)), pltpu.SemaphoreType.DMA((2,)), pltpu.SemaphoreType.DMA],
            compiler_params=params(),
            cost_estimate=pl.CostEstimate(flops=0, bytes_accessed=12 * size * UNIT * columns * 2, transcendentals=0),
        )(*operands)
        swapped = swapping
        if number in parts:
            buffers = [mine, other, hold] + ([crossing] if number >= rounds - 3 else [])
            acc, hold = couple(lists, metric, acc, buffers, done, number, 2)
            done = number
        for i, window in enumerate(ahead):
            sends[window] = going[2 * i : 2 * i + 2]
    hold = pl.pallas_call(
        functools.partial(close_kernel, size, stretch, rounds - 1),
        in_specs=[IN_VMEM] * 2 + [ANY],
        out_specs=ANY,
        out_shape=hold_shape,
        input_output_aliases={2: 0},
        scratch_shapes=[pltpu.SemaphoreType.DMA((2,))],
        compiler_params=params(),
    )(*swapped, hold)
    [acc] = couple(lists, metric, acc, [mine, other, hold, crossing], done, rounds)
    return acc


def shards(
    pno,
    amplitudes,
    pno_count,
    pao_coupling,
    row_owner,
    row_pair,
    row_target,
    row_coef,
    column_owner,
    column_pair,
    column_target,
    column_coef,
):
    pairs, depth, width = pno.shape
    tasks, crossings = row_pair.shape[0], column_pair.shape[0]
    members, groups = lax.axis_size("mem"), lax.axis_size("grp")
    member, group = lax.axis_index("mem"), lax.axis_index("grp")
    row_cap = max(2, 2 * tasks // members)
    col_cap = max(2, 2 * crossings // groups)
    chips = members // 2
    row_owner, column_owner = row_owner[:, 0], column_owner[:, 0]
    row_code = row_owner * pairs + row_pair
    col_code = column_owner * pairs + column_pair
    tell = jnp.concatenate([row_code, col_code, pno_count])
    told = lax.all_to_all(
        jnp.broadcast_to(tell, (groups * members, tell.shape[0])), ("grp", "mem"), split_axis=0, concat_axis=0, tiled=True
    )
    told = told.reshape(groups, members, -1)
    code, cols, count = told[..., :tasks], told[..., tasks : tasks + crossings], told[..., tasks + crossings :]
    blocks = blocks_of(pno, amplitudes, pno_count)
    ids = jnp.arange(members * pairs, dtype=jnp.int32)
    here = pick(count, group).reshape(-1)
    row_count = jnp.sum(jnp.where(row_code[:, None] == ids, here, 0), axis=1)
    beside = lax.dynamic_index_in_dim(count, member, 1, keepdims=False).reshape(-1)
    col_ids = jnp.arange(groups * pairs, dtype=jnp.int32)
    col_count = jnp.sum(jnp.where(col_code[:, None] == col_ids, beside, 0), axis=1)
    ask = lax.dynamic_index_in_dim(cols, member, 1, keepdims=False)
    asked = wanted_from(ask // pairs, ask % pairs, group, col_cap)
    col_row = (column_owner * col_cap + ranks_of(column_owner)) * width

    def metric_of(blocks):
        return metric_blocks(blocks, pao_coupling).reshape(pairs, width, depth)

    def cross_take(blocks):
        return take(blocks, asked.reshape(-1), width, 1)[0]

    def crossed(sent):
        return lax.all_to_all(sent, "grp", split_axis=0, concat_axis=0, tiled=True)

    def lists_of(location, when, first):
        col_location = col_row + (first << ROW_BITS)
        none = jnp.zeros((1,), jnp.int32)
        return (
            jnp.concatenate([location, col_location, none]),
            jnp.concatenate([when, jnp.full_like(col_location, CROSS_AFTER), none]),
            jnp.concatenate([row_count, col_count, none]),
            jnp.concatenate([row_target, column_target, none]),
            jnp.concatenate([row_coef, column_coef, none.astype(jnp.float32)]),
        )

    def plain(*_):
        want = wanted_from(pick(code, group) // pairs, pick(code, group) % pairs, member, row_cap)
        [sent] = take(blocks, want.reshape(-1), width, 1)
        got = lax.all_to_all(sent, "mem", split_axis=0, concat_axis=0, tiled=True)
        location = (row_owner * row_cap + ranks_of(row_owner)) * width + (1 << ROW_BITS)
        lists = lists_of(location, jnp.zeros_like(location), 2)
        [acc] = couple(lists, metric_of(blocks), None, [blocks, got, crossed(cross_take(blocks))], -1, CROSS_AFTER)
        return acc

    if members % 2 or chips < 2 or chips > 4:
        return plain()
    other = lax.ppermute(blocks, "mem", [(i, i ^ 1) for i in range(members)])
    branch, table, place, need, location, when = relay_plan(code, count, group, member, (row_code, width))
    core = (member % 2).reshape(1).astype(jnp.int32)

    lists = lists_of(location, when, 3)

    def relayed(rounds, size):
        return relay(rounds, size, chips, pairs, width, table, place, need, core, lists, blocks, other, metric_of, cross_take, crossed)

    return lax.switch(branch, [functools.partial(relayed, *p) for p in PLANS] + [plain])


def solution(mesh):
    in_specs = (
        P(("grp", "mem"), None, None),
        P(("grp", "mem"), None, None),
        P(("grp", "mem")),
        P(),
        P(("grp", "mem"), None),
        P(("grp", "mem")),
        P(("grp", "mem")),
        P(("grp", "mem")),
        P(("grp", "mem"), None),
        P(("grp", "mem")),
        P(("grp", "mem")),
        P(("grp", "mem")),
    )
    out_specs = P(("grp", "mem"), None, None)
    return jax.shard_map(shards, mesh=mesh, in_specs=in_specs, out_specs=out_specs, check_vma=False)
```
